32 devices in a mesh: ctx: 8 (over y, x, core), wsh: 4 (over z).
Axes of the slice: x: 2, y: 2, z: 4, core: 2. Of those that a mesh axis runs over, the one named last changes fastest.
Arguments:
- tokens: bfloat16 [8, 2048, 1024], P('wsh', 'ctx'), may hold values from -6 to 6
- out_grad: bfloat16 [8, 2048, 1024], P('wsh', 'ctx'), may hold values from -6 to 6
- seg_ids: int32 [8, 2048], P('wsh', 'ctx'), may hold values from 0 to 4, as said below
- positions: int32 [8, 2048], P('wsh', 'ctx'), may hold values from 0 to 1023, as said below
- ln1_gain: bfloat16 [1024], P('wsh'), may hold values from 0.5 to 1.5
- ln1_bias: bfloat16 [1024], P('wsh'), may hold values from -1.5 to 1.5
- w_qkv: bfloat16 [1024, 3072], P('wsh'), may hold values from -0.1875 to 0.1875
- w_out: bfloat16 [1024, 1024], P('wsh'), may hold values from -3 to 3
- ln2_gain: bfloat16 [1024], P('wsh'), may hold values from 0.5 to 1.5
- ln2_bias: bfloat16 [1024], P('wsh'), may hold values from -1.5 to 1.5
- w_up: bfloat16 [1024, 4096], P('wsh'), may hold values from -0.1875 to 0.1875
- w_down: bfloat16 [4096, 1024], P('wsh'), may hold values from -0.09375 to 0.09375
Outputs:
- output: bfloat16 [8, 2048, 1024], P('wsh', 'ctx')
- in_grad: bfloat16 [8, 2048, 1024], P('wsh', 'ctx')
- grad_ln1_gain: float32 [1024], P('wsh')
- grad_ln1_bias: float32 [1024], P('wsh')
- grad_w_qkv: float32 [1024, 3072], P('wsh')
- grad_w_out: float32 [1024, 1024], P('wsh')
- grad_ln2_gain: float32 [1024], P('wsh')
- grad_ln2_bias: float32 [1024], P('wsh')
- grad_w_up: float32 [1024, 4096], P('wsh')
- grad_w_down: float32 [4096, 1024], P('wsh')
The draws below stay inside these ranges and needn't reach their ends.
Inputs may be any that keep to these rules, and one draw needn't show every extreme that they name: `seg_ids`: in every group of 2048 tokens segment 0 holds 1024 tokens and segments 1 to 4 hold 256 tokens each; within a segment each position from 0 to its length minus one appears once. The tokens come in aligned blocks of 128 tokens of one segment with consecutive positions; the blocks stand in any order. The positions that belong to seg_ids, as described there.
All inputs are finite; a program needn't handle non-finite values.
Results may differ from the reference program's by a relative error of at most 0.02.
Values may be sent and summed in bfloat16 or wider, within the bound.
No kernel may reach another device: no remote copies, remote signals or barrier semaphores. Data moves between devices by JAX's collectives and lax.ppermute only.
A program may use at most 384 MiB of HBM per device.

```python
import jax
import jax.numpy as jnp
from jax import lax

D = 1024
HEADS = 16
HEAD_DIM = 64
FF = 4096
PROMPT = 1024
CONT_LEN = 256
GROUP = 2048
GROUPS = 8
BLOCKS = 16
BLK = 128


def label_table(key):
    index_all = jnp.arange(GROUP, dtype=jnp.int32)
    segment = jnp.where(index_all < PROMPT, 0, 1 + (index_all - PROMPT) // CONT_LEN).astype(jnp.int32)
    position = jnp.where(index_all < PROMPT, index_all, (index_all - PROMPT) % CONT_LEN).astype(jnp.int32)
    subkeys = jax.random.split(jax.random.fold_in(key, 11), GROUPS)
    orders = jax.vmap(lambda subkey: jax.random.permutation(subkey, BLOCKS))(subkeys).astype(jnp.int32)
    segment = segment.reshape(BLOCKS, BLK)[orders].reshape(GROUPS, GROUP)
    position = position.reshape(BLOCKS, BLK)[orders].reshape(GROUPS, GROUP)
    return (segment.astype(jnp.int32), position.astype(jnp.int32))


def draw_seg_ids(key, part):
    return label_table(key)[0]


def draw_positions(key, part):
    return label_table(key)[1]


def levels(stream_key, dims, cuts, least, top_value):
    level, own = 1.0, jax.random.fold_in(stream_key, 6)
    for dim, blocks in cuts:
        draws = jnp.exp(jax.random.uniform(jax.random.fold_in(own, dim), (blocks,), jnp.float32, least / len(cuts), top_value / len(cuts)))
        level = level * jnp.repeat(draws, dims[dim] // blocks).reshape([-1 if axis == dim else 1 for axis in range(len(dims))])
    return level


def gaussian(key, extent, spread, limit, cuts=(), kind=jnp.bfloat16):
    array = spread * jax.random.normal(key, extent, jnp.float32)
    if cuts:
        array = array * levels(key, extent, cuts, -0.22, 0.18)
    return jnp.clip(array, -limit, limit).astype(kind)


def setup_inputs(seed: int = 0) -> dict:
    splits = jax.random.split(jax.random.key(seed), 13)
    tokens = gaussian(splits[0], (GROUPS, GROUP, D), 1.0, 6.0, ((0, 4), (1, 8)))
    out_grad = gaussian(splits[1], (GROUPS, GROUP, D), 1.0, 6.0, ((0, 4), (1, 8)))
    seg_ids = draw_seg_ids(jax.random.fold_in(splits[12], 71), 0)
    positions = draw_positions(jax.random.fold_in(splits[12], 71), 0)
    ln1_gain = jnp.clip(1.0 + 0.1 * jax.random.normal(splits[4], (D,), jnp.float32), 0.5, 1.5).astype(jnp.bfloat16)
    ln1_bias = gaussian(splits[5], (D,), 0.3, 1.5, ((0, 4),))
    w_qkv = gaussian(splits[6], (D, 3 * D), D ** -0.5, 0.1875, ((0, 4),))
    w_out = gaussian(splits[7], (D, D), 4 ** -0.5, 3.0, ((0, 4),))
    ln2_gain = jnp.clip(1.0 + 0.1 * jax.random.normal(splits[8], (D,), jnp.float32), 0.5, 1.5).astype(jnp.bfloat16)
    ln2_bias = gaussian(splits[9], (D,), 0.3, 1.5, ((0, 4),))
    w_up = gaussian(splits[10], (D, FF), D ** -0.5, 0.1875, ((0, 4),))
    w_down = gaussian(splits[11], (FF, D), FF ** -0.5, 0.09375, ((0, 4),))
    return {"tokens": tokens, "out_grad": out_grad, "seg_ids": seg_ids, "positions": positions, "ln1_gain": ln1_gain, "ln1_bias": ln1_bias, "w_qkv": w_qkv, "w_out": w_out, "ln2_gain": ln2_gain, "ln2_bias": ln2_bias, "w_up": w_up, "w_down": w_down}


EPSILON = 1e-05
PRECISE = lax.Precision.HIGHEST

@jax.custom_vjp
def low(v):
    return lax.optimization_barrier(v.astype(jnp.bfloat16)).astype(jnp.float32)

@jax.custom_vjp
def low_back(v):
    return v

def low_keep(v):
    return (low(v), None)

def low_pass(kept, grad):
    return (grad,)

def back_keep(v):
    return (v, None)

def back_low(kept, grad):
    return (low(grad),)
low.defvjp(low_keep, low_pass)
low_back.defvjp(back_keep, back_low)

def layer_norm(values, gain, bias):
    average = lax.optimization_barrier(jnp.mean(values, -1, keepdims=True))
    centred = values - average
    return centred * lax.rsqrt(lax.optimization_barrier(jnp.mean(centred * centred, -1, keepdims=True)) + EPSILON) * gain + bias

def group_forward(params, stream, segment, position):
    gain_one, bias_one, w_proj, w_attn_out, gain_two, bias_two, w_upper, w_lower = params
    attn_in = low(layer_norm(stream, gain_one, bias_one))
    projected = low(low_back(jnp.dot(attn_in, w_proj, precision=PRECISE)))
    queries = projected[:, :D].reshape(GROUP, HEADS, HEAD_DIM)
    keys_all = projected[:, D:2 * D].reshape(GROUP, HEADS, HEAD_DIM)
    values_all = projected[:, 2 * D:].reshape(GROUP, HEADS, HEAD_DIM)
    scores = jnp.einsum('qhd,khd->hqk', queries, keys_all, precision=PRECISE) * HEAD_DIM ** (-0.5)
    scores = low_back(scores)
    shared = (segment[None, :] == 0) & (segment[:, None] != 0)
    within = (segment[:, None] == segment[None, :]) & (position[None, :] <= position[:, None])
    scores = jnp.where((shared | within)[None], scores, -1e+30)
    chances = low(jax.nn.softmax(scores, axis=-1))
    mixed_heads = jnp.einsum('hqk,khd->qhd', chances, values_all, precision=PRECISE).reshape(GROUP, D)
    attn_low = low(low_back(mixed_heads))
    residual = stream + low_back(jnp.dot(attn_low, w_attn_out, precision=PRECISE))
    ffn_in = low(layer_norm(residual, gain_two, bias_two))
    up_proj = low_back(jnp.dot(ffn_in, w_upper, precision=PRECISE))
    hidden = low(jax.nn.gelu(up_proj, approximate=False))
    return residual + low_back(jnp.dot(hidden, w_lower, precision=PRECISE))

def reference(tokens, out_grad, seg_ids, positions, ln1_gain, ln1_bias, w_qkv, w_out, ln2_gain, ln2_bias, w_up, w_down):
    params = tuple((weight.astype(jnp.float32) for weight in (ln1_gain, ln1_bias, w_qkv, w_out, ln2_gain, ln2_bias, w_up, w_down)))

    def forward(weights_now, stream):

        def one_group(inputs):
            return jax.checkpoint(group_forward)(weights_now, inputs[0], inputs[1], inputs[2])
        return lax.map(one_group, (stream, seg_ids, positions))
    output, pull_back = jax.vjp(forward, params, tokens.astype(jnp.float32))
    grad_params, grad_stream = pull_back(out_grad.astype(jnp.float32))
    return (output.astype(jnp.bfloat16), grad_stream.astype(jnp.bfloat16), grad_params[0], grad_params[1], grad_params[2], grad_params[3], grad_params[4], grad_params[5], grad_params[6], grad_params[7])
```

```python
import functools

import jax
import jax.numpy as jnp
from jax import lax
from jax.experimental import pallas as pl
from jax.experimental.pallas import tpu as pltpu
from jax.sharding import Mesh
from jax.sharding import PartitionSpec as P

HEADS = 16
PROMPT = 1024
CONT = 256
UNIT = 64
TILE = 256
EPSILON = 1e-05
NEG_BIG = -1e30
CTX = ("a", "b", "c")
F32 = jnp.float32
BF16 = jnp.bfloat16


def layer_norm(values, gain, bias):
    average = jnp.mean(values, -1, keepdims=True)
    centred = values - average
    inv_std = lax.rsqrt(jnp.mean(centred * centred, -1, keepdims=True) + EPSILON)
    normed = centred * inv_std
    return (normed * gain + bias, normed, inv_std)


def norm_back(grad_out, normed, inv_std, gain):
    scaled = grad_out * gain
    return inv_std * (
        scaled
        - jnp.mean(scaled, -1, keepdims=True)
        - normed * jnp.mean(scaled * normed, -1, keepdims=True)
    )


def gelu_exact(values):
    return jax.nn.gelu(values, approximate=False)


def nn(left, right):
    return jnp.dot(left, right, preferred_element_type=F32)


def nt(left, right):
    return lax.dot_general(left, right, (((1,), (1,)), ((), ())), preferred_element_type=F32)


def tn(left, right):
    return lax.dot_general(left, right, (((0,), (0,)), ((), ())), preferred_element_type=F32)


def unit_place(index, per_owner):
    owner = index // per_owner
    return owner, pl.multiple_of((index - owner * per_owner) * UNIT, UNIT)


def forward_attention(heads, width, qkv, g, source, target):
    _, owners, rows, _ = qkv.shape
    total = owners * rows
    units, per_owner = total // UNIT, rows // UNIT
    size = width // heads
    scale = size**-0.5

    def kernel(src, dst, qkv_ref, out_ref, exact_ref, log_ref, qs, ks, vs, vt):
        for s in range(units):
            owner, place = unit_place(src[g * units + s], per_owner)
            block = qkv_ref[0, owner, pl.ds(place, UNIT), :]
            here = slice(s * UNIT, (s + 1) * UNIT)
            qs[here, :] = block[:, :width] * scale
            ks[here, :] = block[:, width : 2 * width]
            vs[here, :] = block[:, 2 * width :]
        vt[...] = vs[...].T
        row = lax.broadcasted_iota(jnp.int32, (TILE, TILE), 0)
        col = lax.broadcasted_iota(jnp.int32, (TILE, TILE), 1)
        causal = row <= col
        for i in range(total // TILE):
            here = slice(i * TILE, (i + 1) * TILE)
            before = min(i * TILE, PROMPT)
            outs = []
            for h in range(heads):
                lanes = slice(h * size, (h + 1) * size)
                query = qs[here, lanes]
                own = jnp.where(causal, nt(ks[here, lanes], query), NEG_BIG)
                high = jnp.max(own, 0, keepdims=True)
                if before:
                    past = nt(ks[:before, lanes], query)
                    high = jnp.maximum(high, jnp.max(past, 0, keepdims=True))
                own = jnp.exp(own - high)
                sums = jnp.sum(own, 0, keepdims=True)
                mixed = nn(vt[lanes, here], own.astype(BF16))
                if before:
                    past = jnp.exp(past - high)
                    sums = sums + jnp.sum(past, 0, keepdims=True)
                    mixed = mixed + nn(vt[lanes, :before], past.astype(BF16))
                log_ref[h : h + 1, here] = high + jnp.log(sums)
                outs.append(mixed / sums)
            both = jnp.concatenate(outs, 0) if heads > 1 else outs[0]
            exact_ref[:, here] = both
            low = both.T.astype(BF16)
            for u in range(TILE // UNIT):
                owner, place = unit_place(dst[g * units + i * (TILE // UNIT) + u], per_owner)
                out_ref[owner, pl.ds(place, UNIT), :] = low[u * UNIT : (u + 1) * UNIT, :]

    return pl.pallas_call(
        kernel,
        grid_spec=pltpu.PrefetchScalarGridSpec(
            num_scalar_prefetch=2,
            grid=(1,),
            in_specs=[pl.BlockSpec((1, owners, rows, 3 * width), lambda i, *_: (g, 0, 0, 0))],
            out_specs=[
                pl.BlockSpec((owners, rows, width), lambda i, *_: (0, 0, 0)),
                pl.BlockSpec((width, total), lambda i, *_: (0, 0)),
                pl.BlockSpec((heads, total), lambda i, *_: (0, 0)),
            ],
            scratch_shapes=[pltpu.VMEM((total, width), BF16)] * 3
            + [pltpu.VMEM((width, total), BF16)],
        ),
        out_shape=[
            jax.ShapeDtypeStruct((owners, rows, width), BF16),
            jax.ShapeDtypeStruct((width, total), F32),
            jax.ShapeDtypeStruct((heads, total), F32),
        ],
        compiler_params=pltpu.CompilerParams(vmem_limit_bytes=48 * 1024 * 1024),
        cost_estimate=pl.CostEstimate(
            flops=12 * total * total * width, bytes_accessed=16 * total * width, transcendentals=0
        ),
    )(source, target, qkv)


def backward_attention(heads, width, qkv, g, grad, exact, logs, source, target):
    _, owners, rows, _ = qkv.shape
    total = owners * rows
    units, per_owner = total // UNIT, rows // UNIT
    size = width // heads
    scale = size**-0.5
    wide = 2 * TILE

    def kernel(
        src, dst, qkv_ref, grad_ref, exact_ref, log_ref, out_ref, qs, ks, vs, gs, kt, delta, dqt, dk, dv
    ):
        for s in range(units):
            owner, place = unit_place(src[g * units + s], per_owner)
            block = qkv_ref[0, owner, pl.ds(place, UNIT), :]
            here = slice(s * UNIT, (s + 1) * UNIT)
            qs[here, :] = block[:, :width] * scale
            ks[here, :] = block[:, width : 2 * width]
            vs[here, :] = block[:, 2 * width :]
            owner, place = unit_place(dst[g * units + s], per_owner)
            gs[here, :] = grad_ref[owner, pl.ds(place, UNIT), :]
        kt[...] = ks[...].T
        for i in range(total // TILE):
            here = slice(i * TILE, (i + 1) * TILE)
            both = gs[here, :].astype(F32).T * exact_ref[:, here]
            for h in range(heads):
                delta[h : h + 1, here] = jnp.sum(
                    both[h * size : (h + 1) * size, :], 0, keepdims=True
                )
        dqt[...] = jnp.zeros_like(dqt)
        for j in range(total // TILE):
            here = slice(j * TILE, (j + 1) * TILE)
            if j * TILE < PROMPT:
                starts = [(j * TILE, TILE)]
                at = (j + 1) * TILE
                if (total - at) % wide:
                    starts.append((at, TILE))
                    at += TILE
                while at < total:
                    starts.append((at, wide))
                    at += wide
            else:
                starts = [(j * TILE, TILE)]
            for h in range(heads):
                lanes = slice(h * size, (h + 1) * size)
                key, value, key_t = ks[here, lanes], vs[here, lanes], kt[lanes, here]
                grad_key = grad_value = None
                for at, count in starts:
                    there = slice(at, at + count)
                    query, pull = qs[there, lanes], gs[there, lanes]
                    powers = jnp.exp(nt(key, query) - log_ref[h : h + 1, there])
                    if at == j * TILE:
                        row = lax.broadcasted_iota(jnp.int32, (TILE, TILE), 0)
                        col = lax.broadcasted_iota(jnp.int32, (TILE, TILE), 1)
                        powers = jnp.where(row <= col, powers, 0.0)
                    slope = powers * (nt(value, pull) - delta[h : h + 1, there])
                    powers, slope = powers.astype(BF16), slope.astype(BF16)
                    more_value, more_key = nn(powers, pull), nn(slope, query)
                    grad_value = more_value if grad_value is None else grad_value + more_value
                    grad_key = more_key if grad_key is None else grad_key + more_key
                    dqt[lanes, there] += nn(key_t, slope)
                dk[here, lanes] = grad_key.astype(BF16)
                dv[here, lanes] = grad_value.astype(BF16)
        for i in range(total // TILE):
            here = slice(i * TILE, (i + 1) * TILE)
            low = (dqt[:, here] * scale).T.astype(BF16)
            for u in range(TILE // UNIT):
                s = i * (TILE // UNIT) + u
                owner, place = unit_place(src[g * units + s], per_owner)
                block = jnp.concatenate(
                    [
                        low[u * UNIT : (u + 1) * UNIT, :],
                        dk[s * UNIT : (s + 1) * UNIT, :],
                        dv[s * UNIT : (s + 1) * UNIT, :],
                    ],
                    1,
                )
                out_ref[owner, pl.ds(place, UNIT), :] = block

    whole = lambda *shape: pl.BlockSpec(shape, lambda i, *_: (0,) * len(shape))
    return pl.pallas_call(
        kernel,
        grid_spec=pltpu.PrefetchScalarGridSpec(
            num_scalar_prefetch=2,
            grid=(1,),
            in_specs=[
                pl.BlockSpec((1, owners, rows, 3 * width), lambda i, *_: (g, 0, 0, 0)),
                whole(owners, rows, width),
                whole(width, total),
                whole(heads, total),
            ],
            out_specs=whole(owners, rows, 3 * width),
            scratch_shapes=[pltpu.VMEM((total, width), BF16)] * 4
            + [
                pltpu.VMEM((width, total), BF16),
                pltpu.VMEM((heads, total), F32),
                pltpu.VMEM((width, total), F32),
                pltpu.VMEM((total, width), BF16),
                pltpu.VMEM((total, width), BF16),
            ],
        ),
        out_shape=jax.ShapeDtypeStruct((owners, rows, 3 * width), BF16),
        compiler_params=pltpu.CompilerParams(vmem_limit_bytes=48 * 1024 * 1024),
        cost_estimate=pl.CostEstimate(
            flops=16 * total * total * width, bytes_accessed=16 * total * width, transcendentals=0
        ),
    )(source, target, qkv, grad, exact, logs)


def feed_forward(h2, pull, sums, others, mine, shares):
    tokens, model = h2.shape
    chunks = others + mine
    ff = chunks[0].shape[1] // 2
    parts = model // ff
    part, rows = model // shares, ff // shares
    first = sums is None
    n_other, n_mine, n_all = len(others), len(mine), len(chunks)
    step = min(ff, TILE)

    def kernel(*refs):
        it = iter(refs)
        h2_ref, pull_ref = next(it), next(it)
        starts = None if first else (next(it), next(it))
        chunk_refs = [next(it) for _ in chunks]
        out_ref, grad_ref = next(it), next(it)
        targets = (next(it), next(it)), (next(it), next(it))
        h2_t, held, down_w, sem = next(it), next(it), next(it), next(it)
        t = pl.program_id(0)
        slot = lax.rem(t, 2)

        def fetch(k, into):
            return pltpu.make_async_copy(chunk_refs[k], held.at[into], sem.at[into])

        @pl.when(t == 0)
        def _():
            fetch(0, 0).start()
            h2_t[...] = h2_ref[...].T
            if first:
                out_ref[...] = jnp.zeros_like(out_ref)
                grad_ref[...] = jnp.zeros_like(grad_ref)
            else:
                out_ref[...] = starts[0][...]
                grad_ref[...] = starts[1][...]

        for k in range(n_all):

            @pl.when(t == k)
            def _(k=k):
                fetch(k, k % 2).wait()
                if k + 1 < n_all:
                    fetch(k + 1, (k + 1) % 2).start()

        for z in range(shares):
            for j in range(parts):
                at = z * part + j * rows
                down_w[z * rows : (z + 1) * rows, j * ff : (j + 1) * ff] = held[
                    slot, at : at + rows, ff:
                ]
        hiddens, slopes = [], []
        for at in range(0, ff, step):
            up = nn(h2_ref[...], held[slot, :, at : at + step])
            cdf = 0.5 * (1.0 + lax.erf(up * (0.5**0.5)))
            slope = cdf + up * (jnp.exp(-0.5 * up * up) * 0.3989422804014327)
            hiddens.append((up * cdf).astype(BF16))
            slopes.append((nt(pull_ref[...], down_w[at : at + step, :]) * slope).astype(BF16))
        hidden = jnp.concatenate(hiddens, 1) if len(hiddens) > 1 else hiddens[0]
        grad_up = jnp.concatenate(slopes, 1) if len(slopes) > 1 else slopes[0]
        out_ref[...] += nn(hidden, down_w[...])
        grad_ref[...] += nt(grad_up, held[slot, :, :ff])
        grad_upper = nn(h2_t[...], grad_up).astype(BF16)
        grad_lower = tn(hidden, pull_ref[...]).astype(BF16)

        def put(refs):
            refs[0][0] = grad_upper
            for z in range(shares):
                for j in range(parts):
                    refs[1][z, 0, j * rows : (j + 1) * rows, :] = grad_lower[
                        z * rows : (z + 1) * rows, j * ff : (j + 1) * ff
                    ]

        @pl.when(t < n_other)
        def _():
            put(targets[0])

        @pl.when(t >= n_other)
        def _():
            put(targets[1])

    whole = pl.BlockSpec((tokens, model), lambda t: (0, 0))
    early = lambda t: jnp.minimum(t, n_other - 1)
    late = lambda t: jnp.maximum(t - n_other, 0)
    acc = jax.ShapeDtypeStruct((tokens, model), F32)
    out_specs, out_shape = [whole, whole], [acc, acc]
    for count, at in ((n_other, early), (n_mine, late)):
        out_specs += [
            pl.BlockSpec((1, model, ff), lambda t, at=at: (at(t), 0, 0)),
            pl.BlockSpec((shares, 1, part, ff), lambda t, at=at: (0, at(t), 0, 0)),
        ]
        out_shape += [
            jax.ShapeDtypeStruct((count, model, ff), BF16),
            jax.ShapeDtypeStruct((shares, count, part, ff), BF16),
        ]
    return pl.pallas_call(
        kernel,
        grid=(n_all,),
        in_specs=[whole] * (2 if first else 4) + [pl.BlockSpec(memory_space=pl.ANY)] * n_all,
        out_specs=out_specs,
        out_shape=out_shape,
        scratch_shapes=[
            pltpu.VMEM((model, tokens), BF16),
            pltpu.VMEM((2, model, 2 * ff), BF16),
            pltpu.VMEM((ff, model), BF16),
            pltpu.SemaphoreType.DMA((2,)),
        ],
        compiler_params=pltpu.CompilerParams(vmem_limit_bytes=56 * 1024 * 1024),
        cost_estimate=pl.CostEstimate(
            flops=12 * tokens * model * ff * n_all,
            bytes_accessed=8 * model * ff * n_all,
            transcendentals=0,
        ),
    )(h2, pull, *(() if first else sums), *chunks)


def outer_gradient(left, right, places, shares):
    tokens, model = left.shape
    owners = places.shape[0]
    part = model // shares
    rows, half = part // owners, model // 2
    per = shares // 2

    def kernel(at_ref, left_ref, right_ref, away_ref, mine_ref, held):
        for z in range(shares):
            held[...] = tn(left_ref[:, z * part : (z + 1) * part], right_ref[...])
            h, at = z // per, z % per * rows
            for k in range(owners):
                ref = mine_ref if k < owners // 2 else away_ref
                block = held[pl.ds(pl.multiple_of(at_ref[k] * rows, rows), rows), :].astype(BF16)
                for j in range(2):
                    lanes = slice(j * half, (j + 1) * half)
                    ref[k % (owners // 2), h, j * per * rows + at : j * per * rows + at + rows, :] = (
                        block[:, lanes]
                    )

    shape = (owners // 2, 2, 2 * per * rows, half)
    whole = lambda *dims: pl.BlockSpec(dims, lambda i, _: (0,) * len(dims))
    return pl.pallas_call(
        kernel,
        grid_spec=pltpu.PrefetchScalarGridSpec(
            num_scalar_prefetch=1,
            grid=(1,),
            in_specs=[whole(tokens, model)] * 2,
            out_specs=[whole(*shape)] * 2,
            scratch_shapes=[pltpu.VMEM((part, model), F32)],
        ),
        out_shape=[jax.ShapeDtypeStruct(shape, BF16)] * 2,
        compiler_params=pltpu.CompilerParams(vmem_limit_bytes=48 * 1024 * 1024),
        cost_estimate=pl.CostEstimate(
            flops=2 * tokens * model * model, bytes_accessed=4 * model * model, transcendentals=0
        ),
    )(places, left, right)


def absolute(owner):
    a, b, c = lax.axis_index("a"), lax.axis_index("b"), lax.axis_index("c")
    owner = owner ^ (c * 4 + a * 2 + b)
    return (owner % 4) * 2 + owner // 4


def project(pieces, places, owners, groups, rows, gain, bias, weight, before):
    model, columns = weight.shape
    mine, steps = groups * rows, groups
    count = len(pieces)
    stride = places[1] - places[0] if count == 2 else 1

    def place(t):
        k = t // steps
        if count == 2:
            at = places[0] + stride * k
        else:
            at = k
            for i in range(1, count):
                if places[i] - places[i - 1] > 1:
                    at = at + (k >= i) * (places[i] - places[i - 1] - 1)
        return t % steps * owners + at

    def kernel(*refs):
        piece_refs = refs[:count]
        gain_ref, bias_ref, weight_ref = refs[count : count + 3]
        norm_ref, out_ref, held = refs[-3:]
        t = pl.program_id(0)
        for k in range(count):

            @pl.when(t // steps == k)
            def _(k=k):
                held[...] = piece_refs[k][...]

        values = held[...].astype(F32)
        normed = layer_norm(values, gain_ref[...], bias_ref[...])[0].astype(BF16)
        norm_ref[...] = normed
        out_ref[...] = nn(normed, weight_ref[...]).astype(BF16)

    specs = [
        pl.BlockSpec((rows, model), lambda t, k=k: (jnp.clip(t - k * steps, 0, steps - 1), 0))
        for k in range(count)
    ]
    fixed = lambda shape: pl.BlockSpec(shape, lambda t: (0, 0))
    specs += [fixed((1, model)), fixed((1, model)), fixed((model, columns))]
    extra = () if before is None else before
    return pl.pallas_call(
        kernel,
        grid=(count * steps,),
        in_specs=specs + [pl.BlockSpec(memory_space=pl.ANY)] * len(extra),
        out_specs=[
            pl.BlockSpec((rows, model), lambda t: (place(t), 0)),
            pl.BlockSpec((rows, columns), lambda t: (place(t), 0)),
        ],
        out_shape=[
            jax.ShapeDtypeStruct((owners * mine, model), BF16),
            jax.ShapeDtypeStruct((owners * mine, columns), BF16),
        ],
        scratch_shapes=[pltpu.VMEM((rows, model), BF16)],
        input_output_aliases={count + 3 + i: i for i in range(len(extra))},
        compiler_params=pltpu.CompilerParams(vmem_limit_bytes=48 * 1024 * 1024),
        cost_estimate=pl.CostEstimate(
            flops=2 * count * mine * model * columns,
            bytes_accessed=2 * count * mine * (2 * model + columns),
            transcendentals=0,
        ),
    )(*pieces, gain[None], bias[None], weight, *extra)


def pack(parts, packed, shares):
    model = packed.shape[0]
    part, half = model // shares, model // 2
    low = part // 2
    outer = (parts[0][0].shape[0] - half) // 2
    per = shares // 2
    out_rows = outer // per
    rows = low + out_rows + low
    flat = [each for terms in parts for each in terms]

    def kernel(*refs):
        packed_ref, out_ref = refs[-2], refs[-1]
        it = iter(refs)
        groups = [[next(it) for _ in terms] for terms in parts]

        def total(refs, at, count):
            summed = refs[0][at : at + count, :].astype(F32)
            for ref in refs[1:]:
                summed = summed + ref[at : at + count, :].astype(F32)
            return summed.astype(BF16)

        for z in range(shares):
            terms, side = groups[z // per], z % per
            for j in range(2):
                lanes = slice(j * half, (j + 1) * half)
                out_ref[z, :low, lanes] = total(terms, side * part + j * low, low)
                out_ref[z, low : low + out_rows, lanes] = total(
                    terms, half + j * outer + side * out_rows, out_rows
                )
                at = z * part + j * low
                out_ref[z, low + out_rows :, lanes] = packed_ref[at : at + low, :]

    return pl.pallas_call(
        kernel,
        out_shape=jax.ShapeDtypeStruct((shares, rows, model), BF16),
        compiler_params=pltpu.CompilerParams(vmem_limit_bytes=48 * 1024 * 1024),
    )(*flat, packed)


def unpack_lower(pieces, places, shares):
    owners = len(pieces)
    part, ff = pieces[0].shape
    parts = part * shares // ff
    rows = part // parts

    def kernel(at_ref, *refs):
        for k in range(owners):
            refs[-1][at_ref[k]] = refs[k][...].astype(F32)

    result = pl.pallas_call(
        kernel,
        grid_spec=pltpu.PrefetchScalarGridSpec(
            num_scalar_prefetch=1,
            grid=(parts,),
            in_specs=[pl.BlockSpec((rows, ff), lambda i, _: (i, 0))] * owners,
            out_specs=pl.BlockSpec((owners, rows, ff), lambda i, _: (0, 0, i)),
        ),
        out_shape=jax.ShapeDtypeStruct((owners, rows, parts * ff), F32),
        compiler_params=pltpu.CompilerParams(vmem_limit_bytes=48 * 1024 * 1024),
    )(places, *pieces)
    return result.reshape(owners * rows, parts * ff)


def unpack(pieces, places, shares, part, width):
    owners = len(pieces)
    rows, model = pieces[0].shape
    half, low = model // 2, part // 2
    out_rows = part // owners
    steps = 4
    block = low // steps
    outer_block = 16

    def kernel(at_ref, *refs):
        mains, outers, projs = refs[:owners], refs[owners : 2 * owners], refs[2 * owners : 3 * owners]
        up_ref, outer_ref, proj_ref, vec_ref = refs[3 * owners :]
        for j in range(2):
            at = j * half + 3 * width
            vectors = [proj[:, at : at + 128].astype(F32) for proj in projs]
            vec_ref[j] = functools.reduce(jnp.add, vectors)
        for k in range(owners):
            d = at_ref[k]
            lane = lambda base: pl.ds(pl.multiple_of(base + d * width, width), width)
            outer_ref[d] = outers[k][...].astype(F32)
            for j in range(2):
                for z in range(shares):
                    at = j * half + z * width
                    up_ref[j, :, lane(z * owners * width)] = mains[k][:, at : at + width].astype(F32)
                for t in range(3):
                    at = j * half + t * width
                    proj_ref[j, :, lane(t * model)] = projs[k][:, at : at + width].astype(F32)

    outer_at, proj_at = low // outer_block, (low + out_rows) // block
    outer_steps = out_rows // outer_block
    results = pl.pallas_call(
        kernel,
        grid_spec=pltpu.PrefetchScalarGridSpec(
            num_scalar_prefetch=1,
            grid=(steps,),
            in_specs=[pl.BlockSpec((block, model), lambda i, _: (i, 0))] * owners
            + [
                pl.BlockSpec(
                    (outer_block, model), lambda i, _: (outer_at + i * outer_steps // steps, 0)
                )
            ]
            * owners
            + [pl.BlockSpec((block, model), lambda i, _: (proj_at + i, 0))] * owners,
            out_specs=[
                pl.BlockSpec((2, block, shares * model), lambda i, _: (0, i, 0)),
                pl.BlockSpec(
                    (owners, outer_block, model), lambda i, _: (0, i * outer_steps // steps, 0)
                ),
                pl.BlockSpec((2, block, 3 * model), lambda i, _: (0, i, 0)),
                pl.BlockSpec((2, block, 128), lambda i, _: (0, i, 0)),
            ],
        ),
        out_shape=[
            jax.ShapeDtypeStruct((2, low, shares * model), F32),
            jax.ShapeDtypeStruct((owners, out_rows, model), F32),
            jax.ShapeDtypeStruct((2, low, 3 * model), F32),
            jax.ShapeDtypeStruct((2, low, 128), F32),
        ],
        compiler_params=pltpu.CompilerParams(vmem_limit_bytes=56 * 1024 * 1024),
    )(places, *pieces, *pieces, *pieces)
    upper, outer, proj, vectors = results
    return (
        upper.reshape(part, shares * model),
        outer.reshape(part, model),
        proj.reshape(part, 3 * model),
        vectors.reshape(part, 128),
    )


def flip(value, axis):
    return lax.ppermute(value, axis, [(0, 1), (1, 0)])


def spread(value):
    if lax.axis_size("a") != 2:
        return list(lax.all_gather(value, CTX, axis=0, tiled=False))
    half = value.shape[0] // 2
    from_b, from_a = flip(value, "b"), flip(value, "a")
    far = jnp.concatenate([flip(from_a[:half], "b"), flip(from_b[half:], "a")], 0)
    near = [value, from_b, from_a, far]
    return near + [flip(each, "c") for each in near]


def add(u, v):
    return (u.astype(F32) + v.astype(F32)).astype(BF16)


def converge_first(from_b, from_a, far):
    far_0, far_1 = flip(far[0], "b"), flip(far[1], "a")
    b_0, a_1 = flip(from_b[0], "b"), flip(from_a[1], "a")
    return add(from_b[1], far_1), add(from_a[0], far_0), b_0, a_1


def converge_last(own, first):
    b_1, a_0, b_0, a_1 = first
    return (own[0], b_0, flip(a_0, "a")), (own[1], flip(b_1, "b"), a_1)


def total(terms):
    return sum(each.astype(F32) for each in terms[1:]) + terms[0].astype(F32)


def shards(
    tokens,
    out_grad,
    seg_ids,
    positions,
    ln1_gain,
    ln1_bias,
    w_qkv,
    w_out,
    ln2_gain,
    ln2_bias,
    w_up,
    w_down,
):
    groups, rows, model = tokens.shape
    owners, shares = lax.axis_size(CTX), lax.axis_size("z")
    square = lax.axis_size("a") == 2
    width = model // owners
    heads = HEADS // owners
    mine = groups * rows
    part = model // shares
    full_ff = w_up.shape[1]
    ff = full_ff // owners
    ff_rows = ff // shares
    ff_parts = model // ff
    me = lax.axis_index(CTX)
    core = lax.axis_index("c")

    first_seg, first_pos = seg_ids[:, ::UNIT], positions[:, ::UNIT]
    slot = jnp.where(
        first_seg == 0,
        first_pos // UNIT,
        PROMPT // UNIT + (first_seg - 1) * (CONT // UNIT) + first_pos // UNIT,
    )
    per_group = rows // UNIT
    note = jnp.zeros((32, model), BF16).at[0, : groups * per_group].set(
        slot.reshape(-1).astype(BF16)
    )
    pieces = spread(jnp.concatenate([tokens.reshape(mine, model), note], 0))
    slots = jnp.stack(
        [each[mine, : groups * per_group].reshape(groups, per_group) for each in pieces], 1
    )
    slots = slots.reshape(groups, owners * per_group).astype(jnp.int32)

    columns = [
        lax.dynamic_slice_in_dim(w_qkv, t * model + me * width, width, 1) for t in range(3)
    ]
    norms = jnp.stack([ln1_gain, ln1_bias, ln2_gain, ln2_bias], 1)
    packed = jnp.concatenate(columns + [norms, jnp.zeros((part, 124), BF16)], 1)
    packed = lax.all_gather(packed, "z", axis=0, tiled=True)
    up_part = [
        lax.dynamic_slice_in_dim(w_up, (z * owners + me) * ff_rows, ff_rows, 1)
        for z in range(shares)
    ]
    down_part = lax.dynamic_slice_in_dim(w_down, me * ff_rows, ff_rows, 0)
    down_part = jnp.concatenate([down_part[:, j * ff : (j + 1) * ff] for j in range(ff_parts)], 0)
    chunk = jnp.concatenate(up_part + [down_part], 1)
    chunk, packed, pieces[1], pieces[2] = lax.optimization_barrier(
        (chunk, packed, pieces[1], pieces[2])
    )
    chunk = lax.all_gather(chunk, "z", axis=0, tiled=True)

    units = owners * per_group
    order = jnp.arange(units, dtype=jnp.int32)
    source = jnp.sum(
        jnp.where(slots[:, None, :] == order[None, :, None], order[None, None, :], 0), -1
    ).reshape(-1)
    w_heads = packed[:, : 3 * width]
    vectors = packed[:, 3 * width : 3 * width + 4].astype(F32).T
    gain_one, bias_one, gain_two, bias_two = vectors[0], vectors[1], vectors[2], vectors[3]

    half = w_out.shape[0] // 2
    piece = lax.dynamic_slice_in_dim(w_out, core * half, half, 0)
    piece, pieces[3], pieces[7] = lax.optimization_barrier((piece, pieces[3], pieces[7]))
    whole_out = lax.all_gather(piece, ("z", "c"), axis=0, tiled=True)

    chunk, pieces[3], pieces[7] = lax.optimization_barrier((chunk, pieces[3], pieces[7]))
    chunks = spread(chunk)
    target = source
    if square:
        owner = source // per_group
        target = absolute(owner) * per_group + source - owner * per_group

    if square:
        early, late = [0, 1, 2, 4, 5, 6], [3, 7]
        calls = [early, late]
    else:
        calls = [list(range(owners))]
    projected = None
    for places in calls:
        projected = project(
            [pieces[k] for k in places],
            places,
            owners,
            groups,
            rows,
            gain_one,
            bias_one,
            w_heads,
            projected,
        )
    attn_in, qkv = projected
    chunk, qkv = lax.optimization_barrier((chunk, qkv))
    chunks = spread(chunk)
    qkv = qkv.reshape(groups, owners, rows, 3 * width)
    attended, attn_low = [], []
    for g in range(groups):
        attn_heads, *kept = forward_attention(heads, width, qkv, g, source, target)
        attended.append(kept)
        attn_low.append(
            lax.all_to_all(attn_heads, CTX, split_axis=0, concat_axis=2, tiled=True)[0]
        )
    attn_low = jnp.concatenate(attn_low, 0)

    stream = tokens.reshape(mine, model).astype(F32)
    residual = stream + nn(attn_low, whole_out)
    ffn_full, ffn_norm, ffn_rstd = layer_norm(residual, gain_two, bias_two)
    ffn_in = ffn_full.astype(BF16)
    grad_low = out_grad.reshape(mine, model)
    cotangent = grad_low.astype(F32)

    if square:
        calls = [([4], [0]), ([5, 6], [1, 2]), ([7], [3])]
    else:
        calls = [([i, i + 1], [i + 2, i + 3]) for i in range(0, owners, 4)]
    sums, chunk_grads = None, []
    for away, here in calls:
        out_sum, in_sum, *each = feed_forward(
            ffn_in, grad_low, sums, [chunks[k] for k in away], [chunks[k] for k in here], shares
        )
        sums = (out_sum, in_sum)
        chunk_grads.append(each)
    output = (residual + sums[0]).astype(BF16)
    grad_ffn_in = sums[1]
    grad_gain_two = jnp.sum(grad_ffn_in * ffn_norm, 0)
    grad_bias_two = jnp.sum(grad_ffn_in, 0)
    grad_resid = cotangent + norm_back(grad_ffn_in, ffn_norm, ffn_rstd, gain_two)
    grad_branch = grad_resid.astype(BF16)
    grad_attn = [
        nt(grad_branch[g * rows : (g + 1) * rows], whole_out).astype(BF16) for g in range(groups)
    ]
    out_rows = part // owners

    if square:
        places = absolute(jnp.arange(owners))
        lower = jnp.concatenate([add(low, flip(away, "c")) for _, away, _, low in chunk_grads], 1)
        lower = lax.psum_scatter(
            lower.reshape(shares * 4, part, ff), "z", scatter_dimension=0, tiled=True
        )
        outer_away, outer = outer_gradient(attn_low, grad_branch, places, shares)
        outer = add(outer, flip(outer_away, "c"))
        upper = [add(up, flip(away, "c")) for away, _, up, _ in chunk_grads]
        upper = [upper[0][0], upper[1][0], upper[1][1], upper[2][0]]
        halves = [
            [
                jnp.concatenate([upper[k][h * model // 2 : (h + 1) * model // 2], outer[k, h]], 0)
                for h in range(2)
            ]
            for k in range(4)
        ]
        halves[3][0], halves[3][1], *grad_attn = lax.optimization_barrier((*halves[3], *grad_attn))
        first = converge_first(*halves[1:])
    else:
        lower = jnp.concatenate([low for _, a, _, b in chunk_grads for low in (a, b)], 1)
        lower = lax.psum_scatter(lower, CTX, scatter_dimension=1, tiled=True)
        lower = lower.reshape(shares, part, ff)
        upper = jnp.concatenate([up for a, _, b, _ in chunk_grads for up in (a, b)], 0)
        upper = lax.psum_scatter(upper, CTX, scatter_dimension=0, tiled=True)
        upper = upper.reshape(shares, part, ff)
        outer = tn(attn_low, grad_branch).astype(BF16)
        outer = outer.reshape(shares, owners, out_rows, model).transpose(1, 0, 2, 3)
        outer = lax.psum_scatter(
            outer.reshape(model, model), CTX, scatter_dimension=0, tiled=True
        )
    grad_heads = [
        lax.all_to_all(each, CTX, split_axis=1, concat_axis=0, tiled=True).reshape(
            owners, rows, width
        )
        for each in grad_attn
    ]

    grad_qkv, near_in = [], []
    split = owners // 2 * rows
    for g in range(groups):
        slopes = backward_attention(
            heads, width, qkv, g, grad_heads[g], *attended[g], source, target
        ).reshape(owners * rows, 3 * width)
        grad_qkv.append(slopes)
        if square:
            away = nt(slopes[split:], w_heads).astype(BF16)
            kept = nt(slopes[:split], w_heads) + flip(away, "c").astype(F32)
            near_in.append(kept.astype(BF16).reshape(4, rows, model))
            if g == 0:
                *first, near_in[0], grad_heads[1] = lax.optimization_barrier(
                    (*first, near_in[0], grad_heads[1])
                )
        else:
            away = nt(slopes, w_heads).astype(BF16)
            near_in.append(lax.psum_scatter(away, CTX, scatter_dimension=0, tiled=True).astype(F32))
    if square:
        upper_terms = converge_last(halves[0], first)
        near_in[1], grad_qkv[0], grad_qkv[1] = lax.optimization_barrier((near_in[1], *grad_qkv))
        pairs = [(near_in[0][k], near_in[1][k]) for k in range(4)]
        terms = converge_last(pairs[0], converge_first(*pairs[1:]))
        near_in = [total(each) for each in terms]
    grad_attn_in = jnp.concatenate(near_in, 0)
    attn_in = attn_in.reshape(groups, owners * rows, model)
    grad_columns = sum(tn(attn_in[g], grad_qkv[g]) for g in range(groups))
    w_wide = w_heads.astype(F32)
    summed = sum(jnp.sum(each.astype(F32), 0) for each in grad_qkv)
    grad_bias_one = jnp.sum(w_wide * summed, 1)
    grad_gain_one = (jnp.sum(w_wide * grad_columns, 1) - bias_one * grad_bias_one) / gain_one
    vector_grads = jnp.stack([grad_gain_one, grad_bias_one, grad_gain_two, grad_bias_two], 1)
    packed_grad = jnp.concatenate(
        [grad_columns, vector_grads, jnp.zeros((model, 124), F32)], 1
    ).astype(BF16)

    if square:
        lower = lower[0].astype(F32) + sum(
            flip(lower[k], axis).astype(F32) for k, axis in ((1, "b"), (2, "a"))
        ) + lax.ppermute(lower[3], ("a", "b"), [(0, 3), (3, 0), (1, 2), (2, 1)]).astype(F32)
        grad_down = unpack_lower(spread(lower.astype(BF16)), places, shares)
        everything = pack(upper_terms, packed_grad, shares)
        everything = lax.psum_scatter(
            everything.reshape(-1, model), "z", scatter_dimension=0, tiled=True
        )
        everything, grad_attn_in, grad_down = lax.optimization_barrier(
            (everything, grad_attn_in, grad_down)
        )
        grad_upper, grad_outer, grad_proj, vector_grads = unpack(
            spread(everything), places, shares, part, width
        )
    else:
        span = 2 * ff
        per_part = packed_grad.shape[1] * part // span
        everything = jnp.concatenate(
            [
                jnp.concatenate([upper, lower], 2),
                outer.reshape(shares, -1, span),
                packed_grad.reshape(shares, per_part, span),
            ],
            1,
        )
        everything = lax.psum_scatter(
            everything.reshape(-1, span), "z", scatter_dimension=0, tiled=True
        )
        everything = lax.all_gather(everything, CTX, axis=0, tiled=False)
        grad_upper = (
            everything[:, :part, :ff]
            .reshape(owners, part, shares, ff_rows)
            .transpose(1, 2, 0, 3)
            .reshape(part, full_ff)
            .astype(F32)
        )
        grad_down = (
            everything[:, :part, ff:]
            .reshape(owners, ff_parts, ff_rows, ff)
            .transpose(0, 2, 1, 3)
            .reshape(owners * ff_rows, model)
            .astype(F32)
        )
        at = part + out_rows * model // span
        grad_outer = everything[:, part:at].reshape(part, model).astype(F32)
        packed_grad = everything[:, at:].reshape(owners, part, -1).astype(F32)
        grad_proj = (
            packed_grad[:, :, : 3 * width]
            .reshape(owners, part, 3, width)
            .transpose(1, 2, 0, 3)
            .reshape(part, 3 * model)
        )
        vector_grads = jnp.sum(packed_grad[:, :, 3 * width : 3 * width + 4], 0)

    attn_full, attn_norm, attn_rstd = layer_norm(stream, gain_one, bias_one)
    in_grad = (grad_resid + norm_back(grad_attn_in, attn_norm, attn_rstd, gain_one)).astype(BF16)

    return (
        output.reshape(tokens.shape),
        in_grad.reshape(tokens.shape),
        vector_grads[:, 0],
        vector_grads[:, 1],
        grad_proj,
        grad_outer,
        vector_grads[:, 2],
        vector_grads[:, 3],
        grad_upper,
        grad_down,
    )


def solution(mesh):
    ctx, wsh = mesh.shape["ctx"], mesh.shape["wsh"]
    fine = Mesh(mesh.devices.reshape(ctx // 4, 2, 2, wsh), ("a", "b", "c", "z"))
    toks = P("z", CTX, None)
    ints = P("z", CTX)
    vec, mat = P("z"), P("z", None)
    in_specs = (toks, toks, ints, ints, vec, vec, mat, mat, vec, vec, mat, mat)
    out_specs = (toks, toks, vec, vec, mat, mat, vec, vec, mat, mat)
    return jax.shard_map(shards, mesh=fine, in_specs=in_specs, out_specs=out_specs, check_vma=False)
```

```python
import functools

import jax
import jax.numpy as jnp
from jax import lax
from jax.experimental import pallas as pl
from jax.experimental.pallas import tpu as pltpu
from jax.sharding import Mesh
from jax.sharding import PartitionSpec as P

HEADS = 16
PROMPT = 1024
CONT = 256
UNIT = 64
TILE = 256
EPSILON = 1e-05
NEG_BIG = -1e30
CTX = ("a", "b", "c")
F32 = jnp.float32
BF16 = jnp.bfloat16


def layer_norm(values, gain, bias):
    average = jnp.mean(values, -1, keepdims=True)
    centred = values - average
    inv_std = lax.rsqrt(jnp.mean(centred * centred, -1, keepdims=True) + EPSILON)
    normed = centred * inv_std
    return (normed * gain + bias, normed, inv_std)


def norm_back(grad_out, normed, inv_std, gain):
    scaled = grad_out * gain
    return inv_std * (
        scaled
        - jnp.mean(scaled, -1, keepdims=True)
        - normed * jnp.mean(scaled * normed, -1, keepdims=True)
    )


def gelu_exact(values):
    return jax.nn.gelu(values, approximate=False)


def nn(left, right):
    return jnp.dot(left, right, preferred_element_type=F32)


def nt(left, right):
    return lax.dot_general(left, right, (((1,), (1,)), ((), ())), preferred_element_type=F32)


def tn(left, right):
    return lax.dot_general(left, right, (((0,), (0,)), ((), ())), preferred_element_type=F32)


def forward_attention(heads, width, qkv, g, slots, places, before):
    owners, groups, rows, _ = qkv.shape
    total = owners * rows
    per_owner = rows // UNIT
    size = width // heads
    scale = size**-0.5

    units = [(k, u) for k in range(owners) for u in range(per_owner)]

    def kernel(slot_ref, at_ref, qkv_ref, *refs):
        out_ref, exact_ref, log_ref, qs, ks, vs, vt, low = refs[-8:]

        def canonical(k, u):
            slot = slot_ref[(k * groups + g) * per_owner + u]
            return pl.ds(pl.multiple_of(slot * UNIT, UNIT), UNIT)

        for k, u in units:
            block = qkv_ref[k, 0, u * UNIT : (u + 1) * UNIT, :]
            here = canonical(k, u)
            qs[here, :] = block[:, :width] * scale
            ks[here, :] = block[:, width : 2 * width]
            vs[here, :] = block[:, 2 * width :]
        vt[...] = vs[...].T
        row = lax.broadcasted_iota(jnp.int32, (TILE, TILE), 0)
        col = lax.broadcasted_iota(jnp.int32, (TILE, TILE), 1)
        causal = row <= col
        for i in range(total // TILE):
            here = slice(i * TILE, (i + 1) * TILE)
            before = min(i * TILE, PROMPT)
            outs = []
            for h in range(heads):
                lanes = slice(h * size, (h + 1) * size)
                query = qs[here, lanes]
                own = jnp.where(causal, nt(ks[here, lanes], query), NEG_BIG)
                high = jnp.max(own, 0, keepdims=True)
                if before:
                    past = nt(ks[:before, lanes], query)
                    high = jnp.maximum(high, jnp.max(past, 0, keepdims=True))
                own = jnp.exp(own - high)
                sums = jnp.sum(own, 0, keepdims=True)
                mixed = nn(vt[lanes, here], own.astype(BF16))
                if before:
                    past = jnp.exp(past - high)
                    sums = sums + jnp.sum(past, 0, keepdims=True)
                    mixed = mixed + nn(vt[lanes, :before], past.astype(BF16))
                log_ref[0, h : h + 1, here] = high + jnp.log(sums)
                outs.append(mixed / sums)
            both = jnp.concatenate(outs, 0) if heads > 1 else outs[0]
            exact_ref[0, :, here] = both
            low[here, :] = both.T.astype(BF16)
        for k, u in units:
            out_ref[at_ref[k], 0, u * UNIT : (u + 1) * UNIT, :] = low[canonical(k, u), :]

    return pl.pallas_call(
        kernel,
        grid_spec=pltpu.PrefetchScalarGridSpec(
            num_scalar_prefetch=2,
            grid=(1,),
            in_specs=[pl.BlockSpec((owners, 1, rows, 3 * width), lambda i, *_: (0, g, 0, 0))]
            + [pl.BlockSpec(memory_space=pl.ANY)] * len(before),
            out_specs=[
                pl.BlockSpec((owners, 1, rows, width), lambda i, *_: (0, g, 0, 0)),
                pl.BlockSpec((1, width, total), lambda i, *_: (g, 0, 0)),
                pl.BlockSpec((1, heads, total), lambda i, *_: (g, 0, 0)),
            ],
            scratch_shapes=[pltpu.VMEM((total, width), BF16)] * 3
            + [pltpu.VMEM((width, total), BF16), pltpu.VMEM((total, width), BF16)],
        ),
        out_shape=[
            jax.ShapeDtypeStruct((owners, groups, rows, width), BF16),
            jax.ShapeDtypeStruct((groups, width, total), F32),
            jax.ShapeDtypeStruct((groups, heads, total), F32),
        ],
        input_output_aliases={3 + i: i for i in range(len(before))},
        compiler_params=pltpu.CompilerParams(vmem_limit_bytes=48 * 1024 * 1024),
        cost_estimate=pl.CostEstimate(flops=1, bytes_accessed=1, transcendentals=0),
    )(slots, places, qkv, *before)


def backward_attention(heads, width, qkv, grad, exact, logs, slots, places):
    owners, groups, rows, _ = qkv.shape
    total = owners * rows
    per_owner = rows // UNIT
    size = width // heads
    scale = size**-0.5
    wide = 2 * TILE
    units = [(k, u) for k in range(owners) for u in range(per_owner)]

    def kernel(slot_ref, at_ref, qkv_ref, grad_ref, exact_ref, log_ref, out_ref, *scratch):
        qs, ks, vs, gs, kt, delta, dqt, dq, dk, dv = scratch
        g = pl.program_id(0)

        def canonical(k, u):
            slot = slot_ref[(k * groups + g) * per_owner + u]
            return pl.ds(pl.multiple_of(slot * UNIT, UNIT), UNIT)

        for k, u in units:
            block = qkv_ref[k, 0, u * UNIT : (u + 1) * UNIT, :]
            here = canonical(k, u)
            qs[here, :] = block[:, :width] * scale
            ks[here, :] = block[:, width : 2 * width]
            vs[here, :] = block[:, 2 * width :]
            gs[here, :] = grad_ref[at_ref[k], 0, u * UNIT : (u + 1) * UNIT, :]
        kt[...] = ks[...].T
        for i in range(total // TILE):
            here = slice(i * TILE, (i + 1) * TILE)
            both = gs[here, :].astype(F32).T * exact_ref[0, :, here]
            for h in range(heads):
                delta[h : h + 1, here] = jnp.sum(
                    both[h * size : (h + 1) * size, :], 0, keepdims=True
                )
        dqt[...] = jnp.zeros_like(dqt)
        for j in range(total // TILE):
            here = slice(j * TILE, (j + 1) * TILE)
            if j * TILE < PROMPT:
                starts = [(j * TILE, TILE)]
                at = (j + 1) * TILE
                if (total - at) % wide:
                    starts.append((at, TILE))
                    at += TILE
                while at < total:
                    starts.append((at, wide))
                    at += wide
            else:
                starts = [(j * TILE, TILE)]
            for h in range(heads):
                lanes = slice(h * size, (h + 1) * size)
                key, value, key_t = ks[here, lanes], vs[here, lanes], kt[lanes, here]
                grad_key = grad_value = None
                for at, count in starts:
                    there = slice(at, at + count)
                    query, pull = qs[there, lanes], gs[there, lanes]
                    powers = jnp.exp(nt(key, query) - log_ref[0, h : h + 1, there])
                    if at == j * TILE:
                        row = lax.broadcasted_iota(jnp.int32, (TILE, TILE), 0)
                        col = lax.broadcasted_iota(jnp.int32, (TILE, TILE), 1)
                        powers = jnp.where(row <= col, powers, 0.0)
                    slope = powers * (nt(value, pull) - delta[h : h + 1, there])
                    powers, slope = powers.astype(BF16), slope.astype(BF16)
                    more_value, more_key = nn(powers, pull), nn(slope, query)
                    grad_value = more_value if grad_value is None else grad_value + more_value
                    grad_key = more_key if grad_key is None else grad_key + more_key
                    dqt[lanes, there] += nn(key_t, slope)
                dk[here, lanes] = grad_key.astype(BF16)
                dv[here, lanes] = grad_value.astype(BF16)
        for i in range(total // TILE):
            here = slice(i * TILE, (i + 1) * TILE)
            dq[here, :] = (dqt[:, here] * scale).T.astype(BF16)
        for k, u in units:
            here = canonical(k, u)
            for at, ref in enumerate((dq, dk, dv)):
                out_ref[k, 0, u * UNIT : (u + 1) * UNIT, at * width : (at + 1) * width] = ref[
                    here, :
                ]

    by_group = lambda lanes: pl.BlockSpec((owners, 1, rows, lanes), lambda g, *_: (0, g, 0, 0))
    kept = lambda lines: pl.BlockSpec((1, lines, total), lambda g, *_: (g, 0, 0))
    return pl.pallas_call(
        kernel,
        grid_spec=pltpu.PrefetchScalarGridSpec(
            num_scalar_prefetch=2,
            grid=(groups,),
            in_specs=[by_group(3 * width), by_group(width), kept(width), kept(heads)],
            out_specs=by_group(3 * width),
            scratch_shapes=[pltpu.VMEM((total, width), BF16)] * 4
            + [
                pltpu.VMEM((width, total), BF16),
                pltpu.VMEM((heads, total), F32),
                pltpu.VMEM((width, total), F32),
                pltpu.VMEM((total, width), BF16),
                pltpu.VMEM((total, width), BF16),
                pltpu.VMEM((total, width), BF16),
            ],
        ),
        out_shape=jax.ShapeDtypeStruct((owners, groups, rows, 3 * width), BF16),
        compiler_params=pltpu.CompilerParams(vmem_limit_bytes=48 * 1024 * 1024),
        cost_estimate=pl.CostEstimate(
            flops=14 * total * total * width, bytes_accessed=1, transcendentals=0
        ),
    )(slots, places, qkv, grad, exact, logs)


def feed_forward(h2, pull, sums, others, mine, shares):
    tokens, model = h2.shape
    chunks = others + mine
    ff = chunks[0].shape[1] // 2
    parts = model // ff
    part, rows = model // shares, ff // shares
    first = sums is None
    n_other, n_mine, n_all = len(others), len(mine), len(chunks)
    step = min(ff, TILE)

    def kernel(*refs):
        it = iter(refs)
        h2_ref, pull_ref = next(it), next(it)
        starts = None if first else (next(it), next(it))
        chunk_refs = [next(it) for _ in chunks]
        out_ref, grad_ref = next(it), next(it)
        targets = (next(it), next(it)), (next(it), next(it))
        h2_t, held, down_w, sem = next(it), next(it), next(it), next(it)
        t = pl.program_id(0)
        slot = lax.rem(t, 2)

        def fetch(k, into):
            return pltpu.make_async_copy(chunk_refs[k], held.at[into], sem.at[into])

        @pl.when(t == 0)
        def _():
            fetch(0, 0).start()
            h2_t[...] = h2_ref[...].T
            if first:
                out_ref[...] = jnp.zeros_like(out_ref)
                grad_ref[...] = jnp.zeros_like(grad_ref)
            else:
                out_ref[...] = starts[0][...]
                grad_ref[...] = starts[1][...]

        for k in range(n_all):

            @pl.when(t == k)
            def _(k=k):
                fetch(k, k % 2).wait()
                if k + 1 < n_all:
                    fetch(k + 1, (k + 1) % 2).start()

        for z in range(shares):
            for j in range(parts):
                at = z * part + j * rows
                down_w[z * rows : (z + 1) * rows, j * ff : (j + 1) * ff] = held[
                    slot, at : at + rows, ff:
                ]
        hiddens, slopes = [], []
        for at in range(0, ff, step):
            up = nn(h2_ref[...], held[slot, :, at : at + step])
            cdf = 0.5 * (1.0 + lax.erf(up * (0.5**0.5)))
            slope = cdf + up * (jnp.exp(-0.5 * up * up) * 0.3989422804014327)
            hiddens.append((up * cdf).astype(BF16))
            slopes.append((nt(pull_ref[...], down_w[at : at + step, :]) * slope).astype(BF16))
        hidden = jnp.concatenate(hiddens, 1) if len(hiddens) > 1 else hiddens[0]
        grad_up = jnp.concatenate(slopes, 1) if len(slopes) > 1 else slopes[0]
        out_ref[...] += nn(hidden, down_w[...])
        grad_ref[...] += nt(grad_up, held[slot, :, :ff])
        grad_upper = nn(h2_t[...], grad_up).astype(BF16)
        grad_lower = tn(hidden, pull_ref[...]).astype(BF16)

        def put(refs):
            refs[0][0] = grad_upper
            for z in range(shares):
                for j in range(parts):
                    refs[1][z, 0, j * rows : (j + 1) * rows, :] = grad_lower[
                        z * rows : (z + 1) * rows, j * ff : (j + 1) * ff
                    ]

        @pl.when(t < n_other)
        def _():
            put(targets[0])

        @pl.when(t >= n_other)
        def _():
            put(targets[1])

    whole = pl.BlockSpec((tokens, model), lambda t: (0, 0))
    early = lambda t: jnp.minimum(t, n_other - 1)
    late = lambda t: jnp.maximum(t - n_other, 0)
    acc = jax.ShapeDtypeStruct((tokens, model), F32)
    out_specs, out_shape = [whole, whole], [acc, acc]
    for count, at in ((n_other, early), (n_mine, late)):
        out_specs += [
            pl.BlockSpec((1, model, ff), lambda t, at=at: (at(t), 0, 0)),
            pl.BlockSpec((shares, 1, part, ff), lambda t, at=at: (0, at(t), 0, 0)),
        ]
        out_shape += [
            jax.ShapeDtypeStruct((count, model, ff), BF16),
            jax.ShapeDtypeStruct((shares, count, part, ff), BF16),
        ]
    return pl.pallas_call(
        kernel,
        grid=(n_all,),
        in_specs=[whole] * (2 if first else 4) + [pl.BlockSpec(memory_space=pl.ANY)] * n_all,
        out_specs=out_specs,
        out_shape=out_shape,
        scratch_shapes=[
            pltpu.VMEM((model, tokens), BF16),
            pltpu.VMEM((2, model, 2 * ff), BF16),
            pltpu.VMEM((ff, model), BF16),
            pltpu.SemaphoreType.DMA((2,)),
        ],
        compiler_params=pltpu.CompilerParams(vmem_limit_bytes=56 * 1024 * 1024),
        cost_estimate=pl.CostEstimate(flops=1, bytes_accessed=1, transcendentals=0),
    )(h2, pull, *(() if first else sums), *chunks)


def attention_output(heads, stream, weight, gain, bias, rows):
    owners, tokens, width = heads.shape
    model = owners * width

    def kernel(heads_ref, stream_ref, weight_ref, gain_ref, bias_ref, low_ref, sum_ref, norm_ref):
        for d in range(owners):
            low_ref[:, d * width : (d + 1) * width] = heads_ref[d]
        total = stream_ref[...].astype(F32) + nn(low_ref[...], weight_ref[...])
        sum_ref[...] = total
        norm_ref[...] = layer_norm(total, gain_ref[...], bias_ref[...])[0].astype(BF16)

    fixed = lambda *shape: pl.BlockSpec(shape, lambda i: (0, 0))
    block = pl.BlockSpec((rows, model), lambda i: (i, 0))
    return pl.pallas_call(
        kernel,
        grid=(tokens // rows,),
        in_specs=[
            pl.BlockSpec((owners, rows, width), lambda i: (0, i, 0)),
            block,
            fixed(model, model),
            fixed(1, model),
            fixed(1, model),
        ],
        out_specs=[block] * 3,
        out_shape=[jax.ShapeDtypeStruct((tokens, model), kind) for kind in (BF16, F32, BF16)],
        compiler_params=pltpu.CompilerParams(vmem_limit_bytes=48 * 1024 * 1024),
        cost_estimate=pl.CostEstimate(flops=1, bytes_accessed=1, transcendentals=0),
    )(heads, stream, weight, gain[None], bias[None])


def norm_gradient(total, grad, direct, weight, gain, owners, rows):
    tokens, model = total.shape
    width = model // owners

    def kernel(total_ref, grad_ref, direct_ref, weight_ref, gain_ref, resid_ref, low_ref, heads_ref, vec_ref):
        i = pl.program_id(0)
        values = total_ref[...]
        centred = values - jnp.mean(values, -1, keepdims=True)
        inv_std = lax.rsqrt(jnp.mean(centred * centred, -1, keepdims=True) + EPSILON)
        normed = centred * inv_std
        grads = grad_ref[...]
        result = direct_ref[...].astype(F32) + norm_back(grads, normed, inv_std, gain_ref[...])
        resid_ref[...] = result
        low = result.astype(BF16)
        low_ref[...] = low
        back = nt(low, weight_ref[...]).astype(BF16)
        for d in range(owners):
            heads_ref[d] = back[:, d * width : (d + 1) * width]
        for_gain = jnp.sum(grads * normed, 0, keepdims=True)
        for_bias = jnp.sum(grads, 0, keepdims=True)

        @pl.when(i == 0)
        def _():
            vec_ref[...] = jnp.zeros_like(vec_ref)

        vec_ref[0:1, :] += for_gain
        vec_ref[1:2, :] += for_bias

    fixed = lambda *shape: pl.BlockSpec(shape, lambda i: (0, 0))
    block = pl.BlockSpec((rows, model), lambda i: (i, 0))
    return pl.pallas_call(
        kernel,
        grid=(tokens // rows,),
        in_specs=[block, block, block, fixed(model, model), fixed(1, model)],
        out_specs=[
            block,
            block,
            pl.BlockSpec((owners, rows, width), lambda i: (0, i, 0)),
            fixed(8, model),
        ],
        out_shape=[
            jax.ShapeDtypeStruct((tokens, model), F32),
            jax.ShapeDtypeStruct((tokens, model), BF16),
            jax.ShapeDtypeStruct((owners, tokens, width), BF16),
            jax.ShapeDtypeStruct((8, model), F32),
        ],
        compiler_params=pltpu.CompilerParams(vmem_limit_bytes=48 * 1024 * 1024),
        cost_estimate=pl.CostEstimate(flops=1, bytes_accessed=1, transcendentals=0),
    )(total, grad, direct, weight, gain[None])


def input_parts(slopes, weight, away):
    count, tokens, columns = slopes.shape
    model = weight.shape[0]
    half = tokens // 2

    def kernel(slope_ref, weight_ref, away_ref, *outs):
        t = pl.program_id(0)
        for h in range(2):
            rows = slice(h * half, (h + 1) * half)
            part = nt(slope_ref[0, rows, :], weight_ref[...]) + away_ref[0, rows, :].astype(F32)
            for k in range(count):

                @pl.when(t == k)
                def _(k=k, h=h, part=part):
                    outs[2 * k + h][...] = part.astype(BF16)

    out = pl.pallas_call(
        kernel,
        grid=(count,),
        in_specs=[
            pl.BlockSpec((1, tokens, columns), lambda t: (t, 0, 0)),
            pl.BlockSpec((model, columns), lambda t: (0, 0)),
            pl.BlockSpec((1, tokens, model), lambda t: (t, 0, 0)),
        ],
        out_specs=[pl.BlockSpec((half, model), lambda t: (0, 0))] * (2 * count),
        out_shape=[jax.ShapeDtypeStruct((half, model), BF16)] * (2 * count),
        compiler_params=pltpu.CompilerParams(vmem_limit_bytes=48 * 1024 * 1024),
        cost_estimate=pl.CostEstimate(flops=1, bytes_accessed=1, transcendentals=0),
    )(slopes, weight, away)
    return [(out[2 * k], out[2 * k + 1]) for k in range(count)]


def projection_gradient(normed, slopes, weight, columns):
    count, width = slopes.shape
    model = normed.shape[1]
    block = min(512, count)
    steps = count // block

    def kernel(normed_ref, slope_ref, weight_ref, columns_ref, out_ref, acc, sums):
        t = pl.program_id(0)
        grad = tn(slope_ref[...], normed_ref[...])
        summed = jnp.sum(slope_ref[...].astype(F32), 0, keepdims=True)

        @pl.when(t == 0)
        def _():
            acc[...] = grad
            sums[...] = summed

        @pl.when(t > 0)
        def _():
            acc[...] += grad
            sums[...] += summed

        @pl.when(t == steps - 1)
        def _():
            whole = acc[...].T
            wide = weight_ref[...].astype(F32)
            given = columns_ref[...]
            bias = jnp.sum(wide * sums[...], 1, keepdims=True)
            gain = jnp.sum(wide * whole, 1, keepdims=True)
            gain = (gain - given[:, 1:2] * bias) / given[:, 0:1]
            lane = lax.broadcasted_iota(jnp.int32, given.shape, 1)
            vectors = jnp.where(lane == 0, gain, jnp.where(lane == 1, bias, given))
            out_ref[:, :width] = whole.astype(BF16)
            out_ref[:, width:] = vectors.astype(BF16)

    return pl.pallas_call(
        kernel,
        grid=(steps,),
        in_specs=[
            pl.BlockSpec((block, model), lambda t: (t, 0)),
            pl.BlockSpec((block, width), lambda t: (t, 0)),
            pl.BlockSpec((model, width), lambda t: (0, 0)),
            pl.BlockSpec((model, 128), lambda t: (0, 0)),
        ],
        out_specs=pl.BlockSpec((model, width + 128), lambda t: (0, 0)),
        out_shape=jax.ShapeDtypeStruct((model, width + 128), BF16),
        scratch_shapes=[pltpu.VMEM((width, model), F32), pltpu.VMEM((1, width), F32)],
        compiler_params=pltpu.CompilerParams(vmem_limit_bytes=48 * 1024 * 1024),
        cost_estimate=pl.CostEstimate(flops=1, bytes_accessed=1, transcendentals=0),
    )(normed, slopes, weight, columns)


def join_lower(mine, away):
    shares, _, part, ff = mine[0].shape
    counts = [each.shape[1] for each in mine]
    n = len(mine)

    def kernel(*refs):
        at = 0
        for k, count in enumerate(counts):
            refs[-1][0, at : at + count] = add(refs[k][0], refs[n + k][0])
            at += count

    spec = lambda count: pl.BlockSpec((1, count, part, ff), lambda z: (z, 0, 0, 0))
    return pl.pallas_call(
        kernel,
        grid=(shares,),
        in_specs=[spec(count) for count in counts] * 2,
        out_specs=spec(sum(counts)),
        out_shape=jax.ShapeDtypeStruct((shares, sum(counts), part, ff), BF16),
        compiler_params=pltpu.CompilerParams(vmem_limit_bytes=48 * 1024 * 1024),
        cost_estimate=pl.CostEstimate(flops=1, bytes_accessed=1, transcendentals=0),
    )(*mine, *away)


def join_upper(mine, away, outer, outer_away):
    _, model, ff = mine[0].shape
    counts = [each.shape[0] for each in mine]
    n, half, extra = len(mine), model // 2, outer.shape[2]

    def kernel(*refs):
        ins, outs = refs[: 2 * n + 2], refs[2 * n + 2 :]
        k = 0
        for i, count in enumerate(counts):
            for j in range(count):
                for h in range(2):
                    rows = slice(h * half, (h + 1) * half)
                    outs[2 * k + h][:half, :] = add(ins[i][j, rows, :], ins[n + i][j, rows, :])
                    outs[2 * k + h][half:, :] = add(ins[2 * n][k, h], ins[2 * n + 1][k, h])
                k += 1

    out = pl.pallas_call(
        kernel,
        out_shape=[jax.ShapeDtypeStruct((half + extra, ff), BF16)] * (2 * sum(counts)),
        compiler_params=pltpu.CompilerParams(vmem_limit_bytes=48 * 1024 * 1024),
        cost_estimate=pl.CostEstimate(flops=1, bytes_accessed=1, transcendentals=0),
    )(*mine, *away, outer, outer_away)
    return [[out[2 * k], out[2 * k + 1]] for k in range(sum(counts))]


def outer_gradient(left, right, places, shares):
    tokens, model = left.shape
    owners = places.shape[0]
    part = model // shares
    rows, half = part // owners, model // 2
    per = shares // 2

    def kernel(at_ref, left_ref, right_ref, away_ref, mine_ref, held):
        for z in range(shares):
            held[...] = tn(left_ref[:, z * part : (z + 1) * part], right_ref[...])
            h, at = z // per, z % per * rows
            for k in range(owners):
                ref = mine_ref if k < owners // 2 else away_ref
                block = held[pl.ds(pl.multiple_of(at_ref[k] * rows, rows), rows), :].astype(BF16)
                for j in range(2):
                    lanes = slice(j * half, (j + 1) * half)
                    ref[k % (owners // 2), h, j * per * rows + at : j * per * rows + at + rows, :] = (
                        block[:, lanes]
                    )

    shape = (owners // 2, 2, 2 * per * rows, half)
    whole = lambda *dims: pl.BlockSpec(dims, lambda i, _: (0,) * len(dims))
    return pl.pallas_call(
        kernel,
        grid_spec=pltpu.PrefetchScalarGridSpec(
            num_scalar_prefetch=1,
            grid=(1,),
            in_specs=[whole(tokens, model)] * 2,
            out_specs=[whole(*shape)] * 2,
            scratch_shapes=[pltpu.VMEM((part, model), F32)],
        ),
        out_shape=[jax.ShapeDtypeStruct(shape, BF16)] * 2,
        compiler_params=pltpu.CompilerParams(vmem_limit_bytes=48 * 1024 * 1024),
        cost_estimate=pl.CostEstimate(flops=1, bytes_accessed=1, transcendentals=0),
    )(places, left, right)


def absolute(owner):
    a, b, c = lax.axis_index("a"), lax.axis_index("b"), lax.axis_index("c")
    owner = owner ^ (c * 4 + a * 2 + b)
    return (owner % 4) * 2 + owner // 4


def project(pieces, places, owners, groups, rows, gain, bias, weight, before):
    model, columns = weight.shape
    mine, steps = groups * rows, groups
    count = len(pieces)
    stride = places[1] - places[0] if count == 2 else 1

    def place(t):
        k = t // steps
        if count == 2:
            at = places[0] + stride * k
        else:
            at = k
            for i in range(1, count):
                if places[i] - places[i - 1] > 1:
                    at = at + (k >= i) * (places[i] - places[i - 1] - 1)
        return at * steps + t % steps

    def kernel(*refs):
        piece_refs = refs[:count]
        gain_ref, bias_ref, weight_ref = refs[count : count + 3]
        norm_ref, out_ref, held = refs[-3:]
        t = pl.program_id(0)
        for k in range(count):

            @pl.when(t // steps == k)
            def _(k=k):
                held[...] = piece_refs[k][...]

        values = held[...].astype(F32)
        normed = layer_norm(values, gain_ref[...], bias_ref[...])[0].astype(BF16)
        norm_ref[...] = normed
        out_ref[...] = nn(normed, weight_ref[...]).astype(BF16)

    specs = [
        pl.BlockSpec((rows, model), lambda t, k=k: (jnp.clip(t - k * steps, 0, steps - 1), 0))
        for k in range(count)
    ]
    fixed = lambda shape: pl.BlockSpec(shape, lambda t: (0, 0))
    specs += [fixed((1, model)), fixed((1, model)), fixed((model, columns))]
    extra = () if before is None else before
    return pl.pallas_call(
        kernel,
        grid=(count * steps,),
        in_specs=specs + [pl.BlockSpec(memory_space=pl.ANY)] * len(extra),
        out_specs=[
            pl.BlockSpec((rows, model), lambda t: (place(t), 0)),
            pl.BlockSpec((rows, columns), lambda t: (place(t), 0)),
        ],
        out_shape=[
            jax.ShapeDtypeStruct((owners * mine, model), BF16),
            jax.ShapeDtypeStruct((owners * mine, columns), BF16),
        ],
        scratch_shapes=[pltpu.VMEM((rows, model), BF16)],
        input_output_aliases={count + 3 + i: i for i in range(len(extra))},
        compiler_params=pltpu.CompilerParams(vmem_limit_bytes=48 * 1024 * 1024),
        cost_estimate=pl.CostEstimate(flops=1, bytes_accessed=1, transcendentals=0),
    )(*pieces, gain[None], bias[None], weight, *extra)


def pack(parts, packed, shares):
    model = packed.shape[0]
    part, half = model // shares, model // 2
    low = part // 2
    outer = (parts[0][0].shape[0] - half) // 2
    per = shares // 2
    out_rows = outer // per
    rows = low + out_rows + low
    flat = [each for terms in parts for each in terms]

    def kernel(*refs):
        packed_ref, out_ref = refs[-2], refs[-1]
        it = iter(refs)
        groups = [[next(it) for _ in terms] for terms in parts]

        def total(refs, at, count):
            summed = refs[0][at : at + count, :].astype(F32)
            for ref in refs[1:]:
                summed = summed + ref[at : at + count, :].astype(F32)
            return summed.astype(BF16)

        for z in range(shares):
            terms, side = groups[z // per], z % per
            for j in range(2):
                lanes = slice(j * half, (j + 1) * half)
                out_ref[z, :low, lanes] = total(terms, side * part + j * low, low)
                out_ref[z, low : low + out_rows, lanes] = total(
                    terms, half + j * outer + side * out_rows, out_rows
                )
                at = z * part + j * low
                out_ref[z, low + out_rows :, lanes] = packed_ref[at : at + low, :]

    return pl.pallas_call(
        kernel,
        out_shape=jax.ShapeDtypeStruct((shares, rows, model), BF16),
        compiler_params=pltpu.CompilerParams(vmem_limit_bytes=48 * 1024 * 1024),
    )(*flat, packed)


def unpack_lower(pieces, places, shares):
    owners = len(pieces)
    part, ff = pieces[0].shape
    parts = part * shares // ff
    rows = part // parts

    def kernel(at_ref, *refs):
        for k in range(owners):
            refs[-1][at_ref[k]] = refs[k][...].astype(F32)

    result = pl.pallas_call(
        kernel,
        grid_spec=pltpu.PrefetchScalarGridSpec(
            num_scalar_prefetch=1,
            grid=(parts,),
            in_specs=[pl.BlockSpec((rows, ff), lambda i, _: (i, 0))] * owners,
            out_specs=pl.BlockSpec((owners, rows, ff), lambda i, _: (0, 0, i)),
        ),
        out_shape=jax.ShapeDtypeStruct((owners, rows, parts * ff), F32),
        compiler_params=pltpu.CompilerParams(vmem_limit_bytes=48 * 1024 * 1024),
    )(places, *pieces)
    return result.reshape(owners * rows, parts * ff)


def unpack(pieces, places, shares, part, width):
    owners = len(pieces)
    rows, model = pieces[0].shape
    half, low = model // 2, part // 2
    out_rows = part // owners
    steps = 4
    block = low // steps
    outer_block = 16

    def kernel(at_ref, *refs):
        mains, outers, projs = refs[:owners], refs[owners : 2 * owners], refs[2 * owners : 3 * owners]
        up_ref, outer_ref, proj_ref, vec_ref = refs[3 * owners :]
        for j in range(2):
            at = j * half + 3 * width
            vectors = [proj[:, at : at + 128].astype(F32) for proj in projs]
            vec_ref[j] = functools.reduce(jnp.add, vectors)
        for k in range(owners):
            d = at_ref[k]
            lane = lambda base: pl.ds(pl.multiple_of(base + d * width, width), width)
            outer_ref[d] = outers[k][...].astype(F32)
            for j in range(2):
                for z in range(shares):
                    at = j * half + z * width
                    up_ref[j, :, lane(z * owners * width)] = mains[k][:, at : at + width].astype(F32)
                for t in range(3):
                    at = j * half + t * width
                    proj_ref[j, :, lane(t * model)] = projs[k][:, at : at + width].astype(F32)

    outer_at, proj_at = low // outer_block, (low + out_rows) // block
    outer_steps = out_rows // outer_block
    results = pl.pallas_call(
        kernel,
        grid_spec=pltpu.PrefetchScalarGridSpec(
            num_scalar_prefetch=1,
            grid=(steps,),
            in_specs=[pl.BlockSpec((block, model), lambda i, _: (i, 0))] * owners
            + [
                pl.BlockSpec(
                    (outer_block, model), lambda i, _: (outer_at + i * outer_steps // steps, 0)
                )
            ]
            * owners
            + [pl.BlockSpec((block, model), lambda i, _: (proj_at + i, 0))] * owners,
            out_specs=[
                pl.BlockSpec((2, block, shares * model), lambda i, _: (0, i, 0)),
                pl.BlockSpec(
                    (owners, outer_block, model), lambda i, _: (0, i * outer_steps // steps, 0)
                ),
                pl.BlockSpec((2, block, 3 * model), lambda i, _: (0, i, 0)),
                pl.BlockSpec((2, block, 128), lambda i, _: (0, i, 0)),
            ],
        ),
        out_shape=[
            jax.ShapeDtypeStruct((2, low, shares * model), F32),
            jax.ShapeDtypeStruct((owners, out_rows, model), F32),
            jax.ShapeDtypeStruct((2, low, 3 * model), F32),
            jax.ShapeDtypeStruct((2, low, 128), F32),
        ],
        compiler_params=pltpu.CompilerParams(vmem_limit_bytes=56 * 1024 * 1024),
    )(places, *pieces, *pieces, *pieces)
    upper, outer, proj, vectors = results
    return (
        upper.reshape(part, shares * model),
        outer.reshape(part, model),
        proj.reshape(part, 3 * model),
        vectors.reshape(part, 128),
    )


def flip(value, axis):
    return lax.ppermute(value, axis, [(0, 1), (1, 0)])


def after(value, *others):
    return lax.optimization_barrier((value, *others))[0]


def spread_near(value):
    return [value, flip(value, "b"), flip(value, "a")]


def spread_far(near):
    half = near[0].shape[0] // 2
    return [flip(near[2][:half], "b"), flip(near[1][half:], "a")]


def spread(value):
    if lax.axis_size("a") != 2:
        return list(lax.all_gather(value, CTX, axis=0, tiled=False))
    half = value.shape[0] // 2
    from_b, from_a = flip(value, "b"), flip(value, "a")
    far = jnp.concatenate([flip(from_a[:half], "b"), flip(from_b[half:], "a")], 0)
    near = [value, from_b, from_a, far]
    return near + [flip(each, "c") for each in near]


def add(u, v):
    return (u.astype(F32) + v.astype(F32)).astype(BF16)


def converge_first(from_b, from_a, far):
    far_0, far_1 = flip(far[0], "b"), flip(far[1], "a")
    b_0, a_1 = flip(from_b[0], "b"), flip(from_a[1], "a")
    return add(from_b[1], far_1), add(from_a[0], far_0), b_0, a_1


def converge_last(own, first):
    b_1, a_0, b_0, a_1 = first
    return (own[0], b_0, flip(a_0, "a")), (own[1], flip(b_1, "b"), a_1)


def total(terms):
    return sum(each.astype(F32) for each in terms[1:]) + terms[0].astype(F32)


def shards(
    tokens,
    out_grad,
    seg_ids,
    positions,
    ln1_gain,
    ln1_bias,
    w_qkv,
    w_out,
    ln2_gain,
    ln2_bias,
    w_up,
    w_down,
):
    groups, rows, model = tokens.shape
    owners, shares = lax.axis_size(CTX), lax.axis_size("z")
    square = lax.axis_size("a") == 2
    width = model // owners
    heads = HEADS // owners
    mine = groups * rows
    part = model // shares
    full_ff = w_up.shape[1]
    ff = full_ff // owners
    ff_rows = ff // shares
    ff_parts = model // ff
    me = lax.axis_index(CTX)
    core = lax.axis_index("c")

    first_seg, first_pos = seg_ids[:, ::UNIT], positions[:, ::UNIT]
    slot = jnp.where(
        first_seg == 0,
        first_pos // UNIT,
        PROMPT // UNIT + (first_seg - 1) * (CONT // UNIT) + first_pos // UNIT,
    )
    per_group = rows // UNIT
    note = jnp.zeros((32, model), BF16).at[0, : groups * per_group].set(
        slot.reshape(-1).astype(BF16)
    )
    sent = jnp.concatenate([tokens.reshape(mine, model), note], 0)
    if square:
        near_pieces = spread_near(sent)
        far_halves = spread_far(near_pieces)
        pieces = [sent] + near_pieces[1:3]
    else:
        pieces = spread(sent)
    places = jnp.arange(owners, dtype=jnp.int32)
    if square:
        places = absolute(places)

    columns = [
        lax.dynamic_slice_in_dim(w_qkv, t * model + me * width, width, 1) for t in range(3)
    ]
    norms = jnp.stack([ln1_gain, ln1_bias, ln2_gain, ln2_bias], 0)
    norms = jnp.pad(norms.reshape(-1, 64), ((0, 0), (0, 3 * width - 64)))
    packed = jnp.concatenate(columns, 1)
    packed = jnp.concatenate([packed, norms], 0)
    packed = lax.all_gather(packed, "z", axis=0, tiled=True)
    up_part = [
        lax.dynamic_slice_in_dim(w_up, (z * owners + me) * ff_rows, ff_rows, 1)
        for z in range(shares)
    ]
    down_part = lax.dynamic_slice_in_dim(w_down, me * ff_rows, ff_rows, 0)
    down_part = jnp.concatenate([down_part[:, j * ff : (j + 1) * ff] for j in range(ff_parts)], 0)
    chunk = jnp.concatenate(up_part + [down_part], 1)
    chunk, packed, pieces[1], pieces[2] = lax.optimization_barrier(
        (chunk, packed, pieces[1], pieces[2])
    )
    chunk = lax.all_gather(chunk, "z", axis=0, tiled=True)

    packed = packed.reshape(shares, -1, 3 * width)
    w_heads = packed[:, :part].reshape(model, 3 * width)
    vectors = packed[:, part:, :64].astype(F32).reshape(shares, 4, part)
    vectors = vectors.transpose(1, 0, 2).reshape(4, model)
    gain_one, bias_one, gain_two, bias_two = vectors[0], vectors[1], vectors[2], vectors[3]

    half = w_out.shape[0] // 2
    piece = lax.dynamic_slice_in_dim(w_out, core * half, half, 0)

    def projection(pieces, chosen, before):
        return project(
            pieces, chosen, owners, groups, rows, gain_one, bias_one, w_heads, before
        )

    if square:
        near_pieces += [flip(each, "c") for each in near_pieces]
        projected = projection(near_pieces, [0, 1, 2, 4, 5, 6], None)
        far_halves[0], far_halves[1], *projected = lax.optimization_barrier(
            (*far_halves, *projected)
        )
        far = jnp.concatenate(far_halves, 0)
        pieces = near_pieces[:3] + [far] + near_pieces[3:] + [flip(far, "c")]
        attn_in, qkv = projection([far, pieces[7]], [3, 7], projected)
    else:
        attn_in, qkv = projection(pieces, list(range(owners)), None)
    slots = jnp.concatenate([each[mine, : groups * per_group] for each in pieces])
    slots = slots.astype(jnp.int32)
    qkv = qkv.reshape(owners, groups, rows, 3 * width)
    attended = forward_attention(heads, width, qkv, 0, slots, places, [])
    for g in range(1, groups):
        if square and g == 1:
            near_chunks = spread_near(after(chunk, attended[0]))
        attended = forward_attention(heads, width, qkv, g, slots, places, attended)
    attn_heads, exact, logs = attended
    whole_out = lax.all_gather(after(piece, attn_heads), ("z", "c"), axis=0, tiled=True)
    attn_heads = lax.all_to_all(
        attn_heads.reshape(owners, mine, width), CTX, split_axis=0, concat_axis=0, tiled=True
    )
    flat = tokens.reshape(mine, model)
    if square:
        other_chunks = [flip(each, "c") for each in near_chunks]
        attn_heads = after(attn_heads, *other_chunks)
    attn_low, residual, ffn_in = attention_output(
        attn_heads, flat, whole_out, gain_two, bias_two, rows
    )
    grad_low = out_grad.reshape(mine, model)

    def feed(sums, others, mine):
        out_sum, in_sum, *grads = feed_forward(ffn_in, grad_low, sums, others, mine, shares)
        chunk_grads.append(grads)
        return out_sum, in_sum

    sums, chunk_grads = None, []
    if square:
        sums = feed(sums, other_chunks, near_chunks)
        far_chunk = spread_far([after(each, ffn_in) for each in near_chunks])
        far_0, far_1, *sums = lax.optimization_barrier((*far_chunk, *sums))
        far = jnp.concatenate([far_0, far_1], 0)
        sums = feed(sums, [flip(far, "c")], [far])
    else:
        chunks = spread(chunk)
        for k in range(0, owners, 4):
            sums = feed(sums, chunks[k : k + 2], chunks[k + 2 : k + 4])
    output = (residual + sums[0]).astype(BF16)
    grad_resid, grad_branch, grad_heads, norm_grads = norm_gradient(
        residual, sums[1], grad_low, whole_out, gain_two, owners, rows
    )
    grad_gain_two, grad_bias_two = norm_grads[0], norm_grads[1]
    late = [grad_branch] + [each for grads in chunk_grads for each in grads]
    grad_heads, grad_branch, *late = lax.optimization_barrier((grad_heads, *late))
    chunk_grads = [late[:4], late[4:8]] if square else chunk_grads
    grad_heads = lax.all_to_all(
        grad_heads, CTX, split_axis=0, concat_axis=0, tiled=True
    ).reshape(owners, groups, rows, width)
    out_rows = part // owners

    if square:
        outer_away, outer = outer_gradient(attn_low, grad_branch, places, shares)
        halves = join_upper(
            [each[2] for each in chunk_grads],
            [flip(each[0], "c") for each in chunk_grads],
            outer,
            flip(outer_away, "c"),
        )
        lower = join_lower(
            [
                after(each[3], grad_heads, *[half for pair in halves for half in pair])
                for each in chunk_grads
            ],
            [flip(each[1], "c") for each in chunk_grads],
        )
        grad_heads = after(grad_heads, lower)
        lower = lax.psum_scatter(
            lower.reshape(shares * 4, part, ff), "z", scatter_dimension=0, tiled=True
        )
    else:
        lower = jnp.concatenate([low for _, a, _, b in chunk_grads for low in (a, b)], 1)
        lower = lax.psum_scatter(lower, CTX, scatter_dimension=1, tiled=True)
        lower = lower.reshape(shares, part, ff)
        upper = jnp.concatenate([up for a, _, b, _ in chunk_grads for up in (a, b)], 0)
        upper = lax.psum_scatter(upper, CTX, scatter_dimension=0, tiled=True)
        upper = upper.reshape(shares, part, ff)
        outer = tn(attn_low, grad_branch).astype(BF16)
        outer = outer.reshape(shares, owners, out_rows, model).transpose(1, 0, 2, 3)
        outer = lax.psum_scatter(
            outer.reshape(model, model), CTX, scatter_dimension=0, tiled=True
        )
    grad_qkv = backward_attention(heads, width, qkv, grad_heads, exact, logs, slots, places)
    if square:
        first = converge_first(*halves[1:])
        columns = jnp.stack([gain_one, bias_one, grad_gain_two, grad_bias_two], 1)
        columns = jnp.pad(columns, ((0, 0), (0, 124)))
        *first, columns, grad_qkv = lax.optimization_barrier((*first, columns, grad_qkv))
        upper_terms = converge_last(halves[0], first)
        grad_qkv = grad_qkv.reshape(owners, mine, 3 * width)
        away = nt(grad_qkv[4:].reshape(4 * mine, 3 * width), w_heads).astype(BF16)
        grad_qkv = after(grad_qkv, away)
        away = flip(away, "c").reshape(4, mine, model)
        pairs = input_parts(grad_qkv[:4], w_heads, away)
        terms = converge_last(pairs[0], converge_first(*pairs[1:]))
        grad_attn_in = jnp.concatenate([total(each) for each in terms], 0)
        packed_grad = projection_gradient(
            attn_in, grad_qkv.reshape(owners * mine, 3 * width), w_heads, columns
        )
        packed_grad = after(packed_grad, lower, *[each for pair in pairs for each in pair])
    else:
        grad_qkv = grad_qkv.reshape(owners * mine, 3 * width)
        away = nt(grad_qkv, w_heads).astype(BF16)
        grad_attn_in = lax.psum_scatter(away, CTX, scatter_dimension=0, tiled=True).astype(F32)
        grad_columns = tn(attn_in, grad_qkv)
        w_wide = w_heads.astype(F32)
        summed = jnp.sum(grad_qkv.astype(F32), 0)
        grad_bias_one = jnp.sum(w_wide * summed, 1)
        grad_gain_one = (jnp.sum(w_wide * grad_columns, 1) - bias_one * grad_bias_one) / gain_one
        vector_grads = jnp.stack([grad_gain_one, grad_bias_one, grad_gain_two, grad_bias_two], 1)
        packed_grad = jnp.concatenate(
            [grad_columns, vector_grads, jnp.zeros((model, 124), F32)], 1
        ).astype(BF16)

    if square:
        lower = lower[0].astype(F32) + sum(
            flip(lower[k], axis).astype(F32) for k, axis in ((1, "b"), (2, "a"))
        ) + lax.ppermute(lower[3], ("a", "b"), [(0, 3), (3, 0), (1, 2), (2, 1)]).astype(F32)
        grad_down = unpack_lower(spread(lower.astype(BF16)), places, shares)
        everything = pack(upper_terms, packed_grad, shares)
        everything = lax.psum_scatter(
            everything.reshape(-1, model), "z", scatter_dimension=0, tiled=True
        )
        grad_upper, grad_outer, grad_proj, vector_grads = unpack(
            spread(after(everything, grad_down)), places, shares, part, width
        )
    else:
        span = 2 * ff
        per_part = packed_grad.shape[1] * part // span
        everything = jnp.concatenate(
            [
                jnp.concatenate([upper, lower], 2),
                outer.reshape(shares, -1, span),
                packed_grad.reshape(shares, per_part, span),
            ],
            1,
        )
        everything = lax.psum_scatter(
            everything.reshape(-1, span), "z", scatter_dimension=0, tiled=True
        )
        everything = lax.all_gather(everything, CTX, axis=0, tiled=False)
        grad_upper = (
            everything[:, :part, :ff]
            .reshape(owners, part, shares, ff_rows)
            .transpose(1, 2, 0, 3)
            .reshape(part, full_ff)
            .astype(F32)
        )
        grad_down = (
            everything[:, :part, ff:]
            .reshape(owners, ff_parts, ff_rows, ff)
            .transpose(0, 2, 1, 3)
            .reshape(owners * ff_rows, model)
            .astype(F32)
        )
        at = part + out_rows * model // span
        grad_outer = everything[:, part:at].reshape(part, model).astype(F32)
        packed_grad = everything[:, at:].reshape(owners, part, -1).astype(F32)
        grad_proj = (
            packed_grad[:, :, : 3 * width]
            .reshape(owners, part, 3, width)
            .transpose(1, 2, 0, 3)
            .reshape(part, 3 * model)
        )
        vector_grads = jnp.sum(packed_grad[:, :, 3 * width : 3 * width + 4], 0)

    attn_full, attn_norm, attn_rstd = layer_norm(flat.astype(F32), gain_one, bias_one)
    in_grad = (grad_resid + norm_back(grad_attn_in, attn_norm, attn_rstd, gain_one)).astype(BF16)

    return (
        output.reshape(tokens.shape),
        in_grad.reshape(tokens.shape),
        vector_grads[:, 0],
        vector_grads[:, 1],
        grad_proj,
        grad_outer,
        vector_grads[:, 2],
        vector_grads[:, 3],
        grad_upper,
        grad_down,
    )


def solution(mesh):
    ctx, wsh = mesh.shape["ctx"], mesh.shape["wsh"]
    fine = Mesh(mesh.devices.reshape(ctx // 4, 2, 2, wsh), ("a", "b", "c", "z"))
    toks = P("z", CTX, None)
    ints = P("z", CTX)
    vec, mat = P("z"), P("z", None)
    in_specs = (toks, toks, ints, ints, vec, vec, mat, mat, vec, vec, mat, mat)
    out_specs = (toks, toks, vec, vec, mat, mat, vec, vec, mat, mat)
    return jax.shard_map(shards, mesh=fine, in_specs=in_specs, out_specs=out_specs, check_vma=False)
```

```python
import functools

import jax
import jax.numpy as jnp
from jax import lax
from jax.experimental import pallas as pl
from jax.experimental.pallas import tpu as pltpu
from jax.sharding import Mesh
from jax.sharding import PartitionSpec as P

HEADS = 16
PROMPT = 1024
CONT = 256
UNIT = 64
TILE = 256
EPSILON = 1e-05
NEG_BIG = -1e30
CTX = ("a", "b", "c")
F32 = jnp.float32
BF16 = jnp.bfloat16


def layer_norm(values, gain, bias):
    average = jnp.mean(values, -1, keepdims=True)
    centred = values - average
    inv_std = lax.rsqrt(jnp.mean(centred * centred, -1, keepdims=True) + EPSILON)
    normed = centred * inv_std
    return (normed * gain + bias, normed, inv_std)


def norm_back(grad_out, normed, inv_std, gain):
    scaled = grad_out * gain
    return inv_std * (
        scaled
        - jnp.mean(scaled, -1, keepdims=True)
        - normed * jnp.mean(scaled * normed, -1, keepdims=True)
    )


def gelu_exact(values):
    return jax.nn.gelu(values, approximate=False)


def nn(left, right):
    return jnp.dot(left, right, preferred_element_type=F32)


def nt(left, right):
    return lax.dot_general(left, right, (((1,), (1,)), ((), ())), preferred_element_type=F32)


def tn(left, right):
    return lax.dot_general(left, right, (((0,), (0,)), ((), ())), preferred_element_type=F32)


def forward_attention(heads, width, qkv, g, slots, places, before):
    owners, groups, rows, _ = qkv.shape
    total = owners * rows
    per_owner = rows // UNIT
    size = width // heads
    scale = size**-0.5

    units = [(k, u) for k in range(owners) for u in range(per_owner)]

    def kernel(slot_ref, at_ref, qkv_ref, *refs):
        out_ref, exact_ref, log_ref, qs, ks, vs, vt, low = refs[-8:]

        def canonical(k, u):
            slot = slot_ref[(k * groups + g) * per_owner + u]
            return pl.ds(pl.multiple_of(slot * UNIT, UNIT), UNIT)

        for k, u in units:
            block = qkv_ref[k, 0, u * UNIT : (u + 1) * UNIT, :]
            here = canonical(k, u)
            qs[here, :] = block[:, :width] * scale
            ks[here, :] = block[:, width : 2 * width]
            vs[here, :] = block[:, 2 * width :]
        vt[...] = vs[...].T
        row = lax.broadcasted_iota(jnp.int32, (TILE, TILE), 0)
        col = lax.broadcasted_iota(jnp.int32, (TILE, TILE), 1)
        causal = row <= col
        for i in range(total // TILE):
            here = slice(i * TILE, (i + 1) * TILE)
            before = min(i * TILE, PROMPT)
            outs = []
            for h in range(heads):
                lanes = slice(h * size, (h + 1) * size)
                query = qs[here, lanes]
                own = jnp.where(causal, nt(ks[here, lanes], query), NEG_BIG)
                high = jnp.max(own, 0, keepdims=True)
                if before:
                    past = nt(ks[:before, lanes], query)
                    high = jnp.maximum(high, jnp.max(past, 0, keepdims=True))
                own = jnp.exp(own - high)
                sums = jnp.sum(own, 0, keepdims=True)
                mixed = nn(vt[lanes, here], own.astype(BF16))
                if before:
                    past = jnp.exp(past - high)
                    sums = sums + jnp.sum(past, 0, keepdims=True)
                    mixed = mixed + nn(vt[lanes, :before], past.astype(BF16))
                log_ref[0, h : h + 1, here] = high + jnp.log(sums)
                outs.append(mixed / sums)
            both = jnp.concatenate(outs, 0) if heads > 1 else outs[0]
            exact_ref[0, :, here] = both
            low[here, :] = both.T.astype(BF16)
        for k, u in units:
            out_ref[at_ref[k], 0, u * UNIT : (u + 1) * UNIT, :] = low[canonical(k, u), :]

    return pl.pallas_call(
        kernel,
        grid_spec=pltpu.PrefetchScalarGridSpec(
            num_scalar_prefetch=2,
            grid=(1,),
            in_specs=[pl.BlockSpec((owners, 1, rows, 3 * width), lambda i, *_: (0, g, 0, 0))]
            + [pl.BlockSpec(memory_space=pl.ANY)] * len(before),
            out_specs=[
                pl.BlockSpec((owners, 1, rows, width), lambda i, *_: (0, g, 0, 0)),
                pl.BlockSpec((1, width, total), lambda i, *_: (g, 0, 0)),
                pl.BlockSpec((1, heads, total), lambda i, *_: (g, 0, 0)),
            ],
            scratch_shapes=[pltpu.VMEM((total, width), BF16)] * 3
            + [pltpu.VMEM((width, total), BF16), pltpu.VMEM((total, width), BF16)],
        ),
        out_shape=[
            jax.ShapeDtypeStruct((owners, groups, rows, width), BF16),
            jax.ShapeDtypeStruct((groups, width, total), F32),
            jax.ShapeDtypeStruct((groups, heads, total), F32),
        ],
        input_output_aliases={3 + i: i for i in range(len(before))},
        compiler_params=pltpu.CompilerParams(vmem_limit_bytes=48 * 1024 * 1024),
        cost_estimate=pl.CostEstimate(flops=1, bytes_accessed=1, transcendentals=0),
    )(slots, places, qkv, *before)


def backward_attention(heads, width, qkv, grad, exact, logs, slots, places):
    owners, groups, rows, _ = qkv.shape
    total = owners * rows
    per_owner = rows // UNIT
    size = width // heads
    scale = size**-0.5
    wide = 2 * TILE
    units = [(k, u) for k in range(owners) for u in range(per_owner)]

    def kernel(slot_ref, at_ref, qkv_ref, grad_ref, exact_ref, log_ref, out_ref, *scratch):
        qs, ks, vs, gs, kt, delta, dqt, dq, dk, dv = scratch
        g = pl.program_id(0)

        def canonical(k, u):
            slot = slot_ref[(k * groups + g) * per_owner + u]
            return pl.ds(pl.multiple_of(slot * UNIT, UNIT), UNIT)

        for k, u in units:
            block = qkv_ref[k, 0, u * UNIT : (u + 1) * UNIT, :]
            here = canonical(k, u)
            qs[here, :] = block[:, :width] * scale
            ks[here, :] = block[:, width : 2 * width]
            vs[here, :] = block[:, 2 * width :]
            gs[here, :] = grad_ref[at_ref[k], 0, u * UNIT : (u + 1) * UNIT, :]
        kt[...] = ks[...].T
        for i in range(total // TILE):
            here = slice(i * TILE, (i + 1) * TILE)
            both = gs[here, :].astype(F32).T * exact_ref[0, :, here]
            for h in range(heads):
                delta[h : h + 1, here] = jnp.sum(
                    both[h * size : (h + 1) * size, :], 0, keepdims=True
                )
        dqt[...] = jnp.zeros_like(dqt)
        for j in range(total // TILE):
            here = slice(j * TILE, (j + 1) * TILE)
            if j * TILE < PROMPT:
                starts = [(j * TILE, TILE)]
                at = (j + 1) * TILE
                if (total - at) % wide:
                    starts.append((at, TILE))
                    at += TILE
                while at < total:
                    starts.append((at, wide))
                    at += wide
            else:
                starts = [(j * TILE, TILE)]
            for h in range(heads):
                lanes = slice(h * size, (h + 1) * size)
                key, value, key_t = ks[here, lanes], vs[here, lanes], kt[lanes, here]
                grad_key = grad_value = None
                for at, count in starts:
                    there = slice(at, at + count)
                    query, pull = qs[there, lanes], gs[there, lanes]
                    powers = jnp.exp(nt(key, query) - log_ref[0, h : h + 1, there])
                    if at == j * TILE:
                        row = lax.broadcasted_iota(jnp.int32, (TILE, TILE), 0)
                        col = lax.broadcasted_iota(jnp.int32, (TILE, TILE), 1)
                        powers = jnp.where(row <= col, powers, 0.0)
                    slope = powers * (nt(value, pull) - delta[h : h + 1, there])
                    powers, slope = powers.astype(BF16), slope.astype(BF16)
                    more_value, more_key = nn(powers, pull), nn(slope, query)
                    grad_value = more_value if grad_value is None else grad_value + more_value
                    grad_key = more_key if grad_key is None else grad_key + more_key
                    dqt[lanes, there] += nn(key_t, slope)
                dk[here, lanes] = grad_key.astype(BF16)
                dv[here, lanes] = grad_value.astype(BF16)
        for i in range(total // TILE):
            here = slice(i * TILE, (i + 1) * TILE)
            dq[here, :] = (dqt[:, here] * scale).T.astype(BF16)
        for k, u in units:
            here = canonical(k, u)
            for at, ref in enumerate((dq, dk, dv)):
                out_ref[k, 0, u * UNIT : (u + 1) * UNIT, at * width : (at + 1) * width] = ref[
                    here, :
                ]

    by_group = lambda lanes: pl.BlockSpec((owners, 1, rows, lanes), lambda g, *_: (0, g, 0, 0))
    kept = lambda lines: pl.BlockSpec((1, lines, total), lambda g, *_: (g, 0, 0))
    return pl.pallas_call(
        kernel,
        grid_spec=pltpu.PrefetchScalarGridSpec(
            num_scalar_prefetch=2,
            grid=(groups,),
            in_specs=[by_group(3 * width), by_group(width), kept(width), kept(heads)],
            out_specs=by_group(3 * width),
            scratch_shapes=[pltpu.VMEM((total, width), BF16)] * 4
            + [
                pltpu.VMEM((width, total), BF16),
                pltpu.VMEM((heads, total), F32),
                pltpu.VMEM((width, total), F32),
                pltpu.VMEM((total, width), BF16),
                pltpu.VMEM((total, width), BF16),
                pltpu.VMEM((total, width), BF16),
            ],
        ),
        out_shape=jax.ShapeDtypeStruct((owners, groups, rows, 3 * width), BF16),
        compiler_params=pltpu.CompilerParams(vmem_limit_bytes=48 * 1024 * 1024),
        cost_estimate=pl.CostEstimate(
            flops=14 * total * total * width, bytes_accessed=1, transcendentals=0
        ),
    )(slots, places, qkv, grad, exact, logs)


def feed_forward(h2, h2_turned, pull, sums, others, mine, shares):
    tokens, model = h2.shape
    chunks = others + mine
    ff = chunks[0][0].shape[1] // 2
    parts = model // ff
    part, rows = model // shares, ff // shares
    first = sums is None
    n_other, n_mine, n_all = len(others), len(mine), len(chunks)
    pieces = [piece for chunk in chunks for piece in chunk]
    step = min(ff, TILE)

    def kernel(*refs):
        it = iter(refs)
        h2_ref, h2_t, pull_ref = next(it), next(it), next(it)
        starts = None if first else (next(it), next(it))
        chunk_refs = [[next(it) for _ in chunk] for chunk in chunks]
        out_ref, grad_ref = next(it), next(it)
        targets = (next(it), next(it)), (next(it), next(it))
        held, down_w, sem, sum_sem = next(it), next(it), next(it), next(it)
        t = pl.program_id(0)
        slot = lax.rem(t, 2)

        def fetch(k, into):
            count = model // len(chunk_refs[k])
            return [
                pltpu.make_async_copy(
                    ref, held.at[into, pl.ds(p * count, count)], sem.at[into, p]
                )
                for p, ref in enumerate(chunk_refs[k])
            ]

        def fetch_sums():
            return [
                pltpu.make_async_copy(ref, into, sum_sem.at[k])
                for k, (ref, into) in enumerate(zip(starts, (out_ref, grad_ref)))
            ]

        @pl.when(t == 0)
        def _():
            for copy in fetch(0, 0):
                copy.start()
            if first:
                out_ref[...] = jnp.zeros_like(out_ref)
                grad_ref[...] = jnp.zeros_like(grad_ref)
            else:
                for copy in fetch_sums():
                    copy.start()

        for k in range(n_all):

            @pl.when(t == k)
            def _(k=k):
                for copy in fetch(k, k % 2):
                    copy.wait()
                if k + 1 < n_all:
                    for copy in fetch(k + 1, (k + 1) % 2):
                        copy.start()

        for z in range(shares):
            for j in range(parts):
                at = z * part + j * rows
                down_w[z * rows : (z + 1) * rows, j * ff : (j + 1) * ff] = held[
                    slot, at : at + rows, ff:
                ]
        hiddens, slopes = [], []
        for at in range(0, ff, step):
            up = nn(h2_ref[...], held[slot, :, at : at + step])
            cdf = 0.5 * (1.0 + lax.erf(up * (0.5**0.5)))
            slope = cdf + up * (jnp.exp(-0.5 * up * up) * 0.3989422804014327)
            hiddens.append((up * cdf).astype(BF16))
            slopes.append((nt(pull_ref[...], down_w[at : at + step, :]) * slope).astype(BF16))
        hidden = jnp.concatenate(hiddens, 1) if len(hiddens) > 1 else hiddens[0]
        grad_up = jnp.concatenate(slopes, 1) if len(slopes) > 1 else slopes[0]
        if not first:

            @pl.when(t == 0)
            def _():
                for copy in fetch_sums():
                    copy.wait()

        out_ref[...] += nn(hidden, down_w[...])
        grad_ref[...] += nt(grad_up, held[slot, :, :ff])
        grad_upper = nn(h2_t[...], grad_up).astype(BF16)
        grad_lower = tn(hidden, pull_ref[...]).astype(BF16)

        def put(refs):
            refs[0][0] = grad_upper
            for z in range(shares):
                for j in range(parts):
                    refs[1][z, 0, j * rows : (j + 1) * rows, :] = grad_lower[
                        z * rows : (z + 1) * rows, j * ff : (j + 1) * ff
                    ]

        @pl.when(t < n_other)
        def _():
            put(targets[0])

        @pl.when(t >= n_other)
        def _():
            put(targets[1])

    whole = pl.BlockSpec((tokens, model), lambda t: (0, 0))
    early = lambda t: jnp.minimum(t, n_other - 1)
    late = lambda t: jnp.maximum(t - n_other, 0)
    acc = jax.ShapeDtypeStruct((tokens, model), F32)
    out_specs, out_shape = [whole, whole], [acc, acc]
    for count, at in ((n_other, early), (n_mine, late)):
        out_specs += [
            pl.BlockSpec((1, model, ff), lambda t, at=at: (at(t), 0, 0)),
            pl.BlockSpec((shares, 1, part, ff), lambda t, at=at: (0, at(t), 0, 0)),
        ]
        out_shape += [
            jax.ShapeDtypeStruct((count, model, ff), BF16),
            jax.ShapeDtypeStruct((shares, count, part, ff), BF16),
        ]
    return pl.pallas_call(
        kernel,
        grid=(n_all,),
        in_specs=[whole, pl.BlockSpec((model, tokens), lambda t: (0, 0)), whole]
        + [pl.BlockSpec(memory_space=pl.ANY)] * (len(pieces) + (0 if first else 2)),
        out_specs=out_specs,
        out_shape=out_shape,
        scratch_shapes=[
            pltpu.VMEM((2, model, 2 * ff), BF16),
            pltpu.VMEM((ff, model), BF16),
            pltpu.SemaphoreType.DMA((2, len(chunks[0]))),
            pltpu.SemaphoreType.DMA((2,)),
        ],
        compiler_params=pltpu.CompilerParams(vmem_limit_bytes=56 * 1024 * 1024),
        cost_estimate=pl.CostEstimate(flops=1, bytes_accessed=1, transcendentals=0),
    )(h2, h2_turned, pull, *(() if first else sums), *pieces)


def attention_output(heads, stream, weight, gain, bias, rows):
    owners, tokens, width = heads.shape
    model = owners * width

    def kernel(heads_ref, stream_ref, weight_ref, gain_ref, bias_ref, *outs):
        low_ref, sum_ref, norm_ref, turned_ref = outs
        for d in range(owners):
            low_ref[:, d * width : (d + 1) * width] = heads_ref[d]
        total = stream_ref[...].astype(F32) + nn(low_ref[...], weight_ref[...])
        sum_ref[...] = total
        normed = layer_norm(total, gain_ref[...], bias_ref[...])[0].astype(BF16)
        norm_ref[...] = normed
        turned_ref[...] = normed.T

    fixed = lambda *shape: pl.BlockSpec(shape, lambda i: (0, 0))
    block = pl.BlockSpec((rows, model), lambda i: (i, 0))
    return pl.pallas_call(
        kernel,
        grid=(tokens // rows,),
        in_specs=[
            pl.BlockSpec((owners, rows, width), lambda i: (0, i, 0)),
            block,
            fixed(model, model),
            fixed(1, model),
            fixed(1, model),
        ],
        out_specs=[block] * 3 + [pl.BlockSpec((model, rows), lambda i: (0, i))],
        out_shape=[jax.ShapeDtypeStruct((tokens, model), kind) for kind in (BF16, F32, BF16)]
        + [jax.ShapeDtypeStruct((model, tokens), BF16)],
        compiler_params=pltpu.CompilerParams(vmem_limit_bytes=48 * 1024 * 1024),
        cost_estimate=pl.CostEstimate(flops=1, bytes_accessed=1, transcendentals=0),
    )(heads, stream, weight, gain[None], bias[None])


def norm_gradient(total, grad, direct, weight, gain, owners, rows):
    tokens, model = total.shape
    width = model // owners

    def kernel(total_ref, grad_ref, direct_ref, weight_ref, gain_ref, resid_ref, low_ref, heads_ref, vec_ref):
        i = pl.program_id(0)
        values = total_ref[...]
        centred = values - jnp.mean(values, -1, keepdims=True)
        inv_std = lax.rsqrt(jnp.mean(centred * centred, -1, keepdims=True) + EPSILON)
        normed = centred * inv_std
        grads = grad_ref[...]
        result = direct_ref[...].astype(F32) + norm_back(grads, normed, inv_std, gain_ref[...])
        resid_ref[...] = result
        low = result.astype(BF16)
        low_ref[...] = low
        back = nt(low, weight_ref[...]).astype(BF16)
        for d in range(owners):
            heads_ref[d] = back[:, d * width : (d + 1) * width]
        for_gain = jnp.sum(grads * normed, 0, keepdims=True)
        for_bias = jnp.sum(grads, 0, keepdims=True)

        @pl.when(i == 0)
        def _():
            vec_ref[...] = jnp.zeros_like(vec_ref)

        vec_ref[0:1, :] += for_gain
        vec_ref[1:2, :] += for_bias

    fixed = lambda *shape: pl.BlockSpec(shape, lambda i: (0, 0))
    block = pl.BlockSpec((rows, model), lambda i: (i, 0))
    return pl.pallas_call(
        kernel,
        grid=(tokens // rows,),
        in_specs=[block, block, block, fixed(model, model), fixed(1, model)],
        out_specs=[
            block,
            block,
            pl.BlockSpec((owners, rows, width), lambda i: (0, i, 0)),
            fixed(8, model),
        ],
        out_shape=[
            jax.ShapeDtypeStruct((tokens, model), F32),
            jax.ShapeDtypeStruct((tokens, model), BF16),
            jax.ShapeDtypeStruct((owners, tokens, width), BF16),
            jax.ShapeDtypeStruct((8, model), F32),
        ],
        compiler_params=pltpu.CompilerParams(vmem_limit_bytes=48 * 1024 * 1024),
        cost_estimate=pl.CostEstimate(flops=1, bytes_accessed=1, transcendentals=0),
    )(total, grad, direct, weight, gain[None])


def input_parts(slopes, weight, away):
    count, tokens, columns = slopes.shape
    model = weight.shape[0]
    half = tokens // 2

    def kernel(slope_ref, weight_ref, away_ref, *outs):
        t = pl.program_id(0)
        for h in range(2):
            rows = slice(h * half, (h + 1) * half)
            part = nt(slope_ref[0, rows, :], weight_ref[...]) + away_ref[0, rows, :].astype(F32)
            for k in range(count):

                @pl.when(t == k)
                def _(k=k, h=h, part=part):
                    outs[2 * k + h][...] = part.astype(BF16)

    out = pl.pallas_call(
        kernel,
        grid=(count,),
        in_specs=[
            pl.BlockSpec((1, tokens, columns), lambda t: (t, 0, 0)),
            pl.BlockSpec((model, columns), lambda t: (0, 0)),
            pl.BlockSpec((1, tokens, model), lambda t: (t, 0, 0)),
        ],
        out_specs=[pl.BlockSpec((half, model), lambda t: (0, 0))] * (2 * count),
        out_shape=[jax.ShapeDtypeStruct((half, model), BF16)] * (2 * count),
        compiler_params=pltpu.CompilerParams(vmem_limit_bytes=48 * 1024 * 1024),
        cost_estimate=pl.CostEstimate(flops=1, bytes_accessed=1, transcendentals=0),
    )(slopes, weight, away)
    return [(out[2 * k], out[2 * k + 1]) for k in range(count)]


def projection_gradient(normed, slopes, weight, columns):
    count, width = slopes.shape
    model = normed.shape[1]
    block = min(512, count)
    steps = count // block

    def kernel(normed_ref, slope_ref, weight_ref, columns_ref, out_ref, acc, sums):
        t = pl.program_id(0)
        grad = tn(slope_ref[...], normed_ref[...])
        summed = jnp.sum(slope_ref[...].astype(F32), 0, keepdims=True)

        @pl.when(t == 0)
        def _():
            acc[...] = grad
            sums[...] = summed

        @pl.when(t > 0)
        def _():
            acc[...] += grad
            sums[...] += summed

        @pl.when(t == steps - 1)
        def _():
            whole = acc[...].T
            wide = weight_ref[...].astype(F32)
            given = columns_ref[...]
            bias = jnp.sum(wide * sums[...], 1, keepdims=True)
            gain = jnp.sum(wide * whole, 1, keepdims=True)
            gain = (gain - given[:, 1:2] * bias) / given[:, 0:1]
            lane = lax.broadcasted_iota(jnp.int32, given.shape, 1)
            vectors = jnp.where(lane == 0, gain, jnp.where(lane == 1, bias, given))
            out_ref[:, :width] = whole.astype(BF16)
            out_ref[:, width:] = vectors.astype(BF16)

    return pl.pallas_call(
        kernel,
        grid=(steps,),
        in_specs=[
            pl.BlockSpec((block, model), lambda t: (t, 0)),
            pl.BlockSpec((block, width), lambda t: (t, 0)),
            pl.BlockSpec((model, width), lambda t: (0, 0)),
            pl.BlockSpec((model, 128), lambda t: (0, 0)),
        ],
        out_specs=pl.BlockSpec((model, width + 128), lambda t: (0, 0)),
        out_shape=jax.ShapeDtypeStruct((model, width + 128), BF16),
        scratch_shapes=[pltpu.VMEM((width, model), F32), pltpu.VMEM((1, width), F32)],
        compiler_params=pltpu.CompilerParams(vmem_limit_bytes=48 * 1024 * 1024),
        cost_estimate=pl.CostEstimate(flops=1, bytes_accessed=1, transcendentals=0),
    )(normed, slopes, weight, columns)


def join_lower(mine, away):
    shares, _, part, ff = mine[0].shape
    counts = [each.shape[1] for each in mine]
    n = len(mine)

    def kernel(*refs):
        at = 0
        for k, count in enumerate(counts):
            refs[-1][0, at : at + count] = add(refs[k][0], refs[n + k][0])
            at += count

    spec = lambda count: pl.BlockSpec((1, count, part, ff), lambda z: (z, 0, 0, 0))
    return pl.pallas_call(
        kernel,
        grid=(shares,),
        in_specs=[spec(count) for count in counts] * 2,
        out_specs=spec(sum(counts)),
        out_shape=jax.ShapeDtypeStruct((shares, sum(counts), part, ff), BF16),
        compiler_params=pltpu.CompilerParams(vmem_limit_bytes=48 * 1024 * 1024),
        cost_estimate=pl.CostEstimate(flops=1, bytes_accessed=6 * shares * part * ff * sum(counts), transcendentals=0),
    )(*mine, *away)


def join_upper(mine, away, outer, outer_away):
    _, model, ff = mine[0].shape
    counts = [each.shape[0] for each in mine]
    n, half, extra = len(mine), model // 2, outer.shape[2]

    def kernel(*refs):
        ins, outs = refs[: 2 * n + 2], refs[2 * n + 2 :]
        k = 0
        for i, count in enumerate(counts):
            for j in range(count):
                for h in range(2):
                    rows = slice(h * half, (h + 1) * half)
                    outs[2 * k + h][:half, :] = add(ins[i][j, rows, :], ins[n + i][j, rows, :])
                    outs[2 * k + h][half:, :] = add(ins[2 * n][k, h], ins[2 * n + 1][k, h])
                k += 1

    out = pl.pallas_call(
        kernel,
        out_shape=[jax.ShapeDtypeStruct((half + extra, ff), BF16)] * (2 * sum(counts)),
        compiler_params=pltpu.CompilerParams(vmem_limit_bytes=48 * 1024 * 1024),
        cost_estimate=pl.CostEstimate(flops=1, bytes_accessed=6 * model * ff * sum(counts), transcendentals=0),
    )(*mine, *away, outer, outer_away)
    return [[out[2 * k], out[2 * k + 1]] for k in range(sum(counts))]


def outer_gradient(left, right, places, shares):
    tokens, model = left.shape
    owners = places.shape[0]
    part = model // shares
    rows, half = part // owners, model // 2
    per = shares // 2

    def kernel(at_ref, left_ref, right_ref, away_ref, mine_ref, held):
        for z in range(shares):
            held[...] = tn(left_ref[:, z * part : (z + 1) * part], right_ref[...])
            h, at = z // per, z % per * rows
            for k in range(owners):
                ref = mine_ref if k < owners // 2 else away_ref
                block = held[pl.ds(pl.multiple_of(at_ref[k] * rows, rows), rows), :].astype(BF16)
                for j in range(2):
                    lanes = slice(j * half, (j + 1) * half)
                    ref[k % (owners // 2), h, j * per * rows + at : j * per * rows + at + rows, :] = (
                        block[:, lanes]
                    )

    shape = (owners // 2, 2, 2 * per * rows, half)
    whole = lambda *dims: pl.BlockSpec(dims, lambda i, _: (0,) * len(dims))
    return pl.pallas_call(
        kernel,
        grid_spec=pltpu.PrefetchScalarGridSpec(
            num_scalar_prefetch=1,
            grid=(1,),
            in_specs=[whole(tokens, model)] * 2,
            out_specs=[whole(*shape)] * 2,
            scratch_shapes=[pltpu.VMEM((part, model), F32)],
        ),
        out_shape=[jax.ShapeDtypeStruct(shape, BF16)] * 2,
        compiler_params=pltpu.CompilerParams(vmem_limit_bytes=48 * 1024 * 1024),
        cost_estimate=pl.CostEstimate(flops=1, bytes_accessed=8 * model * model, transcendentals=0),
    )(places, left, right)


def absolute(owner):
    a, b, c = lax.axis_index("a"), lax.axis_index("b"), lax.axis_index("c")
    owner = owner ^ (c * 4 + a * 2 + b)
    return (owner % 4) * 2 + owner // 4


def project(pieces, places, owners, groups, rows, gain, bias, weight, before):
    model, columns = weight.shape
    mine, steps = groups * rows, groups
    count = len(pieces)
    stride = places[1] - places[0] if count == 2 else 1

    def place(t):
        k = t // steps
        if count == 2:
            at = places[0] + stride * k
        else:
            at = k
            for i in range(1, count):
                if places[i] - places[i - 1] > 1:
                    at = at + (k >= i) * (places[i] - places[i - 1] - 1)
        return at * steps + t % steps

    def kernel(*refs):
        piece_refs = refs[:count]
        gain_ref, bias_ref, weight_ref = refs[count : count + 3]
        norm_ref, out_ref, held = refs[-3:]
        t = pl.program_id(0)
        for k in range(count):

            @pl.when(t // steps == k)
            def _(k=k):
                held[...] = piece_refs[k][...]

        values = held[...].astype(F32)
        normed = layer_norm(values, gain_ref[...], bias_ref[...])[0].astype(BF16)
        norm_ref[...] = normed
        out_ref[...] = nn(normed, weight_ref[...]).astype(BF16)

    specs = [
        pl.BlockSpec((rows, model), lambda t, k=k: (jnp.clip(t - k * steps, 0, steps - 1), 0))
        for k in range(count)
    ]
    fixed = lambda shape: pl.BlockSpec(shape, lambda t: (0, 0))
    specs += [fixed((1, model)), fixed((1, model)), fixed((model, columns))]
    extra = () if before is None else before
    return pl.pallas_call(
        kernel,
        grid=(count * steps,),
        in_specs=specs + [pl.BlockSpec(memory_space=pl.ANY)] * len(extra),
        out_specs=[
            pl.BlockSpec((rows, model), lambda t: (place(t), 0)),
            pl.BlockSpec((rows, columns), lambda t: (place(t), 0)),
        ],
        out_shape=[
            jax.ShapeDtypeStruct((owners * mine, model), BF16),
            jax.ShapeDtypeStruct((owners * mine, columns), BF16),
        ],
        scratch_shapes=[pltpu.VMEM((rows, model), BF16)],
        input_output_aliases={count + 3 + i: i for i in range(len(extra))},
        compiler_params=pltpu.CompilerParams(vmem_limit_bytes=48 * 1024 * 1024),
        cost_estimate=pl.CostEstimate(flops=1, bytes_accessed=1, transcendentals=0),
    )(*pieces, gain[None], bias[None], weight, *extra)


def pack(parts, packed, shares):
    model = packed.shape[0]
    part, half = model // shares, model // 2
    low = part // 2
    outer = (parts[0][0].shape[0] - half) // 2
    per = shares // 2
    out_rows = outer // per
    rows = low + out_rows + low
    flat = [each for terms in parts for each in terms]

    def kernel(*refs):
        packed_ref, out_ref = refs[-2], refs[-1]
        it = iter(refs)
        groups = [[next(it) for _ in terms] for terms in parts]

        def total(refs, at, count):
            summed = refs[0][at : at + count, :].astype(F32)
            for ref in refs[1:]:
                summed = summed + ref[at : at + count, :].astype(F32)
            return summed.astype(BF16)

        for z in range(shares):
            terms, side = groups[z // per], z % per
            for j in range(2):
                lanes = slice(j * half, (j + 1) * half)
                out_ref[z, :low, lanes] = total(terms, side * part + j * low, low)
                out_ref[z, low : low + out_rows, lanes] = total(
                    terms, half + j * outer + side * out_rows, out_rows
                )
                at = z * part + j * low
                out_ref[z, low + out_rows :, lanes] = packed_ref[at : at + low, :]

    return pl.pallas_call(
        kernel,
        out_shape=jax.ShapeDtypeStruct((shares, rows, model), BF16),
        compiler_params=pltpu.CompilerParams(vmem_limit_bytes=48 * 1024 * 1024),
    )(*flat, packed)


def unpack_lower(pieces, places, shares):
    owners = len(pieces)
    part, ff = pieces[0].shape
    parts = part * shares // ff
    rows = part // parts

    def kernel(at_ref, *refs):
        for k in range(owners):
            refs[-1][at_ref[k]] = refs[k][...].astype(F32)

    result = pl.pallas_call(
        kernel,
        grid_spec=pltpu.PrefetchScalarGridSpec(
            num_scalar_prefetch=1,
            grid=(parts,),
            in_specs=[pl.BlockSpec((rows, ff), lambda i, _: (i, 0))] * owners,
            out_specs=pl.BlockSpec((owners, rows, ff), lambda i, _: (0, 0, i)),
        ),
        out_shape=jax.ShapeDtypeStruct((owners, rows, parts * ff), F32),
        compiler_params=pltpu.CompilerParams(vmem_limit_bytes=48 * 1024 * 1024),
    )(places, *pieces)
    return result.reshape(owners * rows, parts * ff)


def unpack(pieces, places, shares, part, width):
    owners = len(pieces)
    rows, model = pieces[0].shape
    half, low = model // 2, part // 2
    out_rows = part // owners
    steps = 4
    block = low // steps
    outer_block = 16

    def kernel(at_ref, *refs):
        mains, outers, projs = refs[:owners], refs[owners : 2 * owners], refs[2 * owners : 3 * owners]
        up_ref, outer_ref, proj_ref, *vec_refs, held = refs[3 * owners :]
        i = pl.program_id(0)
        for j in range(2):
            at = j * half + 3 * width
            vectors = [proj[:, at : at + 128].astype(F32) for proj in projs]
            rows = pl.ds(pl.multiple_of(j * low + i * block, block), block)
            held[rows, :] = functools.reduce(jnp.add, vectors)

        @pl.when(i == steps - 1)
        def _():
            vectors = held[...].T
            for k, ref in enumerate(vec_refs):
                ref[...] = vectors[k : k + 1, :]

        for k in range(owners):
            d = at_ref[k]
            lane = lambda base: pl.ds(pl.multiple_of(base + d * width, width), width)
            outer_ref[d] = outers[k][...].astype(F32)
            for j in range(2):
                for z in range(shares):
                    at = j * half + z * width
                    up_ref[j, :, lane(z * owners * width)] = mains[k][:, at : at + width].astype(F32)
                for t in range(3):
                    at = j * half + t * width
                    proj_ref[j, :, lane(t * model)] = projs[k][:, at : at + width].astype(F32)

    outer_at, proj_at = low // outer_block, (low + out_rows) // block
    outer_steps = out_rows // outer_block
    results = pl.pallas_call(
        kernel,
        grid_spec=pltpu.PrefetchScalarGridSpec(
            num_scalar_prefetch=1,
            grid=(steps,),
            in_specs=[pl.BlockSpec((block, model), lambda i, _: (i, 0))] * owners
            + [
                pl.BlockSpec(
                    (outer_block, model), lambda i, _: (outer_at + i * outer_steps // steps, 0)
                )
            ]
            * owners
            + [pl.BlockSpec((block, model), lambda i, _: (proj_at + i, 0))] * owners,
            out_specs=[
                pl.BlockSpec((2, block, shares * model), lambda i, _: (0, i, 0)),
                pl.BlockSpec(
                    (owners, outer_block, model), lambda i, _: (0, i * outer_steps // steps, 0)
                ),
                pl.BlockSpec((2, block, 3 * model), lambda i, _: (0, i, 0)),
            ]
            + [pl.BlockSpec((1, part), lambda i, _: (0, 0))] * 4,
            scratch_shapes=[pltpu.VMEM((part, 128), F32)],
        ),
        out_shape=[
            jax.ShapeDtypeStruct((2, low, shares * model), F32),
            jax.ShapeDtypeStruct((owners, out_rows, model), F32),
            jax.ShapeDtypeStruct((2, low, 3 * model), F32),
        ]
        + [jax.ShapeDtypeStruct((1, part), F32)] * 4,
        compiler_params=pltpu.CompilerParams(vmem_limit_bytes=56 * 1024 * 1024),
    )(places, *pieces, *pieces, *pieces)
    upper, outer, proj, *vectors = results
    return (
        upper.reshape(part, shares * model),
        outer.reshape(part, model),
        proj.reshape(part, 3 * model),
        [each.reshape(part) for each in vectors],
    )


def flip(value, axis):
    return lax.ppermute(value, axis, [(0, 1), (1, 0)])


def after(value, *others):
    return lax.optimization_barrier((value, *others))[0]


def spread_near(value):
    return [value, flip(value, "b"), flip(value, "a")]


def spread_far(near):
    half = near[0].shape[0] // 2
    return [flip(near[2][:half], "b"), flip(near[1][half:], "a")]


def spread(value):
    if lax.axis_size("a") != 2:
        return list(lax.all_gather(value, CTX, axis=0, tiled=False))
    half = value.shape[0] // 2
    from_b, from_a = flip(value, "b"), flip(value, "a")
    far = jnp.concatenate([flip(from_a[:half], "b"), flip(from_b[half:], "a")], 0)
    near = [value, from_b, from_a]
    return near + [far] + [flip(after(each, far), "c") for each in near] + [flip(far, "c")]


def add(u, v):
    return (u.astype(F32) + v.astype(F32)).astype(BF16)


def converge_first(from_b, from_a, far):
    far_0, far_1 = flip(far[0], "b"), flip(far[1], "a")
    b_0, a_1 = flip(from_b[0], "b"), flip(from_a[1], "a")
    return add(from_b[1], far_1), add(from_a[0], far_0), b_0, a_1


def converge_last(own, first):
    b_1, a_0, b_0, a_1 = first
    return (own[0], b_0, flip(a_0, "a")), (own[1], flip(b_1, "b"), a_1)


def total(terms):
    return sum(each.astype(F32) for each in terms[1:]) + terms[0].astype(F32)


def shards(
    tokens,
    out_grad,
    seg_ids,
    positions,
    ln1_gain,
    ln1_bias,
    w_qkv,
    w_out,
    ln2_gain,
    ln2_bias,
    w_up,
    w_down,
):
    groups, rows, model = tokens.shape
    owners, shares = lax.axis_size(CTX), lax.axis_size("z")
    square = lax.axis_size("a") == 2
    width = model // owners
    heads = HEADS // owners
    mine = groups * rows
    part = model // shares
    full_ff = w_up.shape[1]
    ff = full_ff // owners
    ff_rows = ff // shares
    ff_parts = model // ff
    me = lax.axis_index(CTX)
    core = lax.axis_index("c")

    first_seg, first_pos = seg_ids[:, ::UNIT], positions[:, ::UNIT]
    slot = jnp.where(
        first_seg == 0,
        first_pos // UNIT,
        PROMPT // UNIT + (first_seg - 1) * (CONT // UNIT) + first_pos // UNIT,
    )
    per_group = rows // UNIT
    note = jnp.zeros((32, model), BF16).at[0, : groups * per_group].set(
        slot.reshape(-1).astype(BF16)
    )
    sent = jnp.concatenate([tokens.reshape(mine, model), note], 0)
    if square:
        near_pieces = spread_near(sent)
        far_halves = spread_far(near_pieces)
        pieces = [sent] + near_pieces[1:3]
    else:
        pieces = spread(sent)
    places = jnp.arange(owners, dtype=jnp.int32)
    if square:
        places = absolute(places)

    columns = [
        lax.dynamic_slice_in_dim(w_qkv, t * model + me * width, width, 1) for t in range(3)
    ]
    norms = jnp.stack([ln1_gain, ln1_bias, ln2_gain, ln2_bias], 0)
    norms = jnp.pad(norms.reshape(-1, 64), ((0, 0), (0, 3 * width - 64)))
    packed = jnp.concatenate(columns, 1)
    packed = jnp.concatenate([packed, norms], 0)
    packed = lax.all_gather(packed, "z", axis=0, tiled=True)
    up_part = [
        lax.dynamic_slice_in_dim(w_up, (z * owners + me) * ff_rows, ff_rows, 1)
        for z in range(shares)
    ]
    down_part = lax.dynamic_slice_in_dim(w_down, me * ff_rows, ff_rows, 0)
    down_part = jnp.concatenate([down_part[:, j * ff : (j + 1) * ff] for j in range(ff_parts)], 0)
    chunk = jnp.concatenate(up_part + [down_part], 1)
    chunk, packed, pieces[1], pieces[2] = lax.optimization_barrier(
        (chunk, packed, pieces[1], pieces[2])
    )
    chunk = lax.all_gather(chunk, "z", axis=0, tiled=True)

    packed = packed.reshape(shares, -1, 3 * width)
    w_heads = packed[:, :part].reshape(model, 3 * width)
    vectors = packed[:, part:, :64].astype(F32).reshape(shares, 4, part)
    vectors = vectors.transpose(1, 0, 2).reshape(4, model)
    gain_one, bias_one, gain_two, bias_two = vectors[0], vectors[1], vectors[2], vectors[3]

    half = w_out.shape[0] // 2
    piece = lax.dynamic_slice_in_dim(w_out, core * half, half, 0)

    def projection(pieces, chosen, before):
        return project(
            pieces, chosen, owners, groups, rows, gain_one, bias_one, w_heads, before
        )

    if square:
        near_pieces += [flip(each, "c") for each in near_pieces]
        projected = projection(near_pieces, [0, 1, 2, 4, 5, 6], None)
        far_halves[0], far_halves[1], *projected = lax.optimization_barrier(
            (*far_halves, *projected)
        )
        far = jnp.concatenate(far_halves, 0)
        pieces = near_pieces[:3] + [far] + near_pieces[3:] + [flip(far, "c")]
        attn_in, qkv = projection([far, pieces[7]], [3, 7], projected)
    else:
        attn_in, qkv = projection(pieces, list(range(owners)), None)
    slots = jnp.concatenate([each[mine, : groups * per_group] for each in pieces])
    slots = slots.astype(jnp.int32)
    qkv = qkv.reshape(owners, groups, rows, 3 * width)
    attended = forward_attention(heads, width, qkv, 0, slots, places, [])
    for g in range(1, groups):
        if square and g == 1:
            near_chunks = spread_near(after(chunk, attended[0]))
        attended = forward_attention(heads, width, qkv, g, slots, places, attended)
    attn_heads, exact, logs = attended
    whole_out = lax.all_gather(after(piece, attn_heads), ("z", "c"), axis=0, tiled=True)
    attn_heads = lax.all_to_all(
        attn_heads.reshape(owners, mine, width), CTX, split_axis=0, concat_axis=0, tiled=True
    )
    flat = tokens.reshape(mine, model)
    if square:
        near_chunks = [after(each, attn_heads) for each in near_chunks]
        other_chunks = [flip(each, "c") for each in near_chunks]
    attn_low, residual, *ffn_in = attention_output(
        attn_heads, flat, whole_out, gain_two, bias_two, rows
    )
    grad_low = out_grad.reshape(mine, model)

    def feed(sums, others, mine):
        out_sum, in_sum, *grads = feed_forward(*ffn_in, grad_low, sums, others, mine, shares)
        chunk_grads.append(grads)
        return out_sum, in_sum

    sums, chunk_grads = None, []
    if square:
        sums = feed(sums, [[each] for each in other_chunks], [[each] for each in near_chunks])
        far_chunk = spread_far(near_chunks)
        far_chunk[0], far_chunk[1], *sums = lax.optimization_barrier((*far_chunk, *sums))
        sums = feed(sums, [[flip(part, "c") for part in far_chunk]], [far_chunk])
    else:
        chunks = [[each] for each in spread(chunk)]
        for k in range(0, owners, 4):
            sums = feed(sums, chunks[k : k + 2], chunks[k + 2 : k + 4])
    output = (residual + sums[0]).astype(BF16)
    grad_resid, grad_branch, grad_heads, norm_grads = norm_gradient(
        residual, sums[1], grad_low, whole_out, gain_two, owners, rows
    )
    grad_gain_two, grad_bias_two = norm_grads[0], norm_grads[1]
    late = [grad_branch] + [each for grads in chunk_grads for each in grads]
    grad_heads, grad_branch, *late = lax.optimization_barrier((grad_heads, *late))
    chunk_grads = [late[:4], late[4:8]] if square else chunk_grads
    grad_heads = lax.all_to_all(
        grad_heads, CTX, split_axis=0, concat_axis=0, tiled=True
    ).reshape(owners, groups, rows, width)
    out_rows = part // owners

    if square:
        outer_away, outer = outer_gradient(attn_low, grad_branch, places, shares)
        halves = join_upper(
            [each[2] for each in chunk_grads],
            [flip(each[0], "c") for each in chunk_grads],
            outer,
            flip(outer_away, "c"),
        )
        lower = join_lower(
            [
                after(each[3], grad_heads, *[half for pair in halves for half in pair])
                for each in chunk_grads
            ],
            [flip(each[1], "c") for each in chunk_grads],
        )
        grad_heads = after(grad_heads, lower)
        lower = lax.psum_scatter(
            lower.reshape(shares * 4, part, ff), "z", scatter_dimension=0, tiled=True
        )
    else:
        lower = jnp.concatenate([low for _, a, _, b in chunk_grads for low in (a, b)], 1)
        lower = lax.psum_scatter(lower, CTX, scatter_dimension=1, tiled=True)
        lower = lower.reshape(shares, part, ff)
        upper = jnp.concatenate([up for a, _, b, _ in chunk_grads for up in (a, b)], 0)
        upper = lax.psum_scatter(upper, CTX, scatter_dimension=0, tiled=True)
        upper = upper.reshape(shares, part, ff)
        outer = tn(attn_low, grad_branch).astype(BF16)
        outer = outer.reshape(shares, owners, out_rows, model).transpose(1, 0, 2, 3)
        outer = lax.psum_scatter(
            outer.reshape(model, model), CTX, scatter_dimension=0, tiled=True
        )
    if square:
        first = converge_first(*halves[1:])
    grad_qkv = backward_attention(heads, width, qkv, grad_heads, exact, logs, slots, places)
    if square:
        columns = jnp.stack([gain_one, bias_one, grad_gain_two, grad_bias_two], 1)
        columns = jnp.pad(columns, ((0, 0), (0, 124)))
        *first, columns, grad_qkv = lax.optimization_barrier((*first, columns, grad_qkv))
        upper_terms = converge_last(halves[0], first)
        grad_qkv = grad_qkv.reshape(owners, mine, 3 * width)
        away = nt(grad_qkv[4:].reshape(4 * mine, 3 * width), w_heads).astype(BF16)
        grad_qkv = after(grad_qkv, away)
        away = flip(away, "c").reshape(4, mine, model)
        pairs = input_parts(grad_qkv[:4], w_heads, away)
        second = converge_first(*pairs[1:])
        terms = converge_last(pairs[0], second)
        grad_attn_in = jnp.concatenate([total(each) for each in terms], 0)
        grad_qkv = after(
            grad_qkv, *[each for group in (*pairs, *upper_terms) for each in group]
        )
        packed_grad = projection_gradient(
            attn_in, grad_qkv.reshape(owners * mine, 3 * width), w_heads, columns
        )
        packed_grad = after(packed_grad, lower, *second[:2])
    else:
        grad_qkv = grad_qkv.reshape(owners * mine, 3 * width)
        away = nt(grad_qkv, w_heads).astype(BF16)
        grad_attn_in = lax.psum_scatter(away, CTX, scatter_dimension=0, tiled=True).astype(F32)
        grad_columns = tn(attn_in, grad_qkv)
        w_wide = w_heads.astype(F32)
        summed = jnp.sum(grad_qkv.astype(F32), 0)
        grad_bias_one = jnp.sum(w_wide * summed, 1)
        grad_gain_one = (jnp.sum(w_wide * grad_columns, 1) - bias_one * grad_bias_one) / gain_one
        vector_grads = jnp.stack([grad_gain_one, grad_bias_one, grad_gain_two, grad_bias_two], 1)
        packed_grad = jnp.concatenate(
            [grad_columns, vector_grads, jnp.zeros((model, 124), F32)], 1
        ).astype(BF16)

    if square:
        lower = after(lower, grad_attn_in)
        lower = lower[0].astype(F32) + sum(
            flip(lower[k], axis).astype(F32) for k, axis in ((1, "b"), (2, "a"))
        ) + lax.ppermute(lower[3], ("a", "b"), [(0, 3), (3, 0), (1, 2), (2, 1)]).astype(F32)
        lower = lower.astype(BF16)
        grad_down = unpack_lower(spread(lower), places, shares)
        everything = pack(upper_terms, packed_grad, shares)
        everything = lax.psum_scatter(
            everything.reshape(-1, model), "z", scatter_dimension=0, tiled=True
        )
        grad_upper, grad_outer, grad_proj, vector_grads = unpack(
            spread(after(everything, lower)), places, shares, part, width
        )
    else:
        span = 2 * ff
        per_part = packed_grad.shape[1] * part // span
        everything = jnp.concatenate(
            [
                jnp.concatenate([upper, lower], 2),
                outer.reshape(shares, -1, span),
                packed_grad.reshape(shares, per_part, span),
            ],
            1,
        )
        everything = lax.psum_scatter(
            everything.reshape(-1, span), "z", scatter_dimension=0, tiled=True
        )
        everything = lax.all_gather(everything, CTX, axis=0, tiled=False)
        grad_upper = (
            everything[:, :part, :ff]
            .reshape(owners, part, shares, ff_rows)
            .transpose(1, 2, 0, 3)
            .reshape(part, full_ff)
            .astype(F32)
        )
        grad_down = (
            everything[:, :part, ff:]
            .reshape(owners, ff_parts, ff_rows, ff)
            .transpose(0, 2, 1, 3)
            .reshape(owners * ff_rows, model)
            .astype(F32)
        )
        at = part + out_rows * model // span
        grad_outer = everything[:, part:at].reshape(part, model).astype(F32)
        packed_grad = everything[:, at:].reshape(owners, part, -1).astype(F32)
        grad_proj = (
            packed_grad[:, :, : 3 * width]
            .reshape(owners, part, 3, width)
            .transpose(1, 2, 0, 3)
            .reshape(part, 3 * model)
        )
        vector_grads = jnp.sum(packed_grad[:, :, 3 * width : 3 * width + 4], 0).T

    attn_full, attn_norm, attn_rstd = layer_norm(flat.astype(F32), gain_one, bias_one)
    in_grad = (grad_resid + norm_back(grad_attn_in, attn_norm, attn_rstd, gain_one)).astype(BF16)

    return (
        output.reshape(tokens.shape),
        in_grad.reshape(tokens.shape),
        vector_grads[0],
        vector_grads[1],
        grad_proj,
        grad_outer,
        vector_grads[2],
        vector_grads[3],
        grad_upper,
        grad_down,
    )


def solution(mesh):
    ctx, wsh = mesh.shape["ctx"], mesh.shape["wsh"]
    fine = Mesh(mesh.devices.reshape(ctx // 4, 2, 2, wsh), ("a", "b", "c", "z"))
    toks = P("z", CTX, None)
    ints = P("z", CTX)
    vec, mat = P("z"), P("z", None)
    in_specs = (toks, toks, ints, ints, vec, vec, mat, mat, vec, vec, mat, mat)
    out_specs = (toks, toks, vec, vec, mat, mat, vec, vec, mat, mat)
    return jax.shard_map(shards, mesh=fine, in_specs=in_specs, out_specs=out_specs, check_vma=False)
```

```python
import functools

import jax
import jax.numpy as jnp
from jax import lax
from jax.experimental import pallas as pl
from jax.experimental.pallas import tpu as pltpu
from jax.sharding import Mesh
from jax.sharding import PartitionSpec as P

HEADS = 16
PROMPT = 1024
CONT = 256
UNIT = 64
TILE = 256
EPSILON = 1e-05
NEG_BIG = -1e30
CTX = ("a", "b", "c")
F32 = jnp.float32
BF16 = jnp.bfloat16


def layer_norm(values, gain, bias):
    average = jnp.mean(values, -1, keepdims=True)
    centred = values - average
    inv_std = lax.rsqrt(jnp.mean(centred * centred, -1, keepdims=True) + EPSILON)
    normed = centred * inv_std
    return (normed * gain + bias, normed, inv_std)


def norm_back(grad_out, normed, inv_std, gain):
    scaled = grad_out * gain
    return inv_std * (
        scaled
        - jnp.mean(scaled, -1, keepdims=True)
        - normed * jnp.mean(scaled * normed, -1, keepdims=True)
    )


def gelu_exact(values):
    return jax.nn.gelu(values, approximate=False)


def nn(left, right):
    return jnp.dot(left, right, preferred_element_type=F32)


def nt(left, right):
    return lax.dot_general(left, right, (((1,), (1,)), ((), ())), preferred_element_type=F32)


def tn(left, right):
    return lax.dot_general(left, right, (((0,), (0,)), ((), ())), preferred_element_type=F32)


def forward_attention(heads, width, qkv, g, slots, places, before):
    owners, groups, rows, _ = qkv.shape
    total = owners * rows
    per_owner = rows // UNIT
    size = width // heads
    scale = size**-0.5

    units = [(k, u) for k in range(owners) for u in range(per_owner)]

    def kernel(slot_ref, at_ref, qkv_ref, *refs):
        out_ref, exact_ref, log_ref, qs, ks, vs, vt, low = refs[-8:]

        def canonical(k, u):
            slot = slot_ref[(k * groups + g) * per_owner + u]
            return pl.ds(pl.multiple_of(slot * UNIT, UNIT), UNIT)

        for k, u in units:
            block = qkv_ref[k, 0, u * UNIT : (u + 1) * UNIT, :]
            here = canonical(k, u)
            qs[here, :] = block[:, :width] * scale
            ks[here, :] = block[:, width : 2 * width]
            vs[here, :] = block[:, 2 * width :]
        vt[...] = vs[...].T
        row = lax.broadcasted_iota(jnp.int32, (TILE, TILE), 0)
        col = lax.broadcasted_iota(jnp.int32, (TILE, TILE), 1)
        causal = row <= col
        for i in range(total // TILE):
            here = slice(i * TILE, (i + 1) * TILE)
            before = min(i * TILE, PROMPT)
            outs = []
            for h in range(heads):
                lanes = slice(h * size, (h + 1) * size)
                query = qs[here, lanes]
                own = jnp.where(causal, nt(ks[here, lanes], query), NEG_BIG)
                high = jnp.max(own, 0, keepdims=True)
                if before:
                    past = nt(ks[:before, lanes], query)
                    high = jnp.maximum(high, jnp.max(past, 0, keepdims=True))
                own = jnp.exp(own - high)
                sums = jnp.sum(own, 0, keepdims=True)
                mixed = nn(vt[lanes, here], own.astype(BF16))
                if before:
                    past = jnp.exp(past - high)
                    sums = sums + jnp.sum(past, 0, keepdims=True)
                    mixed = mixed + nn(vt[lanes, :before], past.astype(BF16))
                log_ref[0, h : h + 1, here] = high + jnp.log(sums)
                outs.append(mixed / sums)
            both = jnp.concatenate(outs, 0) if heads > 1 else outs[0]
            exact_ref[0, :, here] = both
            low[here, :] = both.T.astype(BF16)
        for k, u in units:
            out_ref[at_ref[k], 0, u * UNIT : (u + 1) * UNIT, :] = low[canonical(k, u), :]

    return pl.pallas_call(
        kernel,
        grid_spec=pltpu.PrefetchScalarGridSpec(
            num_scalar_prefetch=2,
            grid=(1,),
            in_specs=[pl.BlockSpec((owners, 1, rows, 3 * width), lambda i, *_: (0, g, 0, 0))]
            + [pl.BlockSpec(memory_space=pl.ANY)] * len(before),
            out_specs=[
                pl.BlockSpec((owners, 1, rows, width), lambda i, *_: (0, g, 0, 0)),
                pl.BlockSpec((1, width, total), lambda i, *_: (g, 0, 0)),
                pl.BlockSpec((1, heads, total), lambda i, *_: (g, 0, 0)),
            ],
            scratch_shapes=[pltpu.VMEM((total, width), BF16)] * 3
            + [pltpu.VMEM((width, total), BF16), pltpu.VMEM((total, width), BF16)],
        ),
        out_shape=[
            jax.ShapeDtypeStruct((owners, groups, rows, width), BF16),
            jax.ShapeDtypeStruct((groups, width, total), F32),
            jax.ShapeDtypeStruct((groups, heads, total), F32),
        ],
        input_output_aliases={3 + i: i for i in range(len(before))},
        compiler_params=pltpu.CompilerParams(vmem_limit_bytes=48 * 1024 * 1024),
        cost_estimate=pl.CostEstimate(flops=1, bytes_accessed=1, transcendentals=0),
    )(slots, places, qkv, *before)


def backward_attention(heads, width, qkv, grad, exact, logs, slots, places):
    owners, groups, rows, _ = qkv.shape
    total = owners * rows
    per_owner = rows // UNIT
    size = width // heads
    scale = size**-0.5
    wide = 4 * TILE
    units = [(k, u) for k in range(owners) for u in range(per_owner)]

    def kernel(slot_ref, at_ref, qkv_ref, grad_ref, exact_ref, log_ref, out_ref, *scratch):
        qs, ks, vs, gs, kt, delta, dqt, dq, dk, dv = scratch
        g = pl.program_id(0)

        def canonical(k, u):
            slot = slot_ref[(k * groups + g) * per_owner + u]
            return pl.ds(pl.multiple_of(slot * UNIT, UNIT), UNIT)

        for k, u in units:
            block = qkv_ref[k, 0, u * UNIT : (u + 1) * UNIT, :]
            here = canonical(k, u)
            qs[here, :] = block[:, :width] * scale
            ks[here, :] = block[:, width : 2 * width]
            vs[here, :] = block[:, 2 * width :]
            gs[here, :] = grad_ref[at_ref[k], 0, u * UNIT : (u + 1) * UNIT, :]
        kt[...] = ks[...].T
        for i in range(total // TILE):
            here = slice(i * TILE, (i + 1) * TILE)
            both = gs[here, :].astype(F32).T * exact_ref[0, :, here]
            for h in range(heads):
                delta[h : h + 1, here] = jnp.sum(
                    both[h * size : (h + 1) * size, :], 0, keepdims=True
                )
        dqt[...] = jnp.zeros_like(dqt)
        for j in range(total // TILE):
            here = slice(j * TILE, (j + 1) * TILE)
            if j * TILE < PROMPT:
                starts = [(j * TILE, TILE)]
                at = (j + 1) * TILE
                if (total - at) % wide:
                    starts.append((at, (total - at) % wide))
                    at += (total - at) % wide
                while at < total:
                    starts.append((at, wide))
                    at += wide
            else:
                starts = [(j * TILE, TILE)]
            for h in range(heads):
                lanes = slice(h * size, (h + 1) * size)
                key, value, key_t = ks[here, lanes], vs[here, lanes], kt[lanes, here]
                grad_key = grad_value = None
                for at, count in starts:
                    there = slice(at, at + count)
                    query, pull = qs[there, lanes], gs[there, lanes]
                    powers = jnp.exp(nt(key, query) - log_ref[0, h : h + 1, there])
                    if at == j * TILE:
                        row = lax.broadcasted_iota(jnp.int32, (TILE, TILE), 0)
                        col = lax.broadcasted_iota(jnp.int32, (TILE, TILE), 1)
                        powers = jnp.where(row <= col, powers, 0.0)
                    slope = powers * (nt(value, pull) - delta[h : h + 1, there])
                    powers, slope = powers.astype(BF16), slope.astype(BF16)
                    more_value, more_key = nn(powers, pull), nn(slope, query)
                    grad_value = more_value if grad_value is None else grad_value + more_value
                    grad_key = more_key if grad_key is None else grad_key + more_key
                    dqt[lanes, there] += nn(key_t, slope)
                dk[here, lanes] = grad_key.astype(BF16)
                dv[here, lanes] = grad_value.astype(BF16)
        for i in range(total // TILE):
            here = slice(i * TILE, (i + 1) * TILE)
            dq[here, :] = (dqt[:, here] * scale).T.astype(BF16)
        for k, u in units:
            here = canonical(k, u)
            for at, ref in enumerate((dq, dk, dv)):
                out_ref[k, 0, u * UNIT : (u + 1) * UNIT, at * width : (at + 1) * width] = ref[
                    here, :
                ]

    by_group = lambda lanes: pl.BlockSpec((owners, 1, rows, lanes), lambda g, *_: (0, g, 0, 0))
    kept = lambda lines: pl.BlockSpec((1, lines, total), lambda g, *_: (g, 0, 0))
    return pl.pallas_call(
        kernel,
        grid_spec=pltpu.PrefetchScalarGridSpec(
            num_scalar_prefetch=2,
            grid=(groups,),
            in_specs=[by_group(3 * width), by_group(width), kept(width), kept(heads)],
            out_specs=by_group(3 * width),
            scratch_shapes=[pltpu.VMEM((total, width), BF16)] * 4
            + [
                pltpu.VMEM((width, total), BF16),
                pltpu.VMEM((heads, total), F32),
                pltpu.VMEM((width, total), F32),
                pltpu.VMEM((total, width), BF16),
                pltpu.VMEM((total, width), BF16),
                pltpu.VMEM((total, width), BF16),
            ],
        ),
        out_shape=jax.ShapeDtypeStruct((owners, groups, rows, 3 * width), BF16),
        compiler_params=pltpu.CompilerParams(vmem_limit_bytes=48 * 1024 * 1024),
        cost_estimate=pl.CostEstimate(
            flops=14 * total * total * width, bytes_accessed=1, transcendentals=0
        ),
    )(slots, places, qkv, grad, exact, logs)


def feed_forward(h2, h2_turned, pull, sums, others, mine, shares):
    tokens, model = h2.shape
    chunks = others + mine
    ff = chunks[0][0].shape[-1] // 2
    parts = model // ff
    part, rows = model // shares, ff // shares
    first = sums is None
    n_other, n_mine, n_all = len(others), len(mine), len(chunks)
    pieces = [piece for chunk in chunks for piece in chunk]
    step = min(ff, TILE)

    def kernel(*refs):
        it = iter(refs)
        h2_ref, h2_t, pull_ref = next(it), next(it), next(it)
        starts = None if first else (next(it), next(it))
        chunk_refs = [[next(it) for _ in chunk] for chunk in chunks]
        out_ref, grad_ref = next(it), next(it)
        targets = (next(it), next(it)), (next(it), next(it))
        held, down_w, sem, sum_sem = next(it), next(it), next(it), next(it)
        t = pl.program_id(0)
        slot = lax.rem(t, 2)

        def fetch(k, into):
            ref = chunk_refs[k][0]
            if len(ref.shape) == 2:
                return [pltpu.make_async_copy(ref, held.at[into], sem.at[into, 0])]
            return [
                pltpu.make_async_copy(
                    ref.at[z, pl.ds(0, part)], held.at[into, pl.ds(z * part, part)], sem.at[into, z]
                )
                for z in range(shares)
            ]

        def fetch_sums():
            return [
                pltpu.make_async_copy(ref, into, sum_sem.at[k])
                for k, (ref, into) in enumerate(zip(starts, (out_ref, grad_ref)))
            ]

        @pl.when(t == 0)
        def _():
            for copy in fetch(0, 0):
                copy.start()
            if first:
                out_ref[...] = jnp.zeros_like(out_ref)
                grad_ref[...] = jnp.zeros_like(grad_ref)
            else:
                for copy in fetch_sums():
                    copy.start()

        for k in range(n_all):

            @pl.when(t == k)
            def _(k=k):
                for copy in fetch(k, k % 2):
                    copy.wait()
                if k + 1 < n_all:
                    for copy in fetch(k + 1, (k + 1) % 2):
                        copy.start()

        for z in range(shares):
            for j in range(parts):
                at = z * part + j * rows
                down_w[z * rows : (z + 1) * rows, j * ff : (j + 1) * ff] = held[
                    slot, at : at + rows, ff:
                ]
        hiddens, slopes = [], []
        for at in range(0, ff, step):
            up = nn(h2_ref[...], held[slot, :, at : at + step])
            cdf = 0.5 * (1.0 + lax.erf(up * (0.5**0.5)))
            slope = cdf + up * (jnp.exp(-0.5 * up * up) * 0.3989422804014327)
            hiddens.append((up * cdf).astype(BF16))
            slopes.append((nt(pull_ref[...], down_w[at : at + step, :]) * slope).astype(BF16))
        hidden = jnp.concatenate(hiddens, 1) if len(hiddens) > 1 else hiddens[0]
        grad_up = jnp.concatenate(slopes, 1) if len(slopes) > 1 else slopes[0]
        if not first:

            @pl.when(t == 0)
            def _():
                for copy in fetch_sums():
                    copy.wait()

        out_ref[...] += nn(hidden, down_w[...])
        grad_ref[...] += nt(grad_up, held[slot, :, :ff])
        grad_upper = nn(h2_t[...], grad_up).astype(BF16)
        grad_lower = tn(hidden, pull_ref[...]).astype(BF16)

        def put(refs):
            refs[0][0] = grad_upper
            for z in range(shares):
                for j in range(parts):
                    refs[1][z, 0, j * rows : (j + 1) * rows, :] = grad_lower[
                        z * rows : (z + 1) * rows, j * ff : (j + 1) * ff
                    ]

        @pl.when(t < n_other)
        def _():
            put(targets[0])

        @pl.when(t >= n_other)
        def _():
            put(targets[1])

    whole = pl.BlockSpec((tokens, model), lambda t: (0, 0))
    early = lambda t: jnp.minimum(t, n_other - 1)
    late = lambda t: jnp.maximum(t - n_other, 0)
    acc = jax.ShapeDtypeStruct((tokens, model), F32)
    out_specs, out_shape = [whole, whole], [acc, acc]
    for count, at in ((n_other, early), (n_mine, late)):
        out_specs += [
            pl.BlockSpec((1, model, ff), lambda t, at=at: (at(t), 0, 0)),
            pl.BlockSpec((shares, 1, part, ff), lambda t, at=at: (0, at(t), 0, 0)),
        ]
        out_shape += [
            jax.ShapeDtypeStruct((count, model, ff), BF16),
            jax.ShapeDtypeStruct((shares, count, part, ff), BF16),
        ]
    return pl.pallas_call(
        kernel,
        grid=(n_all,),
        in_specs=[whole, pl.BlockSpec((model, tokens), lambda t: (0, 0)), whole]
        + [pl.BlockSpec(memory_space=pl.ANY)] * (len(pieces) + (0 if first else 2)),
        out_specs=out_specs,
        out_shape=out_shape,
        scratch_shapes=[
            pltpu.VMEM((2, model, 2 * ff), BF16),
            pltpu.VMEM((ff, model), BF16),
            pltpu.SemaphoreType.DMA((2, shares)),
            pltpu.SemaphoreType.DMA((2,)),
        ],
        compiler_params=pltpu.CompilerParams(vmem_limit_bytes=56 * 1024 * 1024),
        cost_estimate=pl.CostEstimate(flops=1, bytes_accessed=1, transcendentals=0),
    )(h2, h2_turned, pull, *(() if first else sums), *pieces)


def attention_output(heads, stream, weight, core, gain, bias, rows):
    owners, tokens, width = heads.shape
    model = owners * width
    split = isinstance(weight, tuple)
    weights = list(weight) if split else [weight]
    if split:
        shares, lines, _ = weight[0].shape
        half = model // shares // 2
        weight_specs = [
            pl.BlockSpec((shares, half, model), lambda i, _: (0, (lines - half) // half, 0))
        ] * 2
    else:
        weight_specs = [pl.BlockSpec((model, model), lambda i, _: (0, 0))]

    def kernel(core_ref, heads_ref, stream_ref, *refs):
        weight_refs, (gain_ref, bias_ref) = refs[: len(weights)], refs[len(weights) : -5]
        low_ref, sum_ref, norm_ref, turned_ref, whole_ref = refs[-5:]

        @pl.when(pl.program_id(0) == 0)
        def _():
            if split:
                for k, ref in enumerate(weight_refs):
                    side = core_ref[0] if k == 0 else 1 - core_ref[0]
                    for z in range(shares):
                        at = pl.multiple_of((2 * z + side) * half, half)
                        whole_ref[pl.ds(at, half), :] = ref[z]
            else:
                whole_ref[...] = weight_refs[0][...]

        for d in range(owners):
            low_ref[:, d * width : (d + 1) * width] = heads_ref[d]
        total = stream_ref[...].astype(F32) + nn(low_ref[...], whole_ref[...])
        sum_ref[...] = total
        normed = layer_norm(total, gain_ref[...], bias_ref[...])[0].astype(BF16)
        norm_ref[...] = normed
        turned_ref[...] = normed.T

    fixed = lambda *shape: pl.BlockSpec(shape, lambda i, _: (0, 0))
    block = pl.BlockSpec((rows, model), lambda i, _: (i, 0))
    return pl.pallas_call(
        kernel,
        grid_spec=pltpu.PrefetchScalarGridSpec(
            num_scalar_prefetch=1,
            grid=(tokens // rows,),
            in_specs=[pl.BlockSpec((owners, rows, width), lambda i, _: (0, i, 0)), block]
            + weight_specs
            + [fixed(1, model), fixed(1, model)],
            out_specs=[block] * 3
            + [pl.BlockSpec((model, rows), lambda i, _: (0, i)), fixed(model, model)],
        ),
        out_shape=[jax.ShapeDtypeStruct((tokens, model), kind) for kind in (BF16, F32, BF16)]
        + [jax.ShapeDtypeStruct((model, tokens), BF16), jax.ShapeDtypeStruct((model, model), BF16)],
        compiler_params=pltpu.CompilerParams(vmem_limit_bytes=48 * 1024 * 1024),
        cost_estimate=pl.CostEstimate(flops=1, bytes_accessed=1, transcendentals=0),
    )(core.reshape(1).astype(jnp.int32), heads, stream, *weights, gain[None], bias[None])


def norm_gradient(total, grad, direct, weight, gain, owners, rows):
    tokens, model = total.shape
    width = model // owners

    def kernel(total_ref, grad_ref, direct_ref, weight_ref, gain_ref, resid_ref, low_ref, heads_ref, vec_ref):
        i = pl.program_id(0)
        values = total_ref[...]
        centred = values - jnp.mean(values, -1, keepdims=True)
        inv_std = lax.rsqrt(jnp.mean(centred * centred, -1, keepdims=True) + EPSILON)
        normed = centred * inv_std
        grads = grad_ref[...]
        result = direct_ref[...].astype(F32) + norm_back(grads, normed, inv_std, gain_ref[...])
        resid_ref[...] = result
        low = result.astype(BF16)
        low_ref[...] = low
        back = nt(low, weight_ref[...]).astype(BF16)
        for d in range(owners):
            heads_ref[d] = back[:, d * width : (d + 1) * width]
        for_gain = jnp.sum(grads * normed, 0, keepdims=True)
        for_bias = jnp.sum(grads, 0, keepdims=True)

        @pl.when(i == 0)
        def _():
            vec_ref[...] = jnp.zeros_like(vec_ref)

        vec_ref[0:1, :] += for_gain
        vec_ref[1:2, :] += for_bias

    fixed = lambda *shape: pl.BlockSpec(shape, lambda i: (0, 0))
    block = pl.BlockSpec((rows, model), lambda i: (i, 0))
    return pl.pallas_call(
        kernel,
        grid=(tokens // rows,),
        in_specs=[block, block, block, fixed(model, model), fixed(1, model)],
        out_specs=[
            block,
            block,
            pl.BlockSpec((owners, rows, width), lambda i: (0, i, 0)),
            fixed(8, model),
        ],
        out_shape=[
            jax.ShapeDtypeStruct((tokens, model), F32),
            jax.ShapeDtypeStruct((tokens, model), BF16),
            jax.ShapeDtypeStruct((owners, tokens, width), BF16),
            jax.ShapeDtypeStruct((8, model), F32),
        ],
        compiler_params=pltpu.CompilerParams(vmem_limit_bytes=48 * 1024 * 1024),
        cost_estimate=pl.CostEstimate(flops=1, bytes_accessed=1, transcendentals=0),
    )(total, grad, direct, weight, gain[None])


def input_parts(slopes, weight, away):
    count, tokens, columns = slopes.shape
    model = weight.shape[0]
    half = tokens // 2

    def kernel(slope_ref, weight_ref, away_ref, *outs):
        t = pl.program_id(0)
        for h in range(2):
            rows = slice(h * half, (h + 1) * half)
            part = nt(slope_ref[0, rows, :], weight_ref[...]) + away_ref[0, rows, :].astype(F32)
            for k in range(count):

                @pl.when(t == k)
                def _(k=k, h=h, part=part):
                    outs[2 * k + h][...] = part.astype(BF16)

    out = pl.pallas_call(
        kernel,
        grid=(count,),
        in_specs=[
            pl.BlockSpec((1, tokens, columns), lambda t: (t, 0, 0)),
            pl.BlockSpec((model, columns), lambda t: (0, 0)),
            pl.BlockSpec((1, tokens, model), lambda t: (t, 0, 0)),
        ],
        out_specs=[pl.BlockSpec((half, model), lambda t: (0, 0))] * (2 * count),
        out_shape=[jax.ShapeDtypeStruct((half, model), BF16)] * (2 * count),
        compiler_params=pltpu.CompilerParams(vmem_limit_bytes=48 * 1024 * 1024),
        cost_estimate=pl.CostEstimate(flops=1, bytes_accessed=1, transcendentals=0),
    )(slopes, weight, away)
    return [(out[2 * k], out[2 * k + 1]) for k in range(count)]


def projection_gradient(normed, slopes, weight, columns):
    count, width = slopes.shape
    model = normed.shape[1]
    block = min(2048, count)
    steps = count // block

    def kernel(normed_ref, slope_ref, weight_ref, columns_ref, out_ref, acc, sums):
        t = pl.program_id(0)
        grad = tn(slope_ref[...], normed_ref[...])
        summed = jnp.sum(slope_ref[...].astype(F32), 0, keepdims=True)

        @pl.when(t == 0)
        def _():
            acc[...] = grad
            sums[...] = summed

        @pl.when(t > 0)
        def _():
            acc[...] += grad
            sums[...] += summed

        @pl.when(t == steps - 1)
        def _():
            whole = acc[...].T
            wide = weight_ref[...].astype(F32)
            given = columns_ref[...]
            bias = jnp.sum(wide * sums[...], 1, keepdims=True)
            gain = jnp.sum(wide * whole, 1, keepdims=True)
            gain = (gain - given[:, 1:2] * bias) / given[:, 0:1]
            lane = lax.broadcasted_iota(jnp.int32, given.shape, 1)
            vectors = jnp.where(lane == 0, gain, jnp.where(lane == 1, bias, given))
            out_ref[:, :width] = whole.astype(BF16)
            out_ref[:, width:] = vectors.astype(BF16)

    return pl.pallas_call(
        kernel,
        grid=(steps,),
        in_specs=[
            pl.BlockSpec((block, model), lambda t: (t, 0)),
            pl.BlockSpec((block, width), lambda t: (t, 0)),
            pl.BlockSpec((model, width), lambda t: (0, 0)),
            pl.BlockSpec((model, 128), lambda t: (0, 0)),
        ],
        out_specs=pl.BlockSpec((model, width + 128), lambda t: (0, 0)),
        out_shape=jax.ShapeDtypeStruct((model, width + 128), BF16),
        scratch_shapes=[pltpu.VMEM((width, model), F32), pltpu.VMEM((1, width), F32)],
        compiler_params=pltpu.CompilerParams(vmem_limit_bytes=48 * 1024 * 1024),
        cost_estimate=pl.CostEstimate(flops=1, bytes_accessed=1, transcendentals=0),
    )(normed, slopes, weight, columns)


def join_lower(mine, away):
    shares, _, part, ff = mine[0].shape
    counts = [each.shape[1] for each in mine]
    n = len(mine)

    def kernel(*refs):
        at = 0
        for k, count in enumerate(counts):
            refs[-1][0, at : at + count] = add(refs[k][0], refs[n + k][0])
            at += count

    spec = lambda count: pl.BlockSpec((1, count, part, ff), lambda z: (z, 0, 0, 0))
    return pl.pallas_call(
        kernel,
        grid=(shares,),
        in_specs=[spec(count) for count in counts] * 2,
        out_specs=spec(sum(counts)),
        out_shape=jax.ShapeDtypeStruct((shares, sum(counts), part, ff), BF16),
        compiler_params=pltpu.CompilerParams(vmem_limit_bytes=48 * 1024 * 1024),
        cost_estimate=pl.CostEstimate(flops=1, bytes_accessed=6 * shares * part * ff * sum(counts), transcendentals=0),
    )(*mine, *away)


def join_upper(mine, away, outer, outer_away):
    _, model, ff = mine[0].shape
    counts = [each.shape[0] for each in mine]
    n, half, extra = len(mine), model // 2, outer.shape[2]

    def kernel(*refs):
        ins, outs = refs[: 2 * n + 2], refs[2 * n + 2 :]
        k = 0
        for i, count in enumerate(counts):
            for j in range(count):
                for h in range(2):
                    rows = slice(h * half, (h + 1) * half)
                    outs[2 * k + h][:half, :] = add(ins[i][j, rows, :], ins[n + i][j, rows, :])
                    outs[2 * k + h][half:, :] = add(ins[2 * n][k, h], ins[2 * n + 1][k, h])
                k += 1

    out = pl.pallas_call(
        kernel,
        out_shape=[jax.ShapeDtypeStruct((half + extra, ff), BF16)] * (2 * sum(counts)),
        compiler_params=pltpu.CompilerParams(vmem_limit_bytes=48 * 1024 * 1024),
        cost_estimate=pl.CostEstimate(flops=1, bytes_accessed=6 * model * ff * sum(counts), transcendentals=0),
    )(*mine, *away, outer, outer_away)
    return [[out[2 * k], out[2 * k + 1]] for k in range(sum(counts))]


def outer_gradient(left, right, places, shares):
    tokens, model = left.shape
    owners = places.shape[0]
    part = model // shares
    rows, half = part // owners, model // 2
    per = shares // 2

    def kernel(at_ref, left_ref, right_ref, away_ref, mine_ref, held):
        for z in range(shares):
            held[...] = tn(left_ref[:, z * part : (z + 1) * part], right_ref[...])
            h, at = z // per, z % per * rows
            for k in range(owners):
                ref = mine_ref if k < owners // 2 else away_ref
                block = held[pl.ds(pl.multiple_of(at_ref[k] * rows, rows), rows), :].astype(BF16)
                for j in range(2):
                    lanes = slice(j * half, (j + 1) * half)
                    ref[k % (owners // 2), h, j * per * rows + at : j * per * rows + at + rows, :] = (
                        block[:, lanes]
                    )

    shape = (owners // 2, 2, 2 * per * rows, half)
    whole = lambda *dims: pl.BlockSpec(dims, lambda i, _: (0,) * len(dims))
    return pl.pallas_call(
        kernel,
        grid_spec=pltpu.PrefetchScalarGridSpec(
            num_scalar_prefetch=1,
            grid=(1,),
            in_specs=[whole(tokens, model)] * 2,
            out_specs=[whole(*shape)] * 2,
            scratch_shapes=[pltpu.VMEM((part, model), F32)],
        ),
        out_shape=[jax.ShapeDtypeStruct(shape, BF16)] * 2,
        compiler_params=pltpu.CompilerParams(vmem_limit_bytes=48 * 1024 * 1024),
        cost_estimate=pl.CostEstimate(flops=1, bytes_accessed=8 * model * model, transcendentals=0),
    )(places, left, right)


def take_chunk(w_up, w_down, device, owners, w_out=None, core=0):
    part, full = w_up.shape
    model = w_down.shape[1]
    ff = full // owners
    shares = model // part
    rows = ff // shares
    parts = model // ff
    if rows % 128:
        up = [
            lax.dynamic_slice_in_dim(w_up, (z * owners + device) * rows, rows, 1)
            for z in range(shares)
        ]
        down = lax.dynamic_slice_in_dim(w_down, device * rows, rows, 0)
        down = jnp.concatenate([down[:, j * ff : (j + 1) * ff] for j in range(parts)], 0)
        return jnp.concatenate(up + [down], 1)

    def kernel(_, *refs):
        out_ref, down_ref = refs[-1], refs[shares]
        if w_out is not None:
            out_ref[part:, :] = refs[shares + 1][...]
        for z in range(shares):
            out_ref[:part, z * rows : (z + 1) * rows] = refs[z][...]
        for j in range(parts):
            out_ref[j * rows : (j + 1) * rows, ff:] = down_ref[:, j * ff : (j + 1) * ff]

    extra = 0 if w_out is None else w_out.shape[0] // 2
    return pl.pallas_call(
        kernel,
        grid_spec=pltpu.PrefetchScalarGridSpec(
            num_scalar_prefetch=1,
            grid=(1,),
            in_specs=[
                pl.BlockSpec((part, rows), lambda i, d, z=z: (0, z * owners + d[0]))
                for z in range(shares)
            ]
            + [pl.BlockSpec((rows, model), lambda i, d: (d[0], 0))]
            + [pl.BlockSpec((extra, model), lambda i, d: (d[1], 0))] * (extra > 0),
            out_specs=pl.BlockSpec((part + extra, 2 * ff), lambda i, d: (0, 0)),
        ),
        out_shape=jax.ShapeDtypeStruct((part + extra, 2 * ff), BF16),
        compiler_params=pltpu.CompilerParams(vmem_limit_bytes=48 * 1024 * 1024),
        cost_estimate=pl.CostEstimate(flops=1, bytes_accessed=1, transcendentals=0),
    )(
        jnp.stack([device, core]).astype(jnp.int32),
        *[w_up] * shares,
        w_down,
        *([] if w_out is None else [w_out]),
    )


def absolute(owner):
    a, b, c = lax.axis_index("a"), lax.axis_index("b"), lax.axis_index("c")
    owner = owner ^ (c * 4 + a * 2 + b)
    return (owner % 4) * 2 + owner // 4


def project(pieces, places, owners, groups, rows, gain, bias, weight, before):
    model, columns = weight.shape
    mine, steps = groups * rows, groups
    count = len(pieces)
    stride = places[1] - places[0] if count == 2 else 1

    def place(t):
        k = t // steps
        if count == 2:
            at = places[0] + stride * k
        else:
            at = k
            for i in range(1, count):
                if places[i] - places[i - 1] > 1:
                    at = at + (k >= i) * (places[i] - places[i - 1] - 1)
        return at * steps + t % steps

    def kernel(*refs):
        piece_refs = refs[:count]
        gain_ref, bias_ref, weight_ref = refs[count : count + 3]
        norm_ref, out_ref, held = refs[-3:]
        t = pl.program_id(0)
        for k in range(count):

            @pl.when(t // steps == k)
            def _(k=k):
                held[...] = piece_refs[k][...]

        values = held[...].astype(F32)
        normed = layer_norm(values, gain_ref[...], bias_ref[...])[0].astype(BF16)
        norm_ref[...] = normed
        out_ref[...] = nn(normed, weight_ref[...]).astype(BF16)

    specs = [
        pl.BlockSpec((rows, model), lambda t, k=k: (jnp.clip(t - k * steps, 0, steps - 1), 0))
        for k in range(count)
    ]
    fixed = lambda shape: pl.BlockSpec(shape, lambda t: (0, 0))
    specs += [fixed((1, model)), fixed((1, model)), fixed((model, columns))]
    extra = () if before is None else before
    return pl.pallas_call(
        kernel,
        grid=(count * steps,),
        in_specs=specs + [pl.BlockSpec(memory_space=pl.ANY)] * len(extra),
        out_specs=[
            pl.BlockSpec((rows, model), lambda t: (place(t), 0)),
            pl.BlockSpec((rows, columns), lambda t: (place(t), 0)),
        ],
        out_shape=[
            jax.ShapeDtypeStruct((owners * mine, model), BF16),
            jax.ShapeDtypeStruct((owners * mine, columns), BF16),
        ],
        scratch_shapes=[pltpu.VMEM((rows, model), BF16)],
        input_output_aliases={count + 3 + i: i for i in range(len(extra))},
        compiler_params=pltpu.CompilerParams(vmem_limit_bytes=48 * 1024 * 1024),
        cost_estimate=pl.CostEstimate(flops=1, bytes_accessed=1, transcendentals=0),
    )(*pieces, gain[None], bias[None], weight, *extra)


def pack(parts, packed, shares):
    model = packed.shape[0]
    part, half = model // shares, model // 2
    low = part // 2
    outer = (parts[0][0].shape[0] - half) // 2
    per = shares // 2
    out_rows = outer // per
    rows = low + out_rows + low
    flat = [each for terms in parts for each in terms]

    def kernel(*refs):
        packed_ref, out_ref = refs[-2], refs[-1]
        it = iter(refs)
        groups = [[next(it) for _ in terms] for terms in parts]

        def total(refs, at, count):
            summed = refs[0][at : at + count, :].astype(F32)
            for ref in refs[1:]:
                summed = summed + ref[at : at + count, :].astype(F32)
            return summed.astype(BF16)

        for z in range(shares):
            terms, side = groups[z // per], z % per
            for j in range(2):
                lanes = slice(j * half, (j + 1) * half)
                out_ref[z, :low, lanes] = total(terms, side * part + j * low, low)
                out_ref[z, low : low + out_rows, lanes] = total(
                    terms, half + j * outer + side * out_rows, out_rows
                )
                at = z * part + j * low
                out_ref[z, low + out_rows :, lanes] = packed_ref[at : at + low, :]

    return pl.pallas_call(
        kernel,
        out_shape=jax.ShapeDtypeStruct((shares, rows, model), BF16),
        compiler_params=pltpu.CompilerParams(vmem_limit_bytes=48 * 1024 * 1024),
    )(*flat, packed)


def unpack_lower(pieces, places, shares):
    owners = len(pieces)
    part, ff = pieces[0].shape
    parts = part * shares // ff
    rows = part // parts

    def kernel(at_ref, *refs):
        for k in range(owners):
            refs[-1][at_ref[k]] = refs[k][...].astype(F32)

    result = pl.pallas_call(
        kernel,
        grid_spec=pltpu.PrefetchScalarGridSpec(
            num_scalar_prefetch=1,
            grid=(parts,),
            in_specs=[pl.BlockSpec((rows, ff), lambda i, _: (i, 0))] * owners,
            out_specs=pl.BlockSpec((owners, rows, ff), lambda i, _: (0, 0, i)),
        ),
        out_shape=jax.ShapeDtypeStruct((owners, rows, parts * ff), F32),
        compiler_params=pltpu.CompilerParams(vmem_limit_bytes=48 * 1024 * 1024),
    )(places, *pieces)
    return result.reshape(owners * rows, parts * ff)


def unpack(pieces, places, shares, part, width):
    owners = len(pieces)
    rows, model = pieces[0].shape
    half, low = model // 2, part // 2
    out_rows = part // owners
    steps = 4
    block = low // steps
    outer_block = 16

    def kernel(at_ref, *refs):
        mains, outers, projs = refs[:owners], refs[owners : 2 * owners], refs[2 * owners : 3 * owners]
        up_ref, outer_ref, proj_ref, *vec_refs, held = refs[3 * owners :]
        i = pl.program_id(0)
        for j in range(2):
            at = j * half + 3 * width
            vectors = [proj[:, at : at + 128].astype(F32) for proj in projs]
            rows = pl.ds(pl.multiple_of(j * low + i * block, block), block)
            held[rows, :] = functools.reduce(jnp.add, vectors)

        @pl.when(i == steps - 1)
        def _():
            vectors = held[...].T
            for k, ref in enumerate(vec_refs):
                ref[...] = vectors[k : k + 1, :]

        for k in range(owners):
            d = at_ref[k]
            lane = lambda base: pl.ds(pl.multiple_of(base + d * width, width), width)
            outer_ref[d] = outers[k][...].astype(F32)
            for j in range(2):
                for z in range(shares):
                    at = j * half + z * width
                    up_ref[j, :, lane(z * owners * width)] = mains[k][:, at : at + width].astype(F32)
                for t in range(3):
                    at = j * half + t * width
                    proj_ref[j, :, lane(t * model)] = projs[k][:, at : at + width].astype(F32)

    outer_at, proj_at = low // outer_block, (low + out_rows) // block
    outer_steps = out_rows // outer_block
    results = pl.pallas_call(
        kernel,
        grid_spec=pltpu.PrefetchScalarGridSpec(
            num_scalar_prefetch=1,
            grid=(steps,),
            in_specs=[pl.BlockSpec((block, model), lambda i, _: (i, 0))] * owners
            + [
                pl.BlockSpec(
                    (outer_block, model), lambda i, _: (outer_at + i * outer_steps // steps, 0)
                )
            ]
            * owners
            + [pl.BlockSpec((block, model), lambda i, _: (proj_at + i, 0))] * owners,
            out_specs=[
                pl.BlockSpec((2, block, shares * model), lambda i, _: (0, i, 0)),
                pl.BlockSpec(
                    (owners, outer_block, model), lambda i, _: (0, i * outer_steps // steps, 0)
                ),
                pl.BlockSpec((2, block, 3 * model), lambda i, _: (0, i, 0)),
            ]
            + [pl.BlockSpec((1, part), lambda i, _: (0, 0))] * 4,
            scratch_shapes=[pltpu.VMEM((part, 128), F32)],
        ),
        out_shape=[
            jax.ShapeDtypeStruct((2, low, shares * model), F32),
            jax.ShapeDtypeStruct((owners, out_rows, model), F32),
            jax.ShapeDtypeStruct((2, low, 3 * model), F32),
        ]
        + [jax.ShapeDtypeStruct((1, part), F32)] * 4,
        compiler_params=pltpu.CompilerParams(vmem_limit_bytes=56 * 1024 * 1024),
    )(places, *pieces, *pieces, *pieces)
    upper, outer, proj, *vectors = results
    return (
        upper.reshape(part, shares * model),
        outer.reshape(part, model),
        proj.reshape(part, 3 * model),
        [each.reshape(part) for each in vectors],
    )


def flip(value, axis):
    return lax.ppermute(value, axis, [(0, 1), (1, 0)])


def after(value, *others):
    return lax.optimization_barrier((value, *others))[0]


def spread_near(value):
    return [value, flip(value, "b"), flip(value, "a")]


def spread_far(near):
    half = near[0].shape[0] // 2
    return [flip(near[2][:half], "b"), flip(near[1][half:], "a")]


def spread(value):
    if lax.axis_size("a") != 2:
        return list(lax.all_gather(value, CTX, axis=0, tiled=False))
    half = value.shape[0] // 2
    from_b, from_a = flip(value, "b"), flip(value, "a")
    far = jnp.concatenate([flip(from_a[:half], "b"), flip(from_b[half:], "a")], 0)
    near = [value, from_b, from_a]
    return near + [far] + [flip(after(each, far), "c") for each in near] + [flip(far, "c")]


def add(u, v):
    return (u.astype(F32) + v.astype(F32)).astype(BF16)


def converge_first(from_b, from_a, far):
    far_0, far_1 = flip(far[0], "b"), flip(far[1], "a")
    b_0, a_1 = flip(from_b[0], "b"), flip(from_a[1], "a")
    return add(from_b[1], far_1), add(from_a[0], far_0), b_0, a_1


def converge_last(own, first):
    b_1, a_0, b_0, a_1 = first
    return (own[0], b_0, flip(a_0, "a")), (own[1], flip(b_1, "b"), a_1)


def total(terms):
    return sum(each.astype(F32) for each in terms[1:]) + terms[0].astype(F32)


def shards(
    tokens,
    out_grad,
    seg_ids,
    positions,
    ln1_gain,
    ln1_bias,
    w_qkv,
    w_out,
    ln2_gain,
    ln2_bias,
    w_up,
    w_down,
):
    groups, rows, model = tokens.shape
    owners, shares = lax.axis_size(CTX), lax.axis_size("z")
    square = lax.axis_size("a") == 2
    width = model // owners
    heads = HEADS // owners
    mine = groups * rows
    part = model // shares
    full_ff = w_up.shape[1]
    ff = full_ff // owners
    ff_rows = ff // shares
    ff_parts = model // ff
    me = lax.axis_index(CTX)
    core = lax.axis_index("c")

    first_seg, first_pos = seg_ids[:, ::UNIT], positions[:, ::UNIT]
    slot = jnp.where(
        first_seg == 0,
        first_pos // UNIT,
        PROMPT // UNIT + (first_seg - 1) * (CONT // UNIT) + first_pos // UNIT,
    )
    per_group = rows // UNIT
    note = jnp.zeros((32, model), BF16).at[0, : groups * per_group].set(
        slot.reshape(-1).astype(BF16)
    )
    sent = jnp.concatenate([tokens.reshape(mine, model), note], 0)
    if square:
        near_pieces = spread_near(sent)
        far_halves = spread_far(near_pieces)
        pieces = [sent] + near_pieces[1:3]
    else:
        pieces = spread(sent)
    places = jnp.arange(owners, dtype=jnp.int32)
    if square:
        places = absolute(places)

    columns = [
        lax.dynamic_slice_in_dim(w_qkv, t * model + me * width, width, 1) for t in range(3)
    ]
    norms = jnp.stack([ln1_gain, ln1_bias, ln2_gain, ln2_bias], 0)
    norms = jnp.pad(norms.reshape(-1, 64), ((0, 0), (0, 3 * width - 64)))
    packed = jnp.concatenate(columns, 1)
    packed = jnp.concatenate([packed, norms], 0)
    packed = lax.all_gather(packed, "z", axis=0, tiled=True)
    chunk = take_chunk(w_up, w_down, me, owners)
    chunk, packed, pieces[1], pieces[2] = lax.optimization_barrier(
        (chunk, packed, pieces[1], pieces[2])
    )
    chunk = lax.all_gather(chunk, "z", axis=0, tiled=True)

    packed = packed.reshape(shares, -1, 3 * width)
    w_heads = packed[:, :part].reshape(model, 3 * width)
    vectors = packed[:, part:, :64].astype(F32).reshape(shares, 4, part)
    vectors = vectors.transpose(1, 0, 2).reshape(4, model)
    gain_one, bias_one, gain_two, bias_two = vectors[0], vectors[1], vectors[2], vectors[3]

    half = w_out.shape[0] // 2
    piece = lax.dynamic_slice_in_dim(w_out, core * half, half, 0)

    def projection(pieces, chosen, before):
        return project(
            pieces, chosen, owners, groups, rows, gain_one, bias_one, w_heads, before
        )

    if square:
        near_pieces += [flip(each, "c") for each in near_pieces]
        projected = projection(near_pieces, [0, 1, 2, 4, 5, 6], None)
        far_halves[0], far_halves[1], *projected = lax.optimization_barrier(
            (*far_halves, *projected)
        )
        far = jnp.concatenate(far_halves, 0)
        pieces = near_pieces[:3] + [far] + near_pieces[3:] + [flip(far, "c")]
        attn_in, qkv = projection([far, pieces[7]], [3, 7], projected)
    else:
        attn_in, qkv = projection(pieces, list(range(owners)), None)
    slots = jnp.concatenate([each[mine, : groups * per_group] for each in pieces])
    slots = slots.astype(jnp.int32)
    qkv = qkv.reshape(owners, groups, rows, 3 * width)
    attended = forward_attention(heads, width, qkv, 0, slots, places, [])
    first_heads = attended[0]
    for g in range(1, groups):
        if square and g == 1:
            near_chunks = spread_near(after(chunk, attended[0]))
            far_chunk = take_chunk(w_up, w_down, places[3], owners, w_out, core)
            far_chunk = lax.all_gather(after(far_chunk, attended[0]), "z", axis=0, tiled=False)
        attended = forward_attention(heads, width, qkv, g, slots, places, attended)
    attn_heads, exact, logs = attended
    if not square:
        whole_out = lax.all_gather(piece, ("z", "c"), axis=0, tiled=True)
    attn_heads = lax.all_to_all(
        attn_heads.reshape(owners, mine, width), CTX, split_axis=0, concat_axis=0, tiled=True
    )
    flat = tokens.reshape(mine, model)
    if square:
        near_chunks = [after(each, attn_heads) for each in near_chunks]
        other_chunks = [flip(each, "c") for each in near_chunks]
    if square:
        far_chunk = after(far_chunk, attn_heads)
        far_other = flip(far_chunk, "c")
        whole_out = (far_chunk, far_other)
    attn_low, residual, *ffn_in, whole_out = attention_output(
        attn_heads, flat, whole_out, core, gain_two, bias_two, rows
    )
    grad_low = out_grad.reshape(mine, model)

    def feed(sums, others, mine):
        out_sum, in_sum, *grads = feed_forward(*ffn_in, grad_low, sums, others, mine, shares)
        chunk_grads.append(grads)
        return out_sum, in_sum

    sums, chunk_grads = None, []
    if square:
        mine_chunks = [[each] for each in near_chunks + [far_chunk]]
        other_chunks = [[each] for each in other_chunks + [far_other]]
        sums = feed(sums, other_chunks, mine_chunks)
    else:
        chunks = [[each] for each in spread(chunk)]
        for k in range(0, owners, 4):
            sums = feed(sums, chunks[k : k + 2], chunks[k + 2 : k + 4])
    output = (residual + sums[0]).astype(BF16)
    grad_resid, grad_branch, grad_heads, norm_grads = norm_gradient(
        residual, sums[1], grad_low, whole_out, gain_two, owners, rows
    )
    grad_gain_two, grad_bias_two = norm_grads[0], norm_grads[1]
    late = [grad_branch] + [each for grads in chunk_grads for each in grads]
    grad_heads, grad_branch, *late = lax.optimization_barrier((grad_heads, *late))
    chunk_grads = [late[:4]] if square else chunk_grads
    grad_heads = lax.all_to_all(
        grad_heads, CTX, split_axis=0, concat_axis=0, tiled=True
    ).reshape(owners, groups, rows, width)
    out_rows = part // owners

    if square:
        outer_away, outer = outer_gradient(attn_low, grad_branch, places, shares)
        halves = join_upper(
            [each[2] for each in chunk_grads],
            [flip(each[0], "c") for each in chunk_grads],
            outer,
            flip(outer_away, "c"),
        )
        lower = join_lower(
            [
                after(each[3], grad_heads, *[half for pair in halves for half in pair])
                for each in chunk_grads
            ],
            [flip(each[1], "c") for each in chunk_grads],
        )
        grad_heads = after(grad_heads, lower)
        lower = lax.psum_scatter(
            lower.reshape(shares * 4, part, ff), "z", scatter_dimension=0, tiled=True
        )
    else:
        lower = jnp.concatenate([low for _, a, _, b in chunk_grads for low in (a, b)], 1)
        lower = lax.psum_scatter(lower, CTX, scatter_dimension=1, tiled=True)
        lower = lower.reshape(shares, part, ff)
        upper = jnp.concatenate([up for a, _, b, _ in chunk_grads for up in (a, b)], 0)
        upper = lax.psum_scatter(upper, CTX, scatter_dimension=0, tiled=True)
        upper = upper.reshape(shares, part, ff)
        outer = tn(attn_low, grad_branch).astype(BF16)
        outer = outer.reshape(shares, owners, out_rows, model).transpose(1, 0, 2, 3)
        outer = lax.psum_scatter(
            outer.reshape(model, model), CTX, scatter_dimension=0, tiled=True
        )
    if square:
        first = converge_first(*halves[1:])
    grad_qkv = backward_attention(heads, width, qkv, grad_heads, exact, logs, slots, places)
    if square:
        columns = jnp.stack([gain_one, bias_one, grad_gain_two, grad_bias_two], 1)
        columns = jnp.pad(columns, ((0, 0), (0, 124)))
        *first, columns, grad_qkv = lax.optimization_barrier((*first, columns, grad_qkv))
        upper_terms = converge_last(halves[0], first)
        grad_qkv = grad_qkv.reshape(owners, mine, 3 * width)
        away = nt(grad_qkv[4:].reshape(4 * mine, 3 * width), w_heads).astype(BF16)
        grad_qkv = after(grad_qkv, away)
        away = flip(away, "c").reshape(4, mine, model)
        pairs = input_parts(grad_qkv[:4], w_heads, away)
        second = converge_first(*pairs[1:])
        terms = converge_last(pairs[0], second)
        grad_attn_in = jnp.concatenate([total(each) for each in terms], 0)
        grad_qkv = after(
            grad_qkv, *[each for group in (*pairs, *upper_terms) for each in group]
        )
        packed_grad = projection_gradient(
            attn_in, grad_qkv.reshape(owners * mine, 3 * width), w_heads, columns
        )
        packed_grad = after(packed_grad, lower, *second[:2])
    else:
        grad_qkv = grad_qkv.reshape(owners * mine, 3 * width)
        away = nt(grad_qkv, w_heads).astype(BF16)
        grad_attn_in = lax.psum_scatter(away, CTX, scatter_dimension=0, tiled=True).astype(F32)
        grad_columns = tn(attn_in, grad_qkv)
        w_wide = w_heads.astype(F32)
        summed = jnp.sum(grad_qkv.astype(F32), 0)
        grad_bias_one = jnp.sum(w_wide * summed, 1)
        grad_gain_one = (jnp.sum(w_wide * grad_columns, 1) - bias_one * grad_bias_one) / gain_one
        vector_grads = jnp.stack([grad_gain_one, grad_bias_one, grad_gain_two, grad_bias_two], 1)
        packed_grad = jnp.concatenate(
            [grad_columns, vector_grads, jnp.zeros((model, 124), F32)], 1
        ).astype(BF16)

    if square:
        lower = after(lower, grad_attn_in)
        lower = lower[0].astype(F32) + sum(
            flip(lower[k], axis).astype(F32) for k, axis in ((1, "b"), (2, "a"))
        ) + lax.ppermute(lower[3], ("a", "b"), [(0, 3), (3, 0), (1, 2), (2, 1)]).astype(F32)
        lower = lower.astype(BF16)
        grad_down = unpack_lower(spread(lower), places, shares)
        everything = pack(upper_terms, packed_grad, shares)
        everything = lax.psum_scatter(
            everything.reshape(-1, model), "z", scatter_dimension=0, tiled=True
        )
        grad_upper, grad_outer, grad_proj, vector_grads = unpack(
            spread(after(everything, lower)), places, shares, part, width
        )
    else:
        span = 2 * ff
        per_part = packed_grad.shape[1] * part // span
        everything = jnp.concatenate(
            [
                jnp.concatenate([upper, lower], 2),
                outer.reshape(shares, -1, span),
                packed_grad.reshape(shares, per_part, span),
            ],
            1,
        )
        everything = lax.psum_scatter(
            everything.reshape(-1, span), "z", scatter_dimension=0, tiled=True
        )
        everything = lax.all_gather(everything, CTX, axis=0, tiled=False)
        grad_upper = (
            everything[:, :part, :ff]
            .reshape(owners, part, shares, ff_rows)
            .transpose(1, 2, 0, 3)
            .reshape(part, full_ff)
            .astype(F32)
        )
        grad_down = (
            everything[:, :part, ff:]
            .reshape(owners, ff_parts, ff_rows, ff)
            .transpose(0, 2, 1, 3)
            .reshape(owners * ff_rows, model)
            .astype(F32)
        )
        at = part + out_rows * model // span
        grad_outer = everything[:, part:at].reshape(part, model).astype(F32)
        packed_grad = everything[:, at:].reshape(owners, part, -1).astype(F32)
        grad_proj = (
            packed_grad[:, :, : 3 * width]
            .reshape(owners, part, 3, width)
            .transpose(1, 2, 0, 3)
            .reshape(part, 3 * model)
        )
        vector_grads = jnp.sum(packed_grad[:, :, 3 * width : 3 * width + 4], 0).T

    attn_full, attn_norm, attn_rstd = layer_norm(flat.astype(F32), gain_one, bias_one)
    in_grad = (grad_resid + norm_back(grad_attn_in, attn_norm, attn_rstd, gain_one)).astype(BF16)

    return (
        output.reshape(tokens.shape),
        in_grad.reshape(tokens.shape),
        vector_grads[0],
        vector_grads[1],
        grad_proj,
        grad_outer,
        vector_grads[2],
        vector_grads[3],
        grad_upper,
        grad_down,
    )


def solution(mesh):
    ctx, wsh = mesh.shape["ctx"], mesh.shape["wsh"]
    fine = Mesh(mesh.devices.reshape(ctx // 4, 2, 2, wsh), ("a", "b", "c", "z"))
    toks = P("z", CTX, None)
    ints = P("z", CTX)
    vec, mat = P("z"), P("z", None)
    in_specs = (toks, toks, ints, ints, vec, vec, mat, mat, vec, vec, mat, mat)
    out_specs = (toks, toks, vec, vec, mat, mat, vec, vec, mat, mat)
    return jax.shard_map(shards, mesh=fine, in_specs=in_specs, out_specs=out_specs, check_vma=False)
```

```python
import functools

import jax
import jax.numpy as jnp
from jax import lax
from jax.experimental import pallas as pl
from jax.experimental.pallas import tpu as pltpu
from jax.sharding import Mesh
from jax.sharding import PartitionSpec as P

HEADS = 16
PROMPT = 1024
CONT = 256
UNIT = 64
TILE = 256
EPSILON = 1e-05
NEG_BIG = -1e30
CTX = ("a", "b", "c")
F32 = jnp.float32
BF16 = jnp.bfloat16


def layer_norm(values, gain, bias):
    average = jnp.mean(values, -1, keepdims=True)
    centred = values - average
    inv_std = lax.rsqrt(jnp.mean(centred * centred, -1, keepdims=True) + EPSILON)
    normed = centred * inv_std
    return (normed * gain + bias, normed, inv_std)


def norm_back(grad_out, normed, inv_std, gain):
    scaled = grad_out * gain
    return inv_std * (
        scaled
        - jnp.mean(scaled, -1, keepdims=True)
        - normed * jnp.mean(scaled * normed, -1, keepdims=True)
    )


def gelu_exact(values):
    return jax.nn.gelu(values, approximate=False)


def nn(left, right):
    return jnp.dot(left, right, preferred_element_type=F32)


def nt(left, right):
    return lax.dot_general(left, right, (((1,), (1,)), ((), ())), preferred_element_type=F32)


def tn(left, right):
    return lax.dot_general(left, right, (((0,), (0,)), ((), ())), preferred_element_type=F32)


def forward_attention(heads, width, qkv, g, slots, places, before):
    owners, groups, rows, _ = qkv.shape
    total = owners * rows
    per_owner = rows // UNIT
    size = width // heads
    scale = size**-0.5

    units = [(k, u) for k in range(owners) for u in range(per_owner)]

    def kernel(slot_ref, at_ref, qkv_ref, *refs):
        out_ref, exact_ref, log_ref, qs, ks, vs, vt, low = refs[-8:]

        def canonical(k, u):
            slot = slot_ref[(k * groups + g) * per_owner + u]
            return pl.ds(pl.multiple_of(slot * UNIT, UNIT), UNIT)

        for k, u in units:
            block = qkv_ref[k, 0, u * UNIT : (u + 1) * UNIT, :]
            here = canonical(k, u)
            qs[here, :] = block[:, :width] * scale
            ks[here, :] = block[:, width : 2 * width]
            vs[here, :] = block[:, 2 * width :]
        vt[...] = vs[...].T
        row = lax.broadcasted_iota(jnp.int32, (TILE, TILE), 0)
        col = lax.broadcasted_iota(jnp.int32, (TILE, TILE), 1)
        causal = row <= col
        for i in range(total // TILE):
            here = slice(i * TILE, (i + 1) * TILE)
            before = min(i * TILE, PROMPT)
            outs = []
            for h in range(heads):
                lanes = slice(h * size, (h + 1) * size)
                query = qs[here, lanes]
                own = jnp.where(causal, nt(ks[here, lanes], query), NEG_BIG)
                high = jnp.max(own, 0, keepdims=True)
                if before:
                    past = nt(ks[:before, lanes], query)
                    high = jnp.maximum(high, jnp.max(past, 0, keepdims=True))
                own = jnp.exp(own - high)
                sums = jnp.sum(own, 0, keepdims=True)
                mixed = nn(vt[lanes, here], own.astype(BF16))
                if before:
                    past = jnp.exp(past - high)
                    sums = sums + jnp.sum(past, 0, keepdims=True)
                    mixed = mixed + nn(vt[lanes, :before], past.astype(BF16))
                log_ref[0, h : h + 1, here] = high + jnp.log(sums)
                outs.append(mixed / sums)
            both = jnp.concatenate(outs, 0) if heads > 1 else outs[0]
            exact_ref[0, :, here] = both
            low[here, :] = both.T.astype(BF16)
        for k, u in units:
            out_ref[at_ref[k], 0, u * UNIT : (u + 1) * UNIT, :] = low[canonical(k, u), :]

    return pl.pallas_call(
        kernel,
        grid_spec=pltpu.PrefetchScalarGridSpec(
            num_scalar_prefetch=2,
            grid=(1,),
            in_specs=[pl.BlockSpec((owners, 1, rows, 3 * width), lambda i, *_: (0, g, 0, 0))]
            + [pl.BlockSpec(memory_space=pl.ANY)] * len(before),
            out_specs=[
                pl.BlockSpec((owners, 1, rows, width), lambda i, *_: (0, g, 0, 0)),
                pl.BlockSpec((1, width, total), lambda i, *_: (g, 0, 0)),
                pl.BlockSpec((1, heads, total), lambda i, *_: (g, 0, 0)),
            ],
            scratch_shapes=[pltpu.VMEM((total, width), BF16)] * 3
            + [pltpu.VMEM((width, total), BF16), pltpu.VMEM((total, width), BF16)],
        ),
        out_shape=[
            jax.ShapeDtypeStruct((owners, groups, rows, width), BF16),
            jax.ShapeDtypeStruct((groups, width, total), F32),
            jax.ShapeDtypeStruct((groups, heads, total), F32),
        ],
        input_output_aliases={3 + i: i for i in range(len(before))},
        compiler_params=pltpu.CompilerParams(vmem_limit_bytes=48 * 1024 * 1024),
        cost_estimate=pl.CostEstimate(flops=1, bytes_accessed=1, transcendentals=0),
    )(slots, places, qkv, *before)


def backward_attention(heads, width, qkv, grad, exact, logs, slots, places):
    owners, groups, rows, _ = qkv.shape
    total = owners * rows
    per_owner = rows // UNIT
    size = width // heads
    scale = size**-0.5
    wide = 4 * TILE
    units = [(k, u) for k in range(owners) for u in range(per_owner)]

    def kernel(slot_ref, at_ref, qkv_ref, grad_ref, exact_ref, log_ref, out_ref, *scratch):
        qs, ks, vs, gs, kt, delta, dqt, dq, dk, dv = scratch
        g = pl.program_id(0)

        def canonical(k, u):
            slot = slot_ref[(k * groups + g) * per_owner + u]
            return pl.ds(pl.multiple_of(slot * UNIT, UNIT), UNIT)

        for k, u in units:
            block = qkv_ref[k, 0, u * UNIT : (u + 1) * UNIT, :]
            here = canonical(k, u)
            qs[here, :] = block[:, :width] * scale
            ks[here, :] = block[:, width : 2 * width]
            vs[here, :] = block[:, 2 * width :]
            gs[here, :] = grad_ref[at_ref[k], 0, u * UNIT : (u + 1) * UNIT, :]
        kt[...] = ks[...].T
        for i in range(total // TILE):
            here = slice(i * TILE, (i + 1) * TILE)
            both = gs[here, :].astype(F32).T * exact_ref[0, :, here]
            for h in range(heads):
                delta[h : h + 1, here] = jnp.sum(
                    both[h * size : (h + 1) * size, :], 0, keepdims=True
                )
        dqt[...] = jnp.zeros_like(dqt)
        for j in range(total // TILE):
            here = slice(j * TILE, (j + 1) * TILE)
            if j * TILE < PROMPT:
                starts = [(j * TILE, TILE)]
                at = (j + 1) * TILE
                if (total - at) % wide:
                    starts.append((at, (total - at) % wide))
                    at += (total - at) % wide
                while at < total:
                    starts.append((at, wide))
                    at += wide
            else:
                starts = [(j * TILE, TILE)]
            for h in range(heads):
                lanes = slice(h * size, (h + 1) * size)
                key, value, key_t = ks[here, lanes], vs[here, lanes], kt[lanes, here]
                grad_key = grad_value = None
                for at, count in starts:
                    there = slice(at, at + count)
                    query, pull = qs[there, lanes], gs[there, lanes]
                    powers = jnp.exp(nt(key, query) - log_ref[0, h : h + 1, there])
                    if at == j * TILE:
                        row = lax.broadcasted_iota(jnp.int32, (TILE, TILE), 0)
                        col = lax.broadcasted_iota(jnp.int32, (TILE, TILE), 1)
                        powers = jnp.where(row <= col, powers, 0.0)
                    slope = powers * (nt(value, pull) - delta[h : h + 1, there])
                    powers, slope = powers.astype(BF16), slope.astype(BF16)
                    more_value, more_key = nn(powers, pull), nn(slope, query)
                    grad_value = more_value if grad_value is None else grad_value + more_value
                    grad_key = more_key if grad_key is None else grad_key + more_key
                    dqt[lanes, there] += nn(key_t, slope)
                dk[here, lanes] = grad_key.astype(BF16)
                dv[here, lanes] = grad_value.astype(BF16)
        for i in range(total // TILE):
            here = slice(i * TILE, (i + 1) * TILE)
            dq[here, :] = (dqt[:, here] * scale).T.astype(BF16)
        for k, u in units:
            here = canonical(k, u)
            for at, ref in enumerate((dq, dk, dv)):
                out_ref[k, 0, u * UNIT : (u + 1) * UNIT, at * width : (at + 1) * width] = ref[
                    here, :
                ]

    by_group = lambda lanes: pl.BlockSpec((owners, 1, rows, lanes), lambda g, *_: (0, g, 0, 0))
    kept = lambda lines: pl.BlockSpec((1, lines, total), lambda g, *_: (g, 0, 0))
    return pl.pallas_call(
        kernel,
        grid_spec=pltpu.PrefetchScalarGridSpec(
            num_scalar_prefetch=2,
            grid=(groups,),
            in_specs=[by_group(3 * width), by_group(width), kept(width), kept(heads)],
            out_specs=by_group(3 * width),
            scratch_shapes=[pltpu.VMEM((total, width), BF16)] * 4
            + [
                pltpu.VMEM((width, total), BF16),
                pltpu.VMEM((heads, total), F32),
                pltpu.VMEM((width, total), F32),
                pltpu.VMEM((total, width), BF16),
                pltpu.VMEM((total, width), BF16),
                pltpu.VMEM((total, width), BF16),
            ],
        ),
        out_shape=jax.ShapeDtypeStruct((owners, groups, rows, 3 * width), BF16),
        compiler_params=pltpu.CompilerParams(vmem_limit_bytes=62 * 1024 * 1024),
        cost_estimate=pl.CostEstimate(
            flops=14 * total * total * width, bytes_accessed=1, transcendentals=0
        ),
    )(slots, places, qkv, grad, exact, logs)


def feed_forward(h2, h2_turned, pull, sums, others, mine, shares):
    tokens, model = h2.shape
    chunks = others + mine
    ff = chunks[0][0].shape[-1] // 2
    parts = model // ff
    part, rows = model // shares, ff // shares
    first = sums is None
    n_other, n_mine, n_all = len(others), len(mine), len(chunks)
    pieces = [piece for chunk in chunks for piece in chunk]
    step = min(ff, TILE)

    def kernel(*refs):
        it = iter(refs)
        h2_ref, h2_t, pull_ref = next(it), next(it), next(it)
        starts = None if first else (next(it), next(it))
        chunk_refs = [[next(it) for _ in chunk] for chunk in chunks]
        out_ref, grad_ref = next(it), next(it)
        targets = (next(it), next(it)), (next(it), next(it))
        held, down_w, sem, sum_sem = next(it), next(it), next(it), next(it)
        t = pl.program_id(0)
        slot = lax.rem(t, 2)

        def fetch(k, into):
            ref = chunk_refs[k][0]
            if len(ref.shape) == 2:
                return [pltpu.make_async_copy(ref, held.at[into], sem.at[into, 0])]
            return [
                pltpu.make_async_copy(
                    ref.at[z, pl.ds(0, part)], held.at[into, pl.ds(z * part, part)], sem.at[into, z]
                )
                for z in range(shares)
            ]

        def fetch_sums():
            return [
                pltpu.make_async_copy(ref, into, sum_sem.at[k])
                for k, (ref, into) in enumerate(zip(starts, (out_ref, grad_ref)))
            ]

        @pl.when(t == 0)
        def _():
            for copy in fetch(0, 0):
                copy.start()
            if first:
                out_ref[...] = jnp.zeros_like(out_ref)
                grad_ref[...] = jnp.zeros_like(grad_ref)
            else:
                for copy in fetch_sums():
                    copy.start()

        for k in range(n_all):

            @pl.when(t == k)
            def _(k=k):
                for copy in fetch(k, k % 2):
                    copy.wait()
                if k + 1 < n_all:
                    for copy in fetch(k + 1, (k + 1) % 2):
                        copy.start()

        for z in range(shares):
            for j in range(parts):
                at = z * part + j * rows
                down_w[z * rows : (z + 1) * rows, j * ff : (j + 1) * ff] = held[
                    slot, at : at + rows, ff:
                ]
        hiddens, slopes = [], []
        for at in range(0, ff, step):
            up = nn(h2_ref[...], held[slot, :, at : at + step])
            cdf = 0.5 * (1.0 + lax.erf(up * (0.5**0.5)))
            slope = cdf + up * (jnp.exp(-0.5 * up * up) * 0.3989422804014327)
            hiddens.append((up * cdf).astype(BF16))
            slopes.append((nt(pull_ref[...], down_w[at : at + step, :]) * slope).astype(BF16))
        hidden = jnp.concatenate(hiddens, 1) if len(hiddens) > 1 else hiddens[0]
        grad_up = jnp.concatenate(slopes, 1) if len(slopes) > 1 else slopes[0]
        if not first:

            @pl.when(t == 0)
            def _():
                for copy in fetch_sums():
                    copy.wait()

        out_ref[...] += nn(hidden, down_w[...])
        grad_ref[...] += nt(grad_up, held[slot, :, :ff])
        grad_upper = nn(h2_t[...], grad_up).astype(BF16)
        grad_lower = tn(hidden, pull_ref[...]).astype(BF16)

        def put(refs):
            refs[0][0] = grad_upper
            for z in range(shares):
                for j in range(parts):
                    refs[1][z, 0, j * rows : (j + 1) * rows, :] = grad_lower[
                        z * rows : (z + 1) * rows, j * ff : (j + 1) * ff
                    ]

        @pl.when(t < n_other)
        def _():
            put(targets[0])

        @pl.when(t >= n_other)
        def _():
            put(targets[1])

    whole = pl.BlockSpec((tokens, model), lambda t: (0, 0))
    early = lambda t: jnp.minimum(t, n_other - 1)
    late = lambda t: jnp.maximum(t - n_other, 0)
    acc = jax.ShapeDtypeStruct((tokens, model), F32)
    out_specs, out_shape = [whole, whole], [acc, acc]
    for count, at in ((n_other, early), (n_mine, late)):
        out_specs += [
            pl.BlockSpec((1, model, ff), lambda t, at=at: (at(t), 0, 0)),
            pl.BlockSpec((shares, 1, part, ff), lambda t, at=at: (0, at(t), 0, 0)),
        ]
        out_shape += [
            jax.ShapeDtypeStruct((count, model, ff), BF16),
            jax.ShapeDtypeStruct((shares, count, part, ff), BF16),
        ]
    return pl.pallas_call(
        kernel,
        grid=(n_all,),
        in_specs=[whole, pl.BlockSpec((model, tokens), lambda t: (0, 0)), whole]
        + [pl.BlockSpec(memory_space=pl.ANY)] * (len(pieces) + (0 if first else 2)),
        out_specs=out_specs,
        out_shape=out_shape,
        scratch_shapes=[
            pltpu.VMEM((2, model, 2 * ff), BF16),
            pltpu.VMEM((ff, model), BF16),
            pltpu.SemaphoreType.DMA((2, shares)),
            pltpu.SemaphoreType.DMA((2,)),
        ],
        compiler_params=pltpu.CompilerParams(vmem_limit_bytes=62 * 1024 * 1024),
        cost_estimate=pl.CostEstimate(flops=1, bytes_accessed=1, transcendentals=0),
    )(h2, h2_turned, pull, *(() if first else sums), *pieces)


def attention_output(heads, stream, weight, core, gain, bias, rows):
    owners, tokens, width = heads.shape
    model = owners * width
    split = isinstance(weight, tuple)
    weights = list(weight) if split else [weight]
    if split:
        shares, lines, _ = weight[0].shape
        half = model // shares // 2
        weight_specs = [
            pl.BlockSpec((shares, half, model), lambda i, _: (0, (lines - half) // half, 0))
        ] * 2
    else:
        weight_specs = [pl.BlockSpec((model, model), lambda i, _: (0, 0))]

    def kernel(core_ref, heads_ref, stream_ref, *refs):
        weight_refs, (gain_ref, bias_ref) = refs[: len(weights)], refs[len(weights) : -5]
        low_ref, sum_ref, norm_ref, turned_ref, whole_ref = refs[-5:]

        @pl.when(pl.program_id(0) == 0)
        def _():
            if split:
                for k, ref in enumerate(weight_refs):
                    side = core_ref[0] if k == 0 else 1 - core_ref[0]
                    for z in range(shares):
                        at = pl.multiple_of((2 * z + side) * half, half)
                        whole_ref[pl.ds(at, half), :] = ref[z]
            else:
                whole_ref[...] = weight_refs[0][...]

        for d in range(owners):
            low_ref[:, d * width : (d + 1) * width] = heads_ref[d]
        total = stream_ref[...].astype(F32) + nn(low_ref[...], whole_ref[...])
        sum_ref[...] = total
        normed = layer_norm(total, gain_ref[...], bias_ref[...])[0].astype(BF16)
        norm_ref[...] = normed
        turned_ref[...] = normed.T

    fixed = lambda *shape: pl.BlockSpec(shape, lambda i, _: (0, 0))
    block = pl.BlockSpec((rows, model), lambda i, _: (i, 0))
    return pl.pallas_call(
        kernel,
        grid_spec=pltpu.PrefetchScalarGridSpec(
            num_scalar_prefetch=1,
            grid=(tokens // rows,),
            in_specs=[pl.BlockSpec((owners, rows, width), lambda i, _: (0, i, 0)), block]
            + weight_specs
            + [fixed(1, model), fixed(1, model)],
            out_specs=[block] * 3
            + [pl.BlockSpec((model, rows), lambda i, _: (0, i)), fixed(model, model)],
        ),
        out_shape=[jax.ShapeDtypeStruct((tokens, model), kind) for kind in (BF16, F32, BF16)]
        + [jax.ShapeDtypeStruct((model, tokens), BF16), jax.ShapeDtypeStruct((model, model), BF16)],
        compiler_params=pltpu.CompilerParams(vmem_limit_bytes=62 * 1024 * 1024),
        cost_estimate=pl.CostEstimate(flops=1, bytes_accessed=1, transcendentals=0),
    )(core.reshape(1).astype(jnp.int32), heads, stream, *weights, gain[None], bias[None])


def norm_gradient(total, grad, direct, weight, gain, owners, rows):
    tokens, model = total.shape
    width = model // owners

    def kernel(total_ref, grad_ref, direct_ref, weight_ref, gain_ref, resid_ref, low_ref, heads_ref, vec_ref):
        i = pl.program_id(0)
        values = total_ref[...]
        centred = values - jnp.mean(values, -1, keepdims=True)
        inv_std = lax.rsqrt(jnp.mean(centred * centred, -1, keepdims=True) + EPSILON)
        normed = centred * inv_std
        grads = grad_ref[...]
        result = direct_ref[...].astype(F32) + norm_back(grads, normed, inv_std, gain_ref[...])
        resid_ref[...] = result
        low = result.astype(BF16)
        low_ref[...] = low
        back = nt(low, weight_ref[...]).astype(BF16)
        for d in range(owners):
            heads_ref[d] = back[:, d * width : (d + 1) * width]
        for_gain = jnp.sum(grads * normed, 0, keepdims=True)
        for_bias = jnp.sum(grads, 0, keepdims=True)

        @pl.when(i == 0)
        def _():
            vec_ref[...] = jnp.zeros_like(vec_ref)

        vec_ref[0:1, :] += for_gain
        vec_ref[1:2, :] += for_bias

    fixed = lambda *shape: pl.BlockSpec(shape, lambda i: (0, 0))
    block = pl.BlockSpec((rows, model), lambda i: (i, 0))
    return pl.pallas_call(
        kernel,
        grid=(tokens // rows,),
        in_specs=[block, block, block, fixed(model, model), fixed(1, model)],
        out_specs=[
            block,
            block,
            pl.BlockSpec((owners, rows, width), lambda i: (0, i, 0)),
            fixed(8, model),
        ],
        out_shape=[
            jax.ShapeDtypeStruct((tokens, model), F32),
            jax.ShapeDtypeStruct((tokens, model), BF16),
            jax.ShapeDtypeStruct((owners, tokens, width), BF16),
            jax.ShapeDtypeStruct((8, model), F32),
        ],
        compiler_params=pltpu.CompilerParams(vmem_limit_bytes=48 * 1024 * 1024),
        cost_estimate=pl.CostEstimate(flops=1, bytes_accessed=1, transcendentals=0),
    )(total, grad, direct, weight, gain[None])


def input_parts(slopes, weight, away):
    count, tokens, columns = slopes.shape
    model = weight.shape[0]
    half = tokens // 2

    def kernel(slope_ref, weight_ref, away_ref, *outs):
        t = pl.program_id(0)
        for h in range(2):
            rows = slice(h * half, (h + 1) * half)
            part = nt(slope_ref[0, rows, :], weight_ref[...]) + away_ref[0, rows, :].astype(F32)
            for k in range(count):

                @pl.when(t == k)
                def _(k=k, h=h, part=part):
                    outs[2 * k + h][...] = part.astype(BF16)

    out = pl.pallas_call(
        kernel,
        grid=(count,),
        in_specs=[
            pl.BlockSpec((1, tokens, columns), lambda t: (t, 0, 0)),
            pl.BlockSpec((model, columns), lambda t: (0, 0)),
            pl.BlockSpec((1, tokens, model), lambda t: (t, 0, 0)),
        ],
        out_specs=[pl.BlockSpec((half, model), lambda t: (0, 0))] * (2 * count),
        out_shape=[jax.ShapeDtypeStruct((half, model), BF16)] * (2 * count),
        compiler_params=pltpu.CompilerParams(vmem_limit_bytes=48 * 1024 * 1024),
        cost_estimate=pl.CostEstimate(flops=1, bytes_accessed=1, transcendentals=0),
    )(slopes, weight, away)
    return [(out[2 * k], out[2 * k + 1]) for k in range(count)]


def projection_gradient(normed, slopes, weight, columns):
    count, width = slopes.shape
    model = normed.shape[1]
    block = min(2048, count)
    steps = count // block

    def kernel(normed_ref, slope_ref, weight_ref, columns_ref, out_ref, acc, sums):
        t = pl.program_id(0)
        grad = tn(slope_ref[...], normed_ref[...])
        summed = jnp.sum(slope_ref[...].astype(F32), 0, keepdims=True)

        @pl.when(t == 0)
        def _():
            acc[...] = grad
            sums[...] = summed

        @pl.when(t > 0)
        def _():
            acc[...] += grad
            sums[...] += summed

        @pl.when(t == steps - 1)
        def _():
            whole = acc[...].T
            wide = weight_ref[...].astype(F32)
            given = columns_ref[...]
            bias = jnp.sum(wide * sums[...], 1, keepdims=True)
            gain = jnp.sum(wide * whole, 1, keepdims=True)
            gain = (gain - given[:, 1:2] * bias) / given[:, 0:1]
            lane = lax.broadcasted_iota(jnp.int32, given.shape, 1)
            vectors = jnp.where(lane == 0, gain, jnp.where(lane == 1, bias, given))
            out_ref[:, :width] = whole.astype(BF16)
            out_ref[:, width:] = vectors.astype(BF16)

    return pl.pallas_call(
        kernel,
        grid=(steps,),
        in_specs=[
            pl.BlockSpec((block, model), lambda t: (t, 0)),
            pl.BlockSpec((block, width), lambda t: (t, 0)),
            pl.BlockSpec((model, width), lambda t: (0, 0)),
            pl.BlockSpec((model, 128), lambda t: (0, 0)),
        ],
        out_specs=pl.BlockSpec((model, width + 128), lambda t: (0, 0)),
        out_shape=jax.ShapeDtypeStruct((model, width + 128), BF16),
        scratch_shapes=[pltpu.VMEM((width, model), F32), pltpu.VMEM((1, width), F32)],
        compiler_params=pltpu.CompilerParams(vmem_limit_bytes=48 * 1024 * 1024),
        cost_estimate=pl.CostEstimate(flops=1, bytes_accessed=1, transcendentals=0),
    )(normed, slopes, weight, columns)


def join_lower(mine, away):
    shares, _, part, ff = mine[0].shape
    counts = [each.shape[1] for each in mine]
    n = len(mine)

    def kernel(*refs):
        at = 0
        for k, count in enumerate(counts):
            refs[-1][0, at : at + count] = add(refs[k][0], refs[n + k][0])
            at += count

    spec = lambda count: pl.BlockSpec((1, count, part, ff), lambda z: (z, 0, 0, 0))
    return pl.pallas_call(
        kernel,
        grid=(shares,),
        in_specs=[spec(count) for count in counts] * 2,
        out_specs=spec(sum(counts)),
        out_shape=jax.ShapeDtypeStruct((shares, sum(counts), part, ff), BF16),
        compiler_params=pltpu.CompilerParams(vmem_limit_bytes=48 * 1024 * 1024),
        cost_estimate=pl.CostEstimate(flops=1, bytes_accessed=6 * shares * part * ff * sum(counts), transcendentals=0),
    )(*mine, *away)


def join_upper(mine, away, outer, outer_away):
    _, model, ff = mine[0].shape
    counts = [each.shape[0] for each in mine]
    n, half, extra = len(mine), model // 2, outer.shape[2]

    def kernel(*refs):
        ins, outs = refs[: 2 * n + 2], refs[2 * n + 2 :]
        k = 0
        for i, count in enumerate(counts):
            for j in range(count):
                for h in range(2):
                    rows = slice(h * half, (h + 1) * half)
                    outs[2 * k + h][:half, :] = add(ins[i][j, rows, :], ins[n + i][j, rows, :])
                    outs[2 * k + h][half:, :] = add(ins[2 * n][k, h], ins[2 * n + 1][k, h])
                k += 1

    out = pl.pallas_call(
        kernel,
        out_shape=[jax.ShapeDtypeStruct((half + extra, ff), BF16)] * (2 * sum(counts)),
        compiler_params=pltpu.CompilerParams(vmem_limit_bytes=48 * 1024 * 1024),
        cost_estimate=pl.CostEstimate(flops=1, bytes_accessed=6 * model * ff * sum(counts), transcendentals=0),
    )(*mine, *away, outer, outer_away)
    return [[out[2 * k], out[2 * k + 1]] for k in range(sum(counts))]


def outer_gradient(left, right, places, shares):
    tokens, model = left.shape
    owners = places.shape[0]
    part = model // shares
    rows, half = part // owners, model // 2
    per = shares // 2

    def kernel(at_ref, left_ref, right_ref, away_ref, mine_ref, held):
        for z in range(shares):
            held[...] = tn(left_ref[:, z * part : (z + 1) * part], right_ref[...])
            h, at = z // per, z % per * rows
            for k in range(owners):
                ref = mine_ref if k < owners // 2 else away_ref
                block = held[pl.ds(pl.multiple_of(at_ref[k] * rows, rows), rows), :].astype(BF16)
                for j in range(2):
                    lanes = slice(j * half, (j + 1) * half)
                    ref[k % (owners // 2), h, j * per * rows + at : j * per * rows + at + rows, :] = (
                        block[:, lanes]
                    )

    shape = (owners // 2, 2, 2 * per * rows, half)
    whole = lambda *dims: pl.BlockSpec(dims, lambda i, _: (0,) * len(dims))
    return pl.pallas_call(
        kernel,
        grid_spec=pltpu.PrefetchScalarGridSpec(
            num_scalar_prefetch=1,
            grid=(1,),
            in_specs=[whole(tokens, model)] * 2,
            out_specs=[whole(*shape)] * 2,
            scratch_shapes=[pltpu.VMEM((part, model), F32)],
        ),
        out_shape=[jax.ShapeDtypeStruct(shape, BF16)] * 2,
        compiler_params=pltpu.CompilerParams(vmem_limit_bytes=48 * 1024 * 1024),
        cost_estimate=pl.CostEstimate(flops=1, bytes_accessed=8 * model * model, transcendentals=0),
    )(places, left, right)


def take_chunk(w_up, w_down, device, owners, w_out=None, core=0):
    part, full = w_up.shape
    model = w_down.shape[1]
    ff = full // owners
    shares = model // part
    rows = ff // shares
    parts = model // ff
    if rows % 128:
        up = [
            lax.dynamic_slice_in_dim(w_up, (z * owners + device) * rows, rows, 1)
            for z in range(shares)
        ]
        down = lax.dynamic_slice_in_dim(w_down, device * rows, rows, 0)
        down = jnp.concatenate([down[:, j * ff : (j + 1) * ff] for j in range(parts)], 0)
        return jnp.concatenate(up + [down], 1)

    def kernel(_, *refs):
        out_ref, down_ref = refs[-1], refs[shares]
        if w_out is not None:
            out_ref[part:, :] = refs[shares + 1][...]
        for z in range(shares):
            out_ref[:part, z * rows : (z + 1) * rows] = refs[z][...]
        for j in range(parts):
            out_ref[j * rows : (j + 1) * rows, ff:] = down_ref[:, j * ff : (j + 1) * ff]

    extra = 0 if w_out is None else w_out.shape[0] // 2
    return pl.pallas_call(
        kernel,
        grid_spec=pltpu.PrefetchScalarGridSpec(
            num_scalar_prefetch=1,
            grid=(1,),
            in_specs=[
                pl.BlockSpec((part, rows), lambda i, d, z=z: (0, z * owners + d[0]))
                for z in range(shares)
            ]
            + [pl.BlockSpec((rows, model), lambda i, d: (d[0], 0))]
            + [pl.BlockSpec((extra, model), lambda i, d: (d[1], 0))] * (extra > 0),
            out_specs=pl.BlockSpec((part + extra, 2 * ff), lambda i, d: (0, 0)),
        ),
        out_shape=jax.ShapeDtypeStruct((part + extra, 2 * ff), BF16),
        compiler_params=pltpu.CompilerParams(vmem_limit_bytes=48 * 1024 * 1024),
        cost_estimate=pl.CostEstimate(flops=1, bytes_accessed=1, transcendentals=0),
    )(
        jnp.stack([device, core]).astype(jnp.int32),
        *[w_up] * shares,
        w_down,
        *([] if w_out is None else [w_out]),
    )


def absolute(owner):
    a, b, c = lax.axis_index("a"), lax.axis_index("b"), lax.axis_index("c")
    owner = owner ^ (c * 4 + a * 2 + b)
    return (owner % 4) * 2 + owner // 4


def project(pieces, places, owners, groups, rows, gain, bias, weight, before):
    model, columns = weight.shape
    mine, steps = groups * rows, groups
    count = len(pieces)
    stride = places[1] - places[0] if count == 2 else 1

    def place(t):
        k = t // steps
        if count == 2:
            at = places[0] + stride * k
        else:
            at = k
            for i in range(1, count):
                if places[i] - places[i - 1] > 1:
                    at = at + (k >= i) * (places[i] - places[i - 1] - 1)
        return at * steps + t % steps

    def kernel(*refs):
        piece_refs = refs[:count]
        gain_ref, bias_ref, weight_ref = refs[count : count + 3]
        norm_ref, out_ref, held = refs[-3:]
        t = pl.program_id(0)
        for k in range(count):

            @pl.when(t // steps == k)
            def _(k=k):
                held[...] = piece_refs[k][...]

        values = held[...].astype(F32)
        normed = layer_norm(values, gain_ref[...], bias_ref[...])[0].astype(BF16)
        norm_ref[...] = normed
        out_ref[...] = nn(normed, weight_ref[...]).astype(BF16)

    specs = [
        pl.BlockSpec((rows, model), lambda t, k=k: (jnp.clip(t - k * steps, 0, steps - 1), 0))
        for k in range(count)
    ]
    fixed = lambda shape: pl.BlockSpec(shape, lambda t: (0, 0))
    specs += [fixed((1, model)), fixed((1, model)), fixed((model, columns))]
    extra = () if before is None else before
    return pl.pallas_call(
        kernel,
        grid=(count * steps,),
        in_specs=specs + [pl.BlockSpec(memory_space=pl.ANY)] * len(extra),
        out_specs=[
            pl.BlockSpec((rows, model), lambda t: (place(t), 0)),
            pl.BlockSpec((rows, columns), lambda t: (place(t), 0)),
        ],
        out_shape=[
            jax.ShapeDtypeStruct((owners * mine, model), BF16),
            jax.ShapeDtypeStruct((owners * mine, columns), BF16),
        ],
        scratch_shapes=[pltpu.VMEM((rows, model), BF16)],
        input_output_aliases={count + 3 + i: i for i in range(len(extra))},
        compiler_params=pltpu.CompilerParams(vmem_limit_bytes=48 * 1024 * 1024),
        cost_estimate=pl.CostEstimate(flops=1, bytes_accessed=1, transcendentals=0),
    )(*pieces, gain[None], bias[None], weight, *extra)


def pack(parts, packed, shares):
    model = packed.shape[0]
    part, half = model // shares, model // 2
    low = part // 2
    outer = (parts[0][0].shape[0] - half) // 2
    per = shares // 2
    out_rows = outer // per
    rows = low + out_rows + low
    flat = [each for terms in parts for each in terms]

    def kernel(*refs):
        packed_ref, out_ref = refs[-2], refs[-1]
        it = iter(refs)
        groups = [[next(it) for _ in terms] for terms in parts]

        def total(refs, at, count):
            summed = refs[0][at : at + count, :].astype(F32)
            for ref in refs[1:]:
                summed = summed + ref[at : at + count, :].astype(F32)
            return summed.astype(BF16)

        for z in range(shares):
            terms, side = groups[z // per], z % per
            for j in range(2):
                lanes = slice(j * half, (j + 1) * half)
                out_ref[z, :low, lanes] = total(terms, side * part + j * low, low)
                out_ref[z, low : low + out_rows, lanes] = total(
                    terms, half + j * outer + side * out_rows, out_rows
                )
                at = z * part + j * low
                out_ref[z, low + out_rows :, lanes] = packed_ref[at : at + low, :]

    return pl.pallas_call(
        kernel,
        out_shape=jax.ShapeDtypeStruct((shares, rows, model), BF16),
        compiler_params=pltpu.CompilerParams(vmem_limit_bytes=48 * 1024 * 1024),
    )(*flat, packed)


def unpack_lower(pieces, places, shares):
    owners = len(pieces)
    part, ff = pieces[0].shape
    parts = part * shares // ff
    rows = part // parts

    def kernel(at_ref, *refs):
        for k in range(owners):
            refs[-1][at_ref[k]] = refs[k][...].astype(F32)

    result = pl.pallas_call(
        kernel,
        grid_spec=pltpu.PrefetchScalarGridSpec(
            num_scalar_prefetch=1,
            grid=(parts,),
            in_specs=[pl.BlockSpec((rows, ff), lambda i, _: (i, 0))] * owners,
            out_specs=pl.BlockSpec((owners, rows, ff), lambda i, _: (0, 0, i)),
        ),
        out_shape=jax.ShapeDtypeStruct((owners, rows, parts * ff), F32),
        compiler_params=pltpu.CompilerParams(vmem_limit_bytes=48 * 1024 * 1024),
    )(places, *pieces)
    return result.reshape(owners * rows, parts * ff)


def unpack(pieces, places, shares, part, width):
    owners = len(pieces)
    rows, model = pieces[0].shape
    half, low = model // 2, part // 2
    out_rows = part // owners
    steps = 4
    block = low // steps
    outer_block = 16

    def kernel(at_ref, *refs):
        mains, outers, projs = refs[:owners], refs[owners : 2 * owners], refs[2 * owners : 3 * owners]
        up_ref, outer_ref, proj_ref, *vec_refs, held = refs[3 * owners :]
        i = pl.program_id(0)
        for j in range(2):
            at = j * half + 3 * width
            vectors = [proj[:, at : at + 128].astype(F32) for proj in projs]
            rows = pl.ds(pl.multiple_of(j * low + i * block, block), block)
            held[rows, :] = functools.reduce(jnp.add, vectors)

        @pl.when(i == steps - 1)
        def _():
            vectors = held[...].T
            for k, ref in enumerate(vec_refs):
                ref[...] = vectors[k : k + 1, :]

        for k in range(owners):
            d = at_ref[k]
            lane = lambda base: pl.ds(pl.multiple_of(base + d * width, width), width)
            outer_ref[d] = outers[k][...].astype(F32)
            for j in range(2):
                for z in range(shares):
                    at = j * half + z * width
                    up_ref[j, :, lane(z * owners * width)] = mains[k][:, at : at + width].astype(F32)
                for t in range(3):
                    at = j * half + t * width
                    proj_ref[j, :, lane(t * model)] = projs[k][:, at : at + width].astype(F32)

    outer_at, proj_at = low // outer_block, (low + out_rows) // block
    outer_steps = out_rows // outer_block
    results = pl.pallas_call(
        kernel,
        grid_spec=pltpu.PrefetchScalarGridSpec(
            num_scalar_prefetch=1,
            grid=(steps,),
            in_specs=[pl.BlockSpec((block, model), lambda i, _: (i, 0))] * owners
            + [
                pl.BlockSpec(
                    (outer_block, model), lambda i, _: (outer_at + i * outer_steps // steps, 0)
                )
            ]
            * owners
            + [pl.BlockSpec((block, model), lambda i, _: (proj_at + i, 0))] * owners,
            out_specs=[
                pl.BlockSpec((2, block, shares * model), lambda i, _: (0, i, 0)),
                pl.BlockSpec(
                    (owners, outer_block, model), lambda i, _: (0, i * outer_steps // steps, 0)
                ),
                pl.BlockSpec((2, block, 3 * model), lambda i, _: (0, i, 0)),
            ]
            + [pl.BlockSpec((1, part), lambda i, _: (0, 0))] * 4,
            scratch_shapes=[pltpu.VMEM((part, 128), F32)],
        ),
        out_shape=[
            jax.ShapeDtypeStruct((2, low, shares * model), F32),
            jax.ShapeDtypeStruct((owners, out_rows, model), F32),
            jax.ShapeDtypeStruct((2, low, 3 * model), F32),
        ]
        + [jax.ShapeDtypeStruct((1, part), F32)] * 4,
        compiler_params=pltpu.CompilerParams(vmem_limit_bytes=56 * 1024 * 1024),
    )(places, *pieces, *pieces, *pieces)
    upper, outer, proj, *vectors = results
    return (
        upper.reshape(part, shares * model),
        outer.reshape(part, model),
        proj.reshape(part, 3 * model),
        [each.reshape(part) for each in vectors],
    )


def flip(value, axis):
    return lax.ppermute(value, axis, [(0, 1), (1, 0)])


def after(value, *others):
    return lax.optimization_barrier((value, *others))[0]


def spread_near(value):
    return [value, flip(value, "b"), flip(value, "a")]


def spread_far(near):
    half = near[0].shape[0] // 2
    return [flip(near[2][:half], "b"), flip(near[1][half:], "a")]


def spread(value):
    if lax.axis_size("a") != 2:
        return list(lax.all_gather(value, CTX, axis=0, tiled=False))
    half = value.shape[0] // 2
    from_b, from_a = flip(value, "b"), flip(value, "a")
    far = jnp.concatenate([flip(from_a[:half], "b"), flip(from_b[half:], "a")], 0)
    near = [value, from_b, from_a]
    return near + [far] + [flip(after(each, far), "c") for each in near] + [flip(far, "c")]


def add(u, v):
    return (u.astype(F32) + v.astype(F32)).astype(BF16)


def converge_first(from_b, from_a, far):
    far_0, far_1 = flip(far[0], "b"), flip(far[1], "a")
    b_0, a_1 = flip(from_b[0], "b"), flip(from_a[1], "a")
    return add(from_b[1], far_1), add(from_a[0], far_0), b_0, a_1


def converge_last(own, first):
    b_1, a_0, b_0, a_1 = first
    return (own[0], b_0, flip(a_0, "a")), (own[1], flip(b_1, "b"), a_1)


def total(terms):
    return sum(each.astype(F32) for each in terms[1:]) + terms[0].astype(F32)


def shards(
    tokens,
    out_grad,
    seg_ids,
    positions,
    ln1_gain,
    ln1_bias,
    w_qkv,
    w_out,
    ln2_gain,
    ln2_bias,
    w_up,
    w_down,
):
    groups, rows, model = tokens.shape
    owners, shares = lax.axis_size(CTX), lax.axis_size("z")
    square = lax.axis_size("a") == 2
    width = model // owners
    heads = HEADS // owners
    mine = groups * rows
    part = model // shares
    full_ff = w_up.shape[1]
    ff = full_ff // owners
    ff_rows = ff // shares
    ff_parts = model // ff
    me = lax.axis_index(CTX)
    core = lax.axis_index("c")

    first_seg, first_pos = seg_ids[:, ::UNIT], positions[:, ::UNIT]
    slot = jnp.where(
        first_seg == 0,
        first_pos // UNIT,
        PROMPT // UNIT + (first_seg - 1) * (CONT // UNIT) + first_pos // UNIT,
    )
    per_group = rows // UNIT
    note = jnp.zeros((32, model), BF16).at[0, : groups * per_group].set(
        slot.reshape(-1).astype(BF16)
    )
    sent = jnp.concatenate([tokens.reshape(mine, model), note], 0)
    if square:
        near_pieces = spread_near(sent)
        far_halves = spread_far(near_pieces)
        pieces = [sent] + near_pieces[1:3]
    else:
        pieces = spread(sent)
    places = jnp.arange(owners, dtype=jnp.int32)
    if square:
        places = absolute(places)

    columns = [
        lax.dynamic_slice_in_dim(w_qkv, t * model + me * width, width, 1) for t in range(3)
    ]
    norms = jnp.stack([ln1_gain, ln1_bias, ln2_gain, ln2_bias], 0)
    norms = jnp.pad(norms.reshape(-1, 64), ((0, 0), (0, 3 * width - 64)))
    packed = jnp.concatenate(columns, 1)
    packed = jnp.concatenate([packed, norms], 0)
    packed = lax.all_gather(packed, "z", axis=0, tiled=True)
    chunk = take_chunk(w_up, w_down, me, owners)
    chunk, packed, pieces[1], pieces[2] = lax.optimization_barrier(
        (chunk, packed, pieces[1], pieces[2])
    )
    chunk = lax.all_gather(chunk, "z", axis=0, tiled=True)

    packed = packed.reshape(shares, -1, 3 * width)
    w_heads = packed[:, :part].reshape(model, 3 * width)
    vectors = packed[:, part:, :64].astype(F32).reshape(shares, 4, part)
    vectors = vectors.transpose(1, 0, 2).reshape(4, model)
    gain_one, bias_one, gain_two, bias_two = vectors[0], vectors[1], vectors[2], vectors[3]

    half = w_out.shape[0] // 2
    piece = lax.dynamic_slice_in_dim(w_out, core * half, half, 0)

    def projection(pieces, chosen, before):
        return project(
            pieces, chosen, owners, groups, rows, gain_one, bias_one, w_heads, before
        )

    if square:
        near_pieces += [flip(each, "c") for each in near_pieces]
        projected = projection(near_pieces, [0, 1, 2, 4, 5, 6], None)
        far_halves[0], far_halves[1], *projected = lax.optimization_barrier(
            (*far_halves, *projected)
        )
        far = jnp.concatenate(far_halves, 0)
        pieces = near_pieces[:3] + [far] + near_pieces[3:] + [flip(far, "c")]
        attn_in, qkv = projection([far, pieces[7]], [3, 7], projected)
    else:
        attn_in, qkv = projection(pieces, list(range(owners)), None)
    slots = jnp.concatenate([each[mine, : groups * per_group] for each in pieces])
    slots = slots.astype(jnp.int32)
    qkv = qkv.reshape(owners, groups, rows, 3 * width)
    attended = forward_attention(heads, width, qkv, 0, slots, places, [])
    first_heads = attended[0]
    for g in range(1, groups):
        if square and g == 1:
            near_chunks = spread_near(after(chunk, attended[0]))
            far_chunk = take_chunk(w_up, w_down, places[3], owners, w_out, core)
            far_chunk = lax.all_gather(after(far_chunk, attended[0]), "z", axis=0, tiled=False)
        attended = forward_attention(heads, width, qkv, g, slots, places, attended)
    attn_heads, exact, logs = attended
    if not square:
        whole_out = lax.all_gather(piece, ("z", "c"), axis=0, tiled=True)
    attn_heads = lax.all_to_all(
        attn_heads.reshape(owners, mine, width), CTX, split_axis=0, concat_axis=0, tiled=True
    )
    flat = tokens.reshape(mine, model)
    if square:
        near_chunks = [after(each, attn_heads) for each in near_chunks]
        other_chunks = [flip(each, "c") for each in near_chunks]
    if square:
        far_chunk = after(far_chunk, attn_heads)
        far_other = flip(far_chunk, "c")
        whole_out = (far_chunk, far_other)
    attn_low, residual, *ffn_in, whole_out = attention_output(
        attn_heads, flat, whole_out, core, gain_two, bias_two, rows
    )
    grad_low = out_grad.reshape(mine, model)

    def feed(sums, others, mine):
        out_sum, in_sum, *grads = feed_forward(*ffn_in, grad_low, sums, others, mine, shares)
        chunk_grads.append(grads)
        return out_sum, in_sum

    sums, chunk_grads = None, []
    if square:
        mine_chunks = [[each] for each in near_chunks + [far_chunk]]
        other_chunks = [[each] for each in other_chunks + [far_other]]
        sums = feed(sums, other_chunks, mine_chunks)
    else:
        chunks = [[each] for each in spread(chunk)]
        for k in range(0, owners, 4):
            sums = feed(sums, chunks[k : k + 2], chunks[k + 2 : k + 4])
    output = (residual + sums[0]).astype(BF16)
    grad_resid, grad_branch, grad_heads, norm_grads = norm_gradient(
        residual, sums[1], grad_low, whole_out, gain_two, owners, rows
    )
    grad_gain_two, grad_bias_two = norm_grads[0], norm_grads[1]
    late = [grad_branch] + [each for grads in chunk_grads for each in grads]
    grad_heads, grad_branch, *late = lax.optimization_barrier((grad_heads, *late))
    chunk_grads = [late[:4]] if square else chunk_grads
    grad_heads = lax.all_to_all(
        grad_heads, CTX, split_axis=0, concat_axis=0, tiled=True
    ).reshape(owners, groups, rows, width)
    out_rows = part // owners

    if square:
        outer_away, outer = outer_gradient(attn_low, grad_branch, places, shares)
        halves = join_upper(
            [each[2] for each in chunk_grads],
            [flip(each[0], "c") for each in chunk_grads],
            outer,
            flip(outer_away, "c"),
        )
        lower = join_lower(
            [
                after(each[3], grad_heads, *[half for pair in halves for half in pair])
                for each in chunk_grads
            ],
            [flip(each[1], "c") for each in chunk_grads],
        )
        grad_heads = after(grad_heads, lower)
        lower = lax.psum_scatter(
            lower.reshape(shares * 4, part, ff), "z", scatter_dimension=0, tiled=True
        )
    else:
        lower = jnp.concatenate([low for _, a, _, b in chunk_grads for low in (a, b)], 1)
        lower = lax.psum_scatter(lower, CTX, scatter_dimension=1, tiled=True)
        lower = lower.reshape(shares, part, ff)
        upper = jnp.concatenate([up for a, _, b, _ in chunk_grads for up in (a, b)], 0)
        upper = lax.psum_scatter(upper, CTX, scatter_dimension=0, tiled=True)
        upper = upper.reshape(shares, part, ff)
        outer = tn(attn_low, grad_branch).astype(BF16)
        outer = outer.reshape(shares, owners, out_rows, model).transpose(1, 0, 2, 3)
        outer = lax.psum_scatter(
            outer.reshape(model, model), CTX, scatter_dimension=0, tiled=True
        )
    if square:
        first = converge_first(*halves[1:])
    grad_qkv = backward_attention(heads, width, qkv, grad_heads, exact, logs, slots, places)
    if square:
        columns = jnp.stack([gain_one, bias_one, grad_gain_two, grad_bias_two], 1)
        columns = jnp.pad(columns, ((0, 0), (0, 124)))
        *first, columns, grad_qkv = lax.optimization_barrier((*first, columns, grad_qkv))
        upper_terms = converge_last(halves[0], first)
        grad_qkv = grad_qkv.reshape(owners, mine, 3 * width)
        away = nt(grad_qkv[4:].reshape(4 * mine, 3 * width), w_heads).astype(BF16)
        grad_qkv = after(grad_qkv, away)
        away = flip(away, "c").reshape(4, mine, model)
        pairs = input_parts(grad_qkv[:4], w_heads, away)
        second = converge_first(*pairs[1:])
        terms = converge_last(pairs[0], second)
        grad_attn_in = jnp.concatenate([total(each) for each in terms], 0)
        grad_qkv = after(
            grad_qkv, *[each for group in (*pairs, *upper_terms) for each in group]
        )
        packed_grad = projection_gradient(
            attn_in, grad_qkv.reshape(owners * mine, 3 * width), w_heads, columns
        )
        packed_grad = after(packed_grad, lower, *second[:2])
    else:
        grad_qkv = grad_qkv.reshape(owners * mine, 3 * width)
        away = nt(grad_qkv, w_heads).astype(BF16)
        grad_attn_in = lax.psum_scatter(away, CTX, scatter_dimension=0, tiled=True).astype(F32)
        grad_columns = tn(attn_in, grad_qkv)
        w_wide = w_heads.astype(F32)
        summed = jnp.sum(grad_qkv.astype(F32), 0)
        grad_bias_one = jnp.sum(w_wide * summed, 1)
        grad_gain_one = (jnp.sum(w_wide * grad_columns, 1) - bias_one * grad_bias_one) / gain_one
        vector_grads = jnp.stack([grad_gain_one, grad_bias_one, grad_gain_two, grad_bias_two], 1)
        packed_grad = jnp.concatenate(
            [grad_columns, vector_grads, jnp.zeros((model, 124), F32)], 1
        ).astype(BF16)

    if square:
        lower = after(lower, grad_attn_in)
        lower = lower[0].astype(F32) + sum(
            flip(lower[k], axis).astype(F32) for k, axis in ((1, "b"), (2, "a"))
        ) + lax.ppermute(lower[3], ("a", "b"), [(0, 3), (3, 0), (1, 2), (2, 1)]).astype(F32)
        lower = lower.astype(BF16)
        grad_down = unpack_lower(spread(lower), places, shares)
        everything = pack(upper_terms, packed_grad, shares)
        everything = lax.psum_scatter(
            everything.reshape(-1, model), "z", scatter_dimension=0, tiled=True
        )
        grad_upper, grad_outer, grad_proj, vector_grads = unpack(
            spread(after(everything, lower)), places, shares, part, width
        )
    else:
        span = 2 * ff
        per_part = packed_grad.shape[1] * part // span
        everything = jnp.concatenate(
            [
                jnp.concatenate([upper, lower], 2),
                outer.reshape(shares, -1, span),
                packed_grad.reshape(shares, per_part, span),
            ],
            1,
        )
        everything = lax.psum_scatter(
            everything.reshape(-1, span), "z", scatter_dimension=0, tiled=True
        )
        everything = lax.all_gather(everything, CTX, axis=0, tiled=False)
        grad_upper = (
            everything[:, :part, :ff]
            .reshape(owners, part, shares, ff_rows)
            .transpose(1, 2, 0, 3)
            .reshape(part, full_ff)
            .astype(F32)
        )
        grad_down = (
            everything[:, :part, ff:]
            .reshape(owners, ff_parts, ff_rows, ff)
            .transpose(0, 2, 1, 3)
            .reshape(owners * ff_rows, model)
            .astype(F32)
        )
        at = part + out_rows * model // span
        grad_outer = everything[:, part:at].reshape(part, model).astype(F32)
        packed_grad = everything[:, at:].reshape(owners, part, -1).astype(F32)
        grad_proj = (
            packed_grad[:, :, : 3 * width]
            .reshape(owners, part, 3, width)
            .transpose(1, 2, 0, 3)
            .reshape(part, 3 * model)
        )
        vector_grads = jnp.sum(packed_grad[:, :, 3 * width : 3 * width + 4], 0).T

    attn_full, attn_norm, attn_rstd = layer_norm(flat.astype(F32), gain_one, bias_one)
    in_grad = (grad_resid + norm_back(grad_attn_in, attn_norm, attn_rstd, gain_one)).astype(BF16)

    return (
        output.reshape(tokens.shape),
        in_grad.reshape(tokens.shape),
        vector_grads[0],
        vector_grads[1],
        grad_proj,
        grad_outer,
        vector_grads[2],
        vector_grads[3],
        grad_upper,
        grad_down,
    )


def solution(mesh):
    ctx, wsh = mesh.shape["ctx"], mesh.shape["wsh"]
    fine = Mesh(mesh.devices.reshape(ctx // 4, 2, 2, wsh), ("a", "b", "c", "z"))
    toks = P("z", CTX, None)
    ints = P("z", CTX)
    vec, mat = P("z"), P("z", None)
    in_specs = (toks, toks, ints, ints, vec, vec, mat, mat, vec, vec, mat, mat)
    out_specs = (toks, toks, vec, vec, mat, mat, vec, vec, mat, mat)
    return jax.shard_map(shards, mesh=fine, in_specs=in_specs, out_specs=out_specs, check_vma=False)
```
